32 devices in a mesh: dp: 2 (over x), gx: 4 (over y, core), gy: 4 (over z).
Axes of the slice: x: 2, y: 2, z: 4, core: 2. Of those that a mesh axis runs over, the one named last changes fastest.
Arguments:
- tokens: bfloat16 [960, 11264], P('gy', ('dp', 'gx')), may hold values from -6 to 6
- segment_ids: int32 [8, 1408], P(('dp', 'gy')), may hold values from 0 to 3, never falling along the last dimension, each value on 1 to 704 neighbouring positions
- slot_table: int32 [5], replicated, may hold values from 0 to 7, as said below
- w_qkv: bfloat16 [960, 2560], P('gy', 'gx'), may hold values from -0.1875 to 0.1875
- w_out: bfloat16 [960, 1536], P('gy', 'gx'), may hold values from -1.5 to 1.5
- w_gate_up: bfloat16 [960, 2, 2560], P('gy', None, 'gx'), may hold values from -0.1875 to 0.1875
- w_down: bfloat16 [960, 2560], P('gy', 'gx'), may hold values from -0.125 to 0.125
- gain_attn: float32 [960], P('gy'), may hold values from 0.5 to 1.5
- gain_mlp: float32 [960], P('gy'), may hold values from 0.5 to 1.5
- cotangent: bfloat16 [960, 11264], P('gy', ('dp', 'gx')), may hold values from -6 to 6
Outputs:
- layer_out: bfloat16 [960, 11264], P('gy', ('dp', 'gx'))
- input_grad: bfloat16 [960, 11264], P('gy', ('dp', 'gx'))
- grad_qkv: float32 [960, 2560], P('gy', 'gx')
- grad_out: float32 [960, 1536], P('gy', 'gx')
- grad_gate_up: float32 [960, 2, 2560], P('gy', None, 'gx')
- grad_down: float32 [960, 2560], P('gy', 'gx')
- grad_gain_attn: float32 [960], P('gy')
- grad_gain_mlp: float32 [960], P('gy')
The draws below stay inside these ranges and needn't reach their ends.
Inputs may be any that keep to these rules, and one draw needn't show every extreme that they name: `slot_table`: the 5 entries name distinct slots; slot // 2 is a weight-grid row. One row holds two groups in its slots 2 r and 2 r + 1, every other row one group in slot 2 r. `segment_ids`: within a sequence ids never fall.
All inputs are finite; a program needn't handle non-finite values.
Results may differ from the reference program's by a relative error of at most 0.019.
Values may be sent and summed in bfloat16 or wider, within the bound.
No kernel may reach another device: no remote copies, remote signals or barrier semaphores. Data moves between devices by JAX's collectives and lax.ppermute only.
A program may use at most 192 MiB of HBM per device.

```python
import math
import jax
import jax.numpy as jnp
import numpy as np
from jax import lax

D = 960
FF = 2560
HD = 64
KVH = 5
QPK = 3
SLOT_DEV = 2
L = 1408
SEGS = 4
SLOTS = 8
BLOCK = 704
SEQS = 8
TOKENS = 11264


def draw_slot_table(key, part):
    key = jax.random.fold_in(key, 7)
    grid_total = SLOTS // SLOT_DEV
    row_order = jax.random.permutation(key, jnp.arange(grid_total, dtype=jnp.int32))
    firsts = row_order * SLOT_DEV
    seconds = row_order[:KVH - grid_total] * SLOT_DEV + 1
    return jnp.concatenate([firsts, seconds]).astype(jnp.int32)


def levels(own_key, dims, split, low, top_value):
    def one(axis_at, shards_of):
        steps = jax.random.uniform(jax.random.fold_in(jax.random.fold_in(own_key, 6), axis_at), (shards_of,), jnp.float32, low / len(split), top_value / len(split))
        return jnp.repeat(jnp.exp(steps), dims[axis_at] // shards_of).reshape((-1,) + (1,) * (len(dims) - axis_at - 1))

    gain = one(*split[0])
    for cut in split[1:]:
        gain = gain * one(*cut)
    return gain


def length_profile(number_of, total, most, slope):
    loads = [(1 << 20) // math.isqrt(standing ** slope) + 1 for standing in range(2, number_of + 1)]
    surplus, given = total - most - (number_of - 1), [1] * (number_of - 1)
    while surplus > 0:
        free = [i for i in range(number_of - 1) if given[i] < most]
        mass, left = sum([loads[i] for i in free]), surplus
        for i in free:
            extra = min(most - given[i], max(1, left * loads[i] // mass), surplus)
            given[i] = given[i] + extra
            surplus = surplus - extra
    return np.array([most] + given)


def ragged(key, number_of, total, most, skew):
    if number_of == 2:
        one = jax.random.randint(key, (), max(1, total - most), min(most, total - 1) + 1)
        return jnp.stack([one, total - one])
    lengths = jnp.asarray(length_profile(number_of, total, most, skew), jnp.int32)
    twos = (number_of - 1) // 2
    source_of, sink = lengths[1:1 + 2 * twos:2], lengths[2:2 + 2 * twos:2]
    slack = jnp.minimum(source_of - 1, most - sink)
    shifted = jax.random.randint(jax.random.fold_in(key, 1), (twos,), 0, 1 << 20) % (slack + 1)
    lengths = lengths.at[1:1 + 2 * twos:2].set(source_of - shifted).at[2:2 + 2 * twos:2].set(sink + shifted)
    return lengths[jax.random.permutation(jax.random.fold_in(key, 2), number_of)]


def noise(rng, extent, deviation, limit, shards=(), kind=jnp.bfloat16):
    factor_of = levels(rng, extent, shards, -0.22, 0.18) if shards else 1.0
    result = jax.random.normal(rng, extent, jnp.float32) * deviation * factor_of
    return jnp.minimum(jnp.maximum(result, -limit), limit).astype(kind)


def setup_inputs(seed: int = 0) -> dict:
    arg_keys = jax.random.split(jax.random.key(seed), 11)
    return {
        "tokens": noise(arg_keys[0], (D, TOKENS), 1.0, 6.0, ((0, 4), (1, 8))),
        "segment_ids": jax.vmap(lambda own: jnp.searchsorted(jnp.cumsum(ragged(own, SEGS, L, L // 2, 2)), jnp.arange(L), side="right"))(jax.random.split(arg_keys[1], SEQS)).reshape((SEQS, L)).astype(jnp.int32),
        "slot_table": draw_slot_table(jax.random.fold_in(arg_keys[10], 71), 0),
        "w_qkv": noise(arg_keys[3], (D, SLOTS * (QPK + 2) * HD), D ** -0.5, 0.1875, ((0, 4), (1, 4))),
        "w_out": noise(arg_keys[4], (D, SLOTS * QPK * HD), (QPK * HD * KVH // 64) ** -0.5, 1.5, ((0, 4), (1, 4))),
        "w_gate_up": noise(arg_keys[5], (D, 2, FF), D ** -0.5, 0.1875, ((0, 4), (2, 4))),
        "w_down": noise(arg_keys[6], (D, FF), FF ** -0.5, 0.125, ((0, 4), (1, 4))),
        "gain_attn": jnp.clip(1.0 + 0.1 * jax.random.normal(arg_keys[7], (D,), jnp.float32), 0.5, 1.5),
        "gain_mlp": jnp.clip(1.0 + 0.1 * jax.random.normal(arg_keys[8], (D,), jnp.float32), 0.5, 1.5),
        "cotangent": noise(arg_keys[9], (D, TOKENS), 1.0, 6.0, ((0, 4), (1, 8))),
    }


EPSILON = 1e-05
THETA_BASE = 100000.0
NEGATIVE = -1e+30
HIGHEST = lax.Precision.HIGHEST

@jax.custom_vjp
def low(v):
    return lax.optimization_barrier(v.astype(jnp.bfloat16)).astype(jnp.float32)

@jax.custom_vjp
def low_back(v):
    return v

def low_keep(v):
    return (low(v), None)

def low_pass(kept, grad):
    return (grad,)

def back_keep(v):
    return (v, None)

def back_low(kept, grad):
    return (low(grad),)
low.defvjp(low_keep, low_pass)
low_back.defvjp(back_keep, back_low)

def rope_angles(segment_row):
    doc_marks = (segment_row[:, None] == jnp.arange(SEGS, dtype=jnp.int32)[None, :]).astype(jnp.int32)
    counts = lax.optimization_barrier(jnp.sum(doc_marks, axis=0))
    starts = jnp.cumsum(counts) - counts
    position = jnp.arange(L, dtype=jnp.int32) - lax.optimization_barrier(jnp.sum(doc_marks * starts[None, :], axis=1))
    frequency = THETA_BASE ** (-2.0 * jnp.arange(HD // 2, dtype=jnp.float32) / HD)
    angles = position.astype(jnp.float32)[:, None] * frequency[None, :]
    return (jnp.cos(angles), jnp.sin(angles))

def rotate(values_in, cos_part, sin_part):
    half_width = values_in.shape[-1] // 2
    first_half = values_in[..., :half_width]
    second_half = values_in[..., half_width:]
    return jnp.concatenate([first_half * cos_part - second_half * sin_part, second_half * cos_part + first_half * sin_part], axis=-1)

def attend(queries, key_rows, value_rows, segment_row):

    def one_block(block_index):
        first_row = block_index * BLOCK
        query_rows = lax.dynamic_slice_in_dim(queries, first_row, BLOCK, 0)
        scores = jnp.einsum('qhd,kd->hqk', query_rows, key_rows, precision=HIGHEST) * HD ** (-0.5)
        scores = low_back(scores)
        query_docs = lax.dynamic_slice_in_dim(segment_row, first_row, BLOCK, 0)
        query_index = first_row + jnp.arange(BLOCK, dtype=jnp.int32)
        allowed = (query_docs[:, None] == segment_row[None, :]) & (jnp.arange(L, dtype=jnp.int32)[None, :] <= query_index[:, None])
        masked = jnp.where(allowed[None], scores, NEGATIVE)
        row_peak = lax.optimization_barrier(jnp.max(masked, axis=-1, keepdims=True))
        exp_scores = jnp.exp(masked - row_peak)
        weights_low = low(exp_scores / lax.optimization_barrier(jnp.sum(exp_scores, axis=-1, keepdims=True)))
        return jnp.einsum('hqk,kd->qhd', weights_low, value_rows, precision=HIGHEST)
    block_out = lax.map(jax.checkpoint(one_block), jnp.arange(L // BLOCK, dtype=jnp.int32))
    return block_out.reshape(L, QPK, HD)

def layer(block_rows, block_segments, slot_table, w_qkv, w_out, w_gate_up, w_down, gain_attn, gain_mlp):
    qkv_slots = jnp.transpose(w_qkv.reshape(D, SLOTS, (QPK + 2) * HD), (1, 0, 2))
    out_slots = jnp.transpose(w_out.reshape(D, SLOTS, QPK * HD), (1, 2, 0))
    down_rows = jnp.transpose(w_down)
    scale_one = lax.rsqrt(lax.optimization_barrier(jnp.mean(block_rows * block_rows, axis=-1, keepdims=True)) + EPSILON)
    normed_one = low(block_rows * scale_one * gain_attn)
    chosen = qkv_slots[slot_table]
    projected = low_back(jnp.einsum('cld,gde->cgle', normed_one, chosen, precision=HIGHEST))
    cos_part, sin_part = jax.vmap(rope_angles)(block_segments)
    query_width = QPK * HD
    queries = projected[..., :query_width].reshape(projected.shape[0], KVH, L, QPK, HD)
    queries = low(rotate(queries, cos_part[:, None, :, None, :], sin_part[:, None, :, None, :]))
    key_rows = low(rotate(projected[..., query_width:query_width + HD], cos_part[:, None], sin_part[:, None]))
    value_rows = low(projected[..., query_width + HD:])
    per_group = jax.vmap(attend, in_axes=(0, 0, 0, None))
    head_out = jax.vmap(per_group, in_axes=(0, 0, 0, 0))(queries, key_rows, value_rows, block_segments)
    head_out = low(low_back(head_out))
    out_proj = out_slots[slot_table].reshape(KVH, QPK, HD, D)
    attention = low_back(jnp.einsum('cglhe,ghed->cld', head_out, out_proj, precision=HIGHEST))
    middle = block_rows + attention
    scale_two = lax.rsqrt(lax.optimization_barrier(jnp.mean(middle * middle, axis=-1, keepdims=True)) + EPSILON)
    normed_two = low(middle * scale_two * gain_mlp)
    gate_up = low_back(jnp.einsum('cld,dkf->clkf', normed_two, w_gate_up, precision=HIGHEST))
    hidden = low(jax.nn.silu(gate_up[:, :, 0]) * gate_up[:, :, 1])
    mlp_out = low_back(jnp.einsum('clf,fd->cld', hidden, down_rows, precision=HIGHEST))
    return middle + mlp_out

def reference(tokens, segment_ids, slot_table, w_qkv, w_out, w_gate_up, w_down, gain_attn, gain_mlp, cotangent):
    weights = tuple((weight_item.astype(jnp.float32) for weight_item in (w_qkv, w_out, w_gate_up, w_down, gain_attn, gain_mlp)))
    inputs = jnp.transpose(tokens.astype(jnp.float32)).reshape(-1, 2, L, D)
    grads_in = jnp.transpose(cotangent.astype(jnp.float32)).reshape(-1, 2, L, D)
    segment_pairs = segment_ids.reshape(-1, 2, L)

    def step_pair(totals, batch_part):
        block_in, block_segments, block_grad = batch_part

        def forward(block_rows, *params):
            return layer(block_rows, block_segments, slot_table, *params)
        layer_value, pullback = jax.vjp(forward, block_in, *weights)
        grads = pullback(block_grad)
        totals = tuple((running + addend for running, addend in zip(totals, grads[1:])))
        return (totals, (layer_value.astype(jnp.bfloat16), grads[0].astype(jnp.bfloat16)))
    empty = tuple((jnp.zeros_like(weight_item) for weight_item in weights))
    totals, (outputs, input_grads) = lax.scan(step_pair, empty, (inputs, segment_pairs, grads_in))
    return (jnp.transpose(outputs.reshape(-1, D)), jnp.transpose(input_grads.reshape(-1, D)), totals[0], totals[1], totals[2], totals[3], totals[4], totals[5])
```

```python
import functools

import jax
import jax.numpy as jnp
from jax import lax
from jax.experimental import pallas as pl
from jax.experimental.pallas import tpu as pltpu
from jax.sharding import PartitionSpec as P

D = 960
HD = 64
QPK = 3
L = 1408
SEGS = 4
QW = QPK * HD
SLOT_W = QW + 2 * HD
PACK = SLOT_W + QW
GROUPS = 5
ROWS = 4
CH = L // ROWS
FB = D // ROWS
ODD = PACK // ROWS

EPSILON = 1e-05
THETA_BASE = 100000.0
NEGATIVE = -1e30
SEQ_MAP = (0, 2, 1, 3)
SEQ_BACK = (0, 2, 1, 3)
BF = jnp.bfloat16
F32 = jnp.float32
VMEM_LIMIT = 40 * 1024 * 1024


def tn(a, b):
    return lax.dot_general(a, b, (((0,), (0,)), ((), ())), preferred_element_type=F32)


def nn(a, b):
    return lax.dot_general(a, b, (((1,), (0,)), ((), ())), preferred_element_type=F32)


def nt(a, b):
    return lax.dot_general(a, b, (((1,), (1,)), ((), ())), preferred_element_type=F32)


def qkv_kernel(x_ref, gain_ref, cos_ref, sin_ref, w_ref, qs_ref, kv_ref, n1_ref, r1_ref):
    @pl.when(pl.program_id(0) == 0)
    def _():
        x = x_ref[...].astype(F32)
        r1 = lax.rsqrt(jnp.sum(x * x, axis=0, keepdims=True) / D + EPSILON)
        r1_ref[...] = r1
        n1_ref[...] = (x * r1 * gain_ref[...]).astype(BF)

    p = tn(w_ref[0, :, :SLOT_W], n1_ref[...])
    cos_a = cos_ref[...]
    sin_a = sin_ref[...]
    half = HD // 2
    for j in range(QPK + 1):
        a = p[j * HD : j * HD + half]
        b = p[j * HD + half : (j + 1) * HD]
        first = (a * cos_a - b * sin_a).astype(BF)
        second = (b * cos_a + a * sin_a).astype(BF)
        if j < QPK:
            first = (first.astype(F32) * HD**-0.5).astype(BF)
            second = (second.astype(F32) * HD**-0.5).astype(BF)
            qs_ref[0, j * HD : j * HD + half] = first
            qs_ref[0, j * HD + half : (j + 1) * HD] = second
        else:
            kv_ref[0, :half] = first
            kv_ref[0, half:HD] = second
    kv_ref[0, HD:] = p[(QPK + 1) * HD :].astype(BF)


def attend_kernel(
    flags, qs_ref, kv0, kv1, kv2, kv3, bias_ref, w_ref, x_ref, gain_ref,
    o_ref, lse_ref, h_ref, n2_ref, r2_ref, m_s, l_s, acc_s,
):
    g = pl.program_id(0)
    kvs = (kv0, kv1, kv2, kv3)

    def fold(k, fresh):
        keys = kvs[k][0, :HD]
        values = kvs[k][0, HD:]
        bias = bias_ref[k]
        for j in range(QPK):
            s = tn(keys, qs_ref[0, j * HD : (j + 1) * HD]) + bias
            top = jnp.max(s, axis=0, keepdims=True)
            if fresh:
                m = top
                e = jnp.exp(s - m)
                l_s[j : j + 1] = jnp.sum(e, axis=0, keepdims=True)
                acc_s[j * HD : (j + 1) * HD] = nn(values, e.astype(BF))
            else:
                old = m_s[j : j + 1]
                m = jnp.maximum(old, top)
                fade = jnp.exp(old - m)
                e = jnp.exp(s - m)
                l_s[j : j + 1] = l_s[j : j + 1] * fade + jnp.sum(e, axis=0, keepdims=True)
                acc_s[j * HD : (j + 1) * HD] = acc_s[j * HD : (j + 1) * HD] * fade + nn(
                    values, e.astype(BF)
                )
            m_s[j : j + 1] = m

    fold(0, True)
    for k in range(1, ROWS):
        pl.when(flags[k] != 0)(functools.partial(fold, k, False))
    for j in range(QPK):
        total = l_s[j : j + 1]
        o_ref[0, j * HD : (j + 1) * HD] = (acc_s[j * HD : (j + 1) * HD] / total).astype(BF)
        lse_ref[0, j : j + 1] = m_s[j : j + 1] + jnp.log(total)
    part = nn(w_ref[0, :, SLOT_W:], o_ref[0])

    @pl.when(g == 0)
    def _():
        h_ref[...] = x_ref[...].astype(F32) + part

    @pl.when(g != 0)
    def _():
        h_ref[...] += part

    @pl.when(g == GROUPS - 1)
    def _():
        h = h_ref[...]
        r2 = lax.rsqrt(jnp.sum(h * h, axis=0, keepdims=True) / D + EPSILON)
        r2_ref[...] = r2
        n2_ref[...] = (h * r2 * gain_ref[...]).astype(BF)


def attend_back_kernel(
    flags, qs_ref, kv0, kv1, kv2, kv3, bias_ref, w_ref, o_ref, lse_ref, datt_ref, cos_ref, sin_ref,
    dq_ref, d0, d1, d2, d3, do_s, dl_s, dq_s,
):
    kvs = (kv0, kv1, kv2, kv3)
    outs = (d0, d1, d2, d3)
    do_s[...] = tn(w_ref[0, :, SLOT_W:], datt_ref[...]).astype(BF)
    for j in range(QPK):
        rows = slice(j * HD, (j + 1) * HD)
        dl_s[j : j + 1] = jnp.sum(
            do_s[rows].astype(F32) * o_ref[0, rows].astype(F32), axis=0, keepdims=True
        )

    def fold(k, fresh):
        keys = kvs[k][0, :HD]
        values = kvs[k][0, HD:]
        bias = bias_ref[k]
        dk = jnp.zeros((HD, CH), F32)
        dv = jnp.zeros((HD, CH), F32)
        for j in range(QPK):
            rows = slice(j * HD, (j + 1) * HD)
            s = tn(keys, qs_ref[0, rows]) + bias
            p = jnp.exp(s - lse_ref[0, j : j + 1])
            do_j = do_s[rows]
            dp = tn(values, do_j)
            ds = (p * (dp - dl_s[j : j + 1])).astype(BF)
            dv = dv + nt(do_j, p.astype(BF))
            dk = dk + nt(qs_ref[0, rows], ds)
            dq = nn(keys, ds)
            if fresh:
                dq_s[rows] = dq
            else:
                dq_s[rows] += dq
        outs[k][0, :HD] = dk.astype(outs[k].dtype)
        outs[k][0, HD:] = dv.astype(outs[k].dtype)

    fold(0, True)
    for k in range(1, ROWS):
        pl.when(flags[k] != 0)(functools.partial(fold, k, False))

        @pl.when(flags[k] == 0)
        def _(k=k):
            outs[k][...] = jnp.zeros(outs[k].shape, outs[k].dtype)

    cos_a = cos_ref[...]
    sin_a = sin_ref[...]
    half = HD // 2
    for j in range(QPK):
        a = dq_s[j * HD : j * HD + half] * HD**-0.5
        b = dq_s[j * HD + half : (j + 1) * HD] * HD**-0.5
        dq_ref[0, j * HD : j * HD + half] = (a * cos_a + b * sin_a).astype(BF)
        dq_ref[0, j * HD + half : (j + 1) * HD] = (b * cos_a - a * sin_a).astype(BF)


def mlp_kernel(wg, wu, wd, *refs):
    count = len(refs) // 7
    for i in range(count):
        n2 = refs[i]
        dy = refs[count + i]
        a_ref, dg_ref, du_ref, mlp_ref, dn_ref = refs[2 * count + 5 * i : 2 * count + 5 * i + 5]
        width = wg.shape[1]
        step = 128
        for f in range(0, width, step):
            cols = slice(f, f + step)
            gate = tn(wg[:, cols], n2[...])
            up = tn(wu[:, cols], n2[...])
            da = tn(wd[:, cols], dy[...])
            sigma = jax.nn.sigmoid(gate)
            silu = gate * sigma
            a_ref[cols] = (silu * up).astype(BF)
            dg_ref[cols] = (da * up * sigma * (1.0 + gate * (1.0 - sigma))).astype(BF)
            du_ref[cols] = (da * silu).astype(BF)
        dn_ref[...] = (nn(wg[...], dg_ref[...]) + nn(wu[...], du_ref[...])).astype(BF)
        mlp_ref[...] = nn(wd[...], a_ref[...]).astype(BF)


def whole(shape):
    return pl.BlockSpec(shape, lambda *_: (0,) * len(shape))


def per_group(*shape):
    return pl.BlockSpec((1,) + shape, lambda g, *_: (g, 0, 0))


def kv_blocks():
    def spec(k):
        return pl.BlockSpec(
            (1, 2 * HD, CH), lambda g, *_: (jnp.where(g < ROWS, g ^ k, g), 0, 0)
        )

    return [spec(k) for k in range(ROWS)]


def params():
    return pltpu.CompilerParams(vmem_limit_bytes=VMEM_LIMIT)


def sds(shape, dtype):
    return jax.ShapeDtypeStruct(shape, dtype)


def call_qkv(x, gain, cos_a, sin_a, w5):
    return pl.pallas_call(
        qkv_kernel,
        grid=(GROUPS,),
        in_specs=[whole((D, CH)), whole((D, 1)), whole((HD // 2, CH)), whole((HD // 2, CH)), per_group(D, PACK)],
        out_specs=[per_group(QW, CH), per_group(2 * HD, CH), whole((D, CH)), whole((1, CH))],
        out_shape=[
            sds((GROUPS, QW, CH), BF), sds((GROUPS, 2 * HD, CH), BF), sds((D, CH), BF), sds((1, CH), F32),
        ],
        compiler_params=params(),
        name="qkv",
    )(x, gain, cos_a, sin_a, w5)


def call_attend(flags, qs, kvs, bias, w5, x, gain):
    return pl.pallas_call(
        attend_kernel,
        grid_spec=pltpu.PrefetchScalarGridSpec(
            num_scalar_prefetch=1,
            grid=(GROUPS,),
            in_specs=[per_group(QW, CH)] + kv_blocks()
            + [whole((ROWS, CH, CH)), per_group(D, PACK), whole((D, CH)), whole((D, 1))],
            out_specs=[per_group(QW, CH), per_group(8, CH), whole((D, CH)), whole((D, CH)), whole((1, CH))],
            scratch_shapes=[pltpu.VMEM((8, CH), F32), pltpu.VMEM((8, CH), F32), pltpu.VMEM((QW, CH), F32)],
        ),
        out_shape=[
            sds((GROUPS, QW, CH), BF), sds((GROUPS, 8, CH), F32), sds((D, CH), F32), sds((D, CH), BF),
            sds((1, CH), F32),
        ],
        compiler_params=params(),
        name="attend",
    )(flags, qs, *kvs, bias, w5, x, gain)


def call_attend_back(flags, qs, kvs, bias, w5, o, lse, datt, cos_a, sin_a):
    return pl.pallas_call(
        attend_back_kernel,
        grid_spec=pltpu.PrefetchScalarGridSpec(
            num_scalar_prefetch=1,
            grid=(GROUPS,),
            in_specs=[per_group(QW, CH)] + kv_blocks()
            + [whole((ROWS, CH, CH)), per_group(D, PACK), per_group(QW, CH), per_group(8, CH),
               whole((D, CH)), whole((HD // 2, CH)), whole((HD // 2, CH))],
            out_specs=[per_group(QW, CH)] + kv_blocks(),
            scratch_shapes=[pltpu.VMEM((QW, CH), BF), pltpu.VMEM((8, CH), F32), pltpu.VMEM((QW, CH), F32)],
        ),
        out_shape=[sds((GROUPS, QW, CH), BF), sds((GROUPS, 2 * HD, CH), F32)]
        + [sds((GROUPS, 2 * HD, CH), BF)] * 3,
        compiler_params=params(),
        name="attend_back",
    )(flags, qs, *kvs, bias, w5, o, lse, datt, cos_a, sin_a)


def call_mlp(wg, wu, wd, n2s, dys):
    width = wg.shape[1]
    count = len(n2s)
    outs = pl.pallas_call(
        mlp_kernel,
        out_shape=[sds((width, CH), BF), sds((width, CH), BF), sds((width, CH), BF), sds((D, CH), BF), sds((D, CH), BF)]
        * count,
        compiler_params=params(),
        name="mlp",
    )(wg, wu, wd, *n2s, *dys)
    return [outs[5 * i : 5 * i + 5] for i in range(count)]


def swap(values, bit):
    return lax.ppermute(values, "gx", [(i, i ^ bit) for i in range(ROWS)])


def row_gather(own):
    mate = swap(own, 1)
    far = swap(own, 2)
    return own, mate, far, swap(far, 1)


def add(a, b):
    return (a.astype(F32) + b.astype(F32)).astype(BF)


def row_scatter(blocks):
    far = add(blocks[2], swap(blocks[3], 1))
    near = blocks[0].astype(F32) + swap(blocks[1], 1).astype(F32)
    return near + swap(far, 2).astype(F32)


def ring(values):
    return lax.ppermute(values, "gy", [(i, (i + 1) % ROWS) for i in range(ROWS)])


def ring_scatter(take, iy):
    moving = take((iy + 3) % ROWS).astype(BF)
    for s in range(ROWS - 1):
        moving = ring(moving).astype(F32) + take((iy + 2 - s) % ROWS).astype(F32)
        if s < ROWS - 2:
            moving = moving.astype(BF)
    return moving


def dp_sum(values):
    if lax.axis_size("dp") == 2:
        return values.astype(F32) + lax.ppermute(values, "dp", [(0, 1), (1, 0)]).astype(F32)
    return lax.psum(values, "dp").astype(F32)


def to_tokens(values, ix, iy):
    parts = jnp.transpose(values.reshape(FB, ROWS, CH), (1, 0, 2))
    out = jnp.zeros((D, CH), values.dtype)
    for k in range(ROWS):
        pairs = [(a * ROWS + b, (b ^ k) * ROWS + SEQ_MAP[a]) for a in range(ROWS) for b in range(ROWS)]
        piece = lax.ppermute(lax.dynamic_index_in_dim(parts, iy ^ k, 0, keepdims=False), ("gx", "gy"), pairs)
        out = lax.dynamic_update_slice(out, piece, (FB * (ix ^ k), 0))
    return out


def to_features(values, ix, iy):
    out = jnp.zeros((ROWS, FB, CH), values.dtype)
    for k in range(ROWS):
        pairs = [(a * ROWS + b, SEQ_BACK[b] * ROWS + (a ^ k)) for a in range(ROWS) for b in range(ROWS)]
        piece = lax.ppermute(
            lax.dynamic_slice(values, (FB * (ix ^ k), 0), (FB, CH)), ("gx", "gy"), pairs
        )
        out = lax.dynamic_update_slice(out, piece[None], (iy ^ k, 0, 0))
    return jnp.transpose(out, (1, 0, 2)).reshape(FB, L)


def gather_attention_weights(w_qkv, w_out, odd_row, ix, iy):
    even = jnp.concatenate([w_qkv[:, :SLOT_W], w_out[:, :QW]], axis=1)
    odd = jnp.concatenate([w_qkv[:, SLOT_W:], w_out[:, QW:]], axis=1)
    odd = jnp.where(ix == odd_row, odd, jnp.zeros_like(odd))
    quarters = [lax.dynamic_slice(odd, (0, ODD * (ix ^ k)), (FB, ODD)) for k in range(ROWS)]
    quarter = row_scatter(quarters).astype(BF)
    moving = jnp.concatenate([even, quarter], axis=1)
    w5 = jnp.zeros((GROUPS, D, PACK), BF)
    for j in range(ROWS):
        if j:
            moving = ring(moving)
        at = FB * ((iy - j) % ROWS)
        for k, piece in enumerate(row_gather(moving)):
            w5 = lax.dynamic_update_slice(w5, piece[None, :, :PACK], (k, at, 0))
            w5 = lax.dynamic_update_slice(w5, piece[None, :, PACK:], (GROUPS - 1, at, ODD * (ix ^ k)))
    return w5


def gather_mlp_weights(packed, iy):
    width = packed.shape[1]
    full = jnp.zeros((D, width), BF)
    if lax.axis_size("dp") == 2:
        part = (width // 2 + 127) // 128 * 128
        at_own = lax.axis_index("dp") * (width - part)
        at_other = (1 - lax.axis_index("dp")) * (width - part)
        moving = lax.dynamic_slice(packed, (0, at_own), (FB, part))
        full = lax.dynamic_update_slice(full, packed, (FB * iy, 0))
        for j in range(1, ROWS):
            moving = ring(moving)
            other = lax.ppermute(moving, "dp", [(0, 1), (1, 0)])
            at = FB * ((iy - j) % ROWS)
            full = lax.dynamic_update_slice(full, moving, (at, at_own))
            full = lax.dynamic_update_slice(full, other, (at, at_other))
        return full
    moving = packed
    for j in range(ROWS):
        if j:
            moving = ring(moving)
        full = lax.dynamic_update_slice(full, moving, (FB * ((iy - j) % ROWS), 0))
    return full


def norm_back(values, scale, gain, grad):
    weighted = grad * gain
    inner = jnp.sum(weighted * values, axis=0, keepdims=True)
    return (
        scale * weighted - values * (scale**3 * inner / D),
        jnp.sum(grad * values * scale, axis=1),
    )


def per_device(
    tokens, segment_ids, slot_table, w_qkv, w_out, w_gate_up, w_down, gain_attn, gain_mlp, cotangent
):
    ix = lax.axis_index("gx")
    iy = lax.axis_index("gy")
    ff = w_down.shape[1]
    odd_row = jnp.sum(jnp.where(slot_table % 2 == 1, slot_table // 2, 0))

    x = to_tokens(tokens, ix, iy)
    w5 = gather_attention_weights(w_qkv, w_out, odd_row, ix, iy)
    gains = lax.all_gather(jnp.stack([gain_attn, gain_mlp]), "gy", axis=1, tiled=True)
    gain_one = gains[0][:, None]
    gain_two = gains[1][:, None]
    seg = lax.ppermute(segment_ids, "gy", [(i, SEQ_MAP[i]) for i in range(ROWS)]).reshape(ROWS, CH)
    w_mlp = gather_mlp_weights(
        jnp.concatenate([w_gate_up[:, 0], w_gate_up[:, 1], w_down], axis=1), iy
    )
    dy = to_tokens(cotangent, ix, iy)

    seg_own = lax.dynamic_index_in_dim(seg, ix, 0, keepdims=False)
    starts = jnp.stack([jnp.sum(seg < s) for s in range(SEGS)]).astype(jnp.int32)
    first = sum(jnp.where(seg_own == s, starts[s], 0) for s in range(SEGS))
    at_own = ix * CH + jnp.arange(CH, dtype=jnp.int32)
    position = (at_own - first).astype(F32)
    frequency = THETA_BASE ** (-2.0 * jnp.arange(HD // 2, dtype=F32) / HD)
    angles = frequency[:, None] * position[None, :]
    cos_a = jnp.cos(angles)
    sin_a = jnp.sin(angles)
    biases = []
    flags = []
    for k in range(ROWS):
        seg_k = lax.dynamic_index_in_dim(seg, ix ^ k, 0, keepdims=False)
        at_k = (ix ^ k) * CH + jnp.arange(CH, dtype=jnp.int32)
        allowed = (seg_k[:, None] == seg_own[None, :]) & (at_k[:, None] <= at_own[None, :])
        biases.append(jnp.where(allowed, 0.0, NEGATIVE).astype(F32))
        flags.append(((ix ^ k) <= ix) & (seg_k[CH - 1] >= seg_own[0]))
    bias = jnp.stack(biases)
    flags = jnp.stack(flags).astype(jnp.int32)

    qs, kv, n1, r1 = call_qkv(x, gain_one, cos_a, sin_a, w5)
    kvs = row_gather(kv)
    o, lse, h, n2, r2 = call_attend(flags, qs, kvs, bias, w5, x, gain_two)

    n2s = row_gather(n2)
    dys = row_gather(dy)
    wg, wu, wd = w_mlp[:, :ff], w_mlp[:, ff : 2 * ff], w_mlp[:, 2 * ff :]
    near = call_mlp(wg, wu, wd, n2s[:2], dys[:2])
    far = call_mlp(wg, wu, wd, n2s[2:], dys[2:])
    blocks = near + far
    dn2 = row_scatter([b[4] for b in blocks])
    mlp = row_scatter([b[3] for b in blocks])
    layer_out = to_features((h + mlp).astype(BF), ix, iy)

    grad_norm, grad_gain_mlp = norm_back(h, r2, gain_two, dn2)
    dh = dy.astype(F32) + grad_norm
    datt = dh.astype(BF)

    dq, dkv0, dkv1, dkv2, dkv3 = call_attend_back(flags, qs, kvs, bias, w5, o, lse, datt, cos_a, sin_a)
    dkv = row_scatter([dkv0, dkv1, dkv2, dkv3])
    half = HD // 2
    dk_a = dkv[:, :half]
    dk_b = dkv[:, half:HD]
    dpg = jnp.concatenate(
        [
            dq,
            (dk_a * cos_a + dk_b * sin_a).astype(BF),
            (dk_b * cos_a - dk_a * sin_a).astype(BF),
            dkv[:, HD:].astype(BF),
        ],
        axis=1,
    )
    dn1 = jnp.einsum("gdc,gct->dt", w5[:, :, :SLOT_W], dpg, preferred_element_type=F32)
    x32 = x.astype(F32)
    grad_in, grad_gain_attn = norm_back(x32, r1, gain_one, dn1)
    input_grad = to_features((dh + grad_in).astype(BF), ix, iy)

    n2_all = jnp.concatenate(n2s, axis=1)
    dy_all = jnp.concatenate(dys, axis=1)
    gate_all = jnp.concatenate([b[1] for b in blocks], axis=1)
    up_all = jnp.concatenate([b[2] for b in blocks], axis=1)
    a_all = jnp.concatenate([b[0] for b in blocks], axis=1)
    g_mlp = jnp.concatenate(
        [nt(n2_all, gate_all).astype(BF), nt(n2_all, up_all).astype(BF), nt(dy_all, a_all).astype(BF)],
        axis=1,
    )
    g_mlp = ring_scatter(lambda at: lax.dynamic_slice(g_mlp, (FB * at, 0), (FB, 3 * ff)), iy)
    g_mlp = dp_sum(g_mlp.astype(BF))

    g_qkv = jnp.einsum("dt,gct->gdc", n1, dpg, preferred_element_type=F32).astype(BF)
    g_out = jnp.einsum("dt,get->gde", datt, o, preferred_element_type=F32).astype(BF)
    g5 = jnp.concatenate([g_qkv, g_out], axis=2)
    packs = [
        jnp.concatenate([g5[k], lax.dynamic_slice(g5[GROUPS - 1], (0, ODD * (ix ^ k)), (D, ODD))], axis=1)
        for k in range(ROWS)
    ]
    g_attn = row_scatter(packs).astype(BF)
    g_attn = ring_scatter(lambda at: lax.dynamic_slice(g_attn, (FB * at, 0), (FB, PACK + ODD)), iy)
    g_attn = dp_sum(g_attn.astype(BF))
    even = g_attn[:, :PACK]
    odd = jnp.zeros((FB, PACK), F32)
    for k, piece in enumerate(row_gather(g_attn[:, PACK:])):
        odd = lax.dynamic_update_slice(odd, piece, (0, ODD * (ix ^ k)))
    odd = jnp.where(ix == odd_row, odd, 0.0)
    grad_qkv = jnp.concatenate([even[:, :SLOT_W], odd[:, :SLOT_W]], axis=1)
    grad_out = jnp.concatenate([even[:, SLOT_W:], odd[:, SLOT_W:]], axis=1)
    grad_gate_up = jnp.stack([g_mlp[:, :ff], g_mlp[:, ff : 2 * ff]], axis=1)
    grad_down = g_mlp[:, 2 * ff :]

    gain_grads = lax.psum(jnp.stack([grad_gain_attn, grad_gain_mlp]), ("dp", "gx", "gy"))
    gain_grads = lax.dynamic_slice(gain_grads, (0, FB * iy), (2, FB))
    return (
        layer_out,
        input_grad,
        grad_qkv,
        grad_out,
        grad_gate_up,
        grad_down,
        gain_grads[0],
        gain_grads[1],
    )


def solution(mesh):
    placed = (
        P("gy", ("dp", "gx")),
        P(("dp", "gy"), None),
        P(),
        P("gy", "gx"),
        P("gy", "gx"),
        P("gy", None, "gx"),
        P("gy", "gx"),
        P("gy"),
        P("gy"),
        P("gy", ("dp", "gx")),
    )
    return jax.shard_map(
        per_device,
        mesh=mesh,
        in_specs=placed,
        out_specs=(
            P("gy", ("dp", "gx")),
            P("gy", ("dp", "gx")),
            P("gy", "gx"),
            P("gy", "gx"),
            P("gy", None, "gx"),
            P("gy", "gx"),
            P("gy"),
            P("gy"),
        ),
        check_vma=False,
    )
```

```python
import functools

import jax
import jax.numpy as jnp
from jax import lax
from jax.experimental import pallas as pl
from jax.experimental.pallas import tpu as pltpu
from jax.sharding import PartitionSpec as P

D = 960
HD = 64
QPK = 3
L = 1408
SEGS = 4
QW = QPK * HD
SLOT_W = QW + 2 * HD
PACK = SLOT_W + QW
GROUPS = 5
ROWS = 4
CH = L // ROWS
CP = 384
FB = D // ROWS
ODD = PACK // ROWS

EPSILON = 1e-05
THETA_BASE = 100000.0
NEGATIVE = -1e30
SEQ_MAP = (0, 2, 1, 3)
SEQ_BACK = (0, 2, 1, 3)
BF = jnp.bfloat16
F32 = jnp.float32
VMEM_LIMIT = 32 * 1024 * 1024
HALF = HD // 2
AW = 2 * QW
AP = AW + AW // ROWS
KV = 2 * HD
BP = KV + KV // ROWS + 16


def tn(a, b):
    return lax.dot_general(a, b, (((0,), (0,)), ((), ())), preferred_element_type=F32)


def nn(a, b):
    return lax.dot_general(a, b, (((1,), (0,)), ((), ())), preferred_element_type=F32)


def nt(a, b):
    return lax.dot_general(a, b, (((1,), (1,)), ((), ())), preferred_element_type=F32)


def rows_at(block, size=FB):
    return pl.ds(pl.multiple_of(block * FB, 16), size)


def rope(a, b, cos_a, sin_a):
    return a * cos_a - b * sin_a, b * cos_a + a * sin_a


def split_kernel(with_tail, sc, *refs):
    t_ref = refs[0]
    outs = refs[-ROWS:]
    iy = sc[1]
    if with_tail:
        lane = lax.broadcasted_iota(jnp.int32, (FB, CP - CH), 1)
        tail = jnp.zeros((FB, CP - CH), F32)
        for i in range(2):
            rest = refs[1 + i][...]
            for part in range(3):
                piece = rest.astype(BF).astype(F32)
                rest = rest - piece
                tail = jnp.where(lane == 3 * i + part, piece, tail)
        tail = tail.astype(BF)
    else:
        tail = jnp.zeros((FB, CP - CH), BF)
    for q in range(ROWS):
        block = jnp.concatenate([t_ref[:, q * CH : (q + 1) * CH], tail], axis=1)
        for k in range(ROWS):

            @pl.when((iy ^ k) == q)
            def _(k=k, block=block):
                outs[k][...] = block


def join_kernel(sc, *refs):
    for k in range(ROWS):
        refs[ROWS][rows_at(sc[0] ^ k)] = refs[k][...]


def merge_kernel(sc, *refs):
    iy = sc[1]
    parts = []
    for q in range(ROWS):
        value = refs[0][:, :CH]
        for k in range(1, ROWS):
            value = jnp.where((iy ^ k) == q, refs[k][:, :CH], value)
        parts.append(value)
    refs[ROWS][...] = jnp.concatenate(parts, axis=1)


def qkv_kernel(sc, *refs):
    toks = refs[:4]
    evens = refs[4:20]
    odds = refs[20:24]
    cos_ref, sin_ref = refs[24:26]
    x_ref, n1_ref, r1_ref, g1_ref, g2_ref, w5_ref, qs_ref, kv_ref = refs[26:]
    ix = sc[0]
    iy = sc[1]
    lane = lax.broadcasted_iota(jnp.int32, (FB, CP), 1)
    for k in range(ROWS):
        rows = rows_at(ix ^ k)
        piece = toks[k][...].astype(F32)
        x_ref[rows] = jnp.where(lane < CH, piece, 0.0).astype(BF)
        for i, out in enumerate((g1_ref, g2_ref)):
            here = (lane >= CH + 3 * i) & (lane < CH + 3 * i + 3)
            out[rows] = jnp.sum(jnp.where(here, piece, 0.0), axis=1, keepdims=True)
    x = x_ref[...].astype(F32)
    r1 = lax.rsqrt(jnp.sum(x * x, axis=0, keepdims=True) / D + EPSILON)
    r1_ref[...] = r1
    n1_ref[...] = (x * r1 * g1_ref[...]).astype(BF)
    for j in range(ROWS):
        rows = rows_at((iy + ROWS - j) % ROWS)
        for k in range(ROWS):
            w5_ref[k, rows] = evens[ROWS * k + j][...]
            lanes = pl.ds(pl.multiple_of((ix ^ k) * ODD, ODD), ODD)
            w5_ref[GROUPS - 1, rows, lanes] = odds[k][j * FB : (j + 1) * FB]
    cos_a = cos_ref[...]
    sin_a = sin_ref[...]
    for g in range(GROUPS):
        p = tn(w5_ref[g, :, :SLOT_W], n1_ref[...])
        for j in range(QPK + 1):
            first, second = rope(
                p[j * HD : j * HD + HALF], p[j * HD + HALF : (j + 1) * HD], cos_a, sin_a
            )
            first = first.astype(BF)
            second = second.astype(BF)
            if j < QPK:
                qs_ref[g, j * HD : j * HD + HALF] = (first.astype(F32) * HD**-0.5).astype(BF)
                qs_ref[g, j * HD + HALF : (j + 1) * HD] = (second.astype(F32) * HD**-0.5).astype(BF)
            else:
                kv_ref[g, :HALF] = first
                kv_ref[g, HALF:HD] = second
        kv_ref[g, HD:] = p[(QPK + 1) * HD :].astype(BF)


def attend_kernel(
    sc, qs_ref, kv0, kv1, kv2, kv3, bias_ref, w_ref, x_ref, gain_ref,
    o_ref, lse_ref, h_ref, n2_ref, r2_ref, m_s, l_s, acc_s,
):
    g = pl.program_id(0)
    kvs = (kv0, kv1, kv2, kv3)

    def fold(k, fresh):
        keys = kvs[k][0, :HD]
        values = kvs[k][0, HD:]
        bias = bias_ref[k]
        for j in range(QPK):
            s = tn(keys, qs_ref[0, j * HD : (j + 1) * HD]) + bias
            top = jnp.max(s, axis=0, keepdims=True)
            if fresh:
                m = top
                e = jnp.exp(s - m)
                l_s[j : j + 1] = jnp.sum(e, axis=0, keepdims=True)
                acc_s[j * HD : (j + 1) * HD] = nn(values, e.astype(BF))
            else:
                old = m_s[j : j + 1]
                m = jnp.maximum(old, top)
                fade = jnp.exp(old - m)
                e = jnp.exp(s - m)
                l_s[j : j + 1] = l_s[j : j + 1] * fade + jnp.sum(e, axis=0, keepdims=True)
                acc_s[j * HD : (j + 1) * HD] = acc_s[j * HD : (j + 1) * HD] * fade + nn(
                    values, e.astype(BF)
                )
            m_s[j : j + 1] = m

    fold(0, True)
    for k in range(1, ROWS):
        pl.when(sc[3 + k] != 0)(functools.partial(fold, k, False))
    for j in range(QPK):
        total = l_s[j : j + 1]
        o_ref[0, j * HD : (j + 1) * HD] = (acc_s[j * HD : (j + 1) * HD] / total).astype(BF)
        lse_ref[0, j : j + 1] = m_s[j : j + 1] + jnp.log(total)
    part = nn(w_ref[0, :, SLOT_W:], o_ref[0])

    @pl.when(g == 0)
    def _():
        h_ref[...] = x_ref[...].astype(F32) + part

    @pl.when(g != 0)
    def _():
        h_ref[...] += part

    @pl.when(g == GROUPS - 1)
    def _():
        h = h_ref[...]
        r2 = lax.rsqrt(jnp.sum(h * h, axis=0, keepdims=True) / D + EPSILON)
        r2_ref[...] = r2
        n2_ref[...] = (h * r2 * gain_ref[...]).astype(BF)


def row_sums(values):
    return lax.dot_general(
        jnp.ones((16, CP), F32), values, (((1,), (1,)), ((), ())),
        precision=lax.Precision.HIGHEST, preferred_element_type=F32,
    )


def attend_back_kernel(
    sc, qs_ref, kv0, kv1, kv2, kv3, bias_ref, w_ref, o_ref, lse_ref, n1_ref, cos_ref, sin_ref,
    dn_a, dn_b, dn_c, h_ref, r2_ref, gain_ref, dy_ref,
    dq_ref, d0, d1, d2, d3, dh_ref, gg_ref, pa0, pa1, pa2, pa3, datt_s, do_s, dl_s, dq_s,
):
    g = pl.program_id(0)
    kvs = (kv0, kv1, kv2, kv3)
    outs = (d0, d1, d2, d3)
    packs = (pa0, pa1, pa2, pa3)

    @pl.when(g == 0)
    def _():
        dn2 = dn_a[...].astype(F32) + dn_b[...].astype(F32) + dn_c[...].astype(F32)
        h = h_ref[...]
        r2 = r2_ref[...]
        weighted = dn2 * gain_ref[...]
        inner = jnp.sum(weighted * h, axis=0, keepdims=True)
        dh = dy_ref[...].astype(F32) + r2 * weighted - h * (r2 * r2 * r2 * inner / D)
        dh_ref[...] = dh
        datt_s[...] = dh.astype(BF)
        for b in range(ROWS):
            rows = slice(b * FB, (b + 1) * FB)
            gg_ref[b] = row_sums(dn2[rows] * h[rows] * r2)

    do_s[...] = tn(w_ref[0, :, SLOT_W:], datt_s[...]).astype(BF)
    for j in range(QPK):
        rows = slice(j * HD, (j + 1) * HD)
        dl_s[j : j + 1] = jnp.sum(
            do_s[rows].astype(F32) * o_ref[0, rows].astype(F32), axis=0, keepdims=True
        )

    def fold(k, fresh):
        keys = kvs[k][0, :HD]
        values = kvs[k][0, HD:]
        bias = bias_ref[k]
        dk = jnp.zeros((HD, CP), F32)
        dv = jnp.zeros((HD, CP), F32)
        for j in range(QPK):
            rows = slice(j * HD, (j + 1) * HD)
            s = tn(keys, qs_ref[0, rows]) + bias
            p = jnp.exp(s - lse_ref[0, j : j + 1])
            do_j = do_s[rows]
            dp = tn(values, do_j)
            ds = (p * (dp - dl_s[j : j + 1])).astype(BF)
            dv = dv + nt(do_j, p.astype(BF))
            dk = dk + nt(qs_ref[0, rows], ds)
            dq = nn(keys, ds)
            if fresh:
                dq_s[rows] = dq
            else:
                dq_s[rows] += dq
        outs[k][0, :HD] = dk.astype(outs[k].dtype)
        outs[k][0, HD:] = dv.astype(outs[k].dtype)

    fold(0, True)
    for k in range(1, ROWS):
        pl.when(sc[3 + k] != 0)(functools.partial(fold, k, False))

        @pl.when(sc[3 + k] == 0)
        def _(k=k):
            outs[k][...] = jnp.zeros(outs[k].shape, outs[k].dtype)

    cos_a = cos_ref[...]
    sin_a = sin_ref[...]
    for j in range(QPK):
        first, second = rope(
            dq_s[j * HD : j * HD + HALF] * HD**-0.5,
            dq_s[j * HD + HALF : (j + 1) * HD] * HD**-0.5,
            cos_a, -sin_a,
        )
        dq_ref[0, j * HD : j * HD + HALF] = first.astype(BF)
        dq_ref[0, j * HD + HALF : (j + 1) * HD] = second.astype(BF)

    for b in range(ROWS):
        rows = slice(b * FB, (b + 1) * FB)
        block = jnp.concatenate(
            [nt(dq_ref[0], n1_ref[rows]).astype(BF), nt(o_ref[0], datt_s[rows]).astype(BF)], axis=0
        )
        for k in range(ROWS):

            @pl.when(g == k)
            def _(k=k, block=block, b=b):
                packs[k][b, :AW] = block

        @pl.when(g == GROUPS - 1)
        def _(block=block, b=b):
            for k in range(ROWS):
                share = AW // ROWS
                for q in range(ROWS):

                    @pl.when((sc[0] ^ k) == q)
                    def _(k=k, q=q):
                        packs[k][b, AW:] = block[q * share : (q + 1) * share]


def final_kernel(
    sc, dq_ref, d0, d1, d2, w_ref, n1_ref, cos_ref, sin_ref, x_ref, r1_ref, gain_ref, dh_ref, gg_ref,
    pb0, pb1, pb2, pb3, out0, out1, out2, out3, dn_s, dpg_s, dx_s,
):
    g = pl.program_id(0)
    packs = (pb0, pb1, pb2, pb3)
    outs = (out0, out1, out2, out3)
    dkv = d0[0] + d1[0].astype(F32) + d2[0].astype(F32)
    first, second = rope(dkv[:HALF], dkv[HALF:HD], cos_ref[...], -sin_ref[...])
    dpg_s[:QW] = dq_ref[0]
    dpg_s[QW : QW + HALF] = first.astype(BF)
    dpg_s[QW + HALF : QW + HD] = second.astype(BF)
    dpg_s[QW + HD :] = dkv[HD:].astype(BF)
    part = nn(w_ref[0, :, :SLOT_W], dpg_s[...])

    @pl.when(g == 0)
    def _():
        dn_s[...] = part

    @pl.when(g != 0)
    def _():
        dn_s[...] += part

    for b in range(ROWS):
        block = nt(dpg_s[QW:], n1_ref[b * FB : (b + 1) * FB]).astype(BF)
        for k in range(ROWS):

            @pl.when(g == k)
            def _(k=k, block=block, b=b):
                packs[k][b, :KV] = block

        @pl.when(g == GROUPS - 1)
        def _(block=block, b=b):
            share = KV // ROWS
            for k in range(ROWS):
                for q in range(ROWS):

                    @pl.when((sc[0] ^ k) == q)
                    def _(k=k, q=q):
                        packs[k][b, KV : KV + share] = block[q * share : (q + 1) * share]

    @pl.when(g == GROUPS - 1)
    def _():
        dn1 = dn_s[...]
        x = x_ref[...].astype(F32)
        r1 = r1_ref[...]
        weighted = dn1 * gain_ref[...]
        inner = jnp.sum(weighted * x, axis=0, keepdims=True)
        dx = dh_ref[...] + r1 * weighted - x * (r1 * r1 * r1 * inner / D)
        dx_s[...] = dx.astype(BF)
        row = lax.broadcasted_iota(jnp.int32, (16, FB), 0)
        for b in range(ROWS):
            rows = slice(b * FB, (b + 1) * FB)
            sums = row_sums(dn1[rows] * x[rows] * r1)
            sums = jnp.where(row == 0, sums, jnp.where(row == 1, gg_ref[b], 0.0)).astype(BF)
            for k in range(ROWS):
                packs[k][b, KV + KV // ROWS :] = sums
        for k in range(ROWS):
            outs[k][...] = dx_s[rows_at(sc[0] ^ k)]


def mlp_kernel(offsets, count, made, *refs):
    if made:
        w = refs[0]
        refs = refs[1:]
    else:
        at = refs[0]
        pieces = refs[1 : 1 + offsets]
        refs = refs[1 + offsets :]
        w = refs[2 * count]
        refs = refs[: 2 * count] + refs[2 * count + 1 :]
        for i, piece in enumerate(pieces):
            w[pl.ds(pl.multiple_of(at[i], 16), piece.shape[0])] = piece[...]
    width = w.shape[1] // 3
    for i in range(count):
        n2 = refs[i]
        dy = refs[count + i]
        a_ref, dg_ref, du_ref, mlp_ref, dn_ref = refs[2 * count + 5 * i : 2 * count + 5 * i + 5]
        step = 128
        for f in range(0, width, step):
            cols = slice(f, f + step)
            gate = tn(w[:, f : f + step], n2[...])
            up = tn(w[:, width + f : width + f + step], n2[...])
            da = tn(w[:, 2 * width + f : 2 * width + f + step], dy[...])
            sigma = jax.nn.sigmoid(gate)
            silu = gate * sigma
            a_ref[cols] = (silu * up).astype(BF)
            dg_ref[cols] = (da * up * sigma * (1.0 + gate * (1.0 - sigma))).astype(BF)
            du_ref[cols] = (da * silu).astype(BF)
        dn_ref[...] = (nn(w[:, :width], dg_ref[...]) + nn(w[:, width : 2 * width], du_ref[...])).astype(BF)
        mlp_ref[...] = nn(w[:, 2 * width :], a_ref[...]).astype(BF)


def mlp_grad_kernel(*refs):
    n2s, dys, acts, gates, ups = (refs[ROWS * i : ROWS * (i + 1)] for i in range(5))
    out = refs[-1]
    width = acts[0].shape[0]
    step = 128
    for part, (left, right) in enumerate(((n2s, gates), (n2s, ups), (dys, acts))):
        for f in range(0, width, step):
            total = nt(left[0][...], right[0][f : f + step])
            for k in range(1, ROWS):
                total = total + nt(left[k][...], right[k][f : f + step])
            total = total.astype(BF)
            for b in range(ROWS):
                out[b, :, part * width + f : part * width + f + step] = total[b * FB : (b + 1) * FB]


def out_kernel(sc, h_ref, a, b, c, out0, out1, out2, out3, sum_s):
    sum_s[...] = (
        h_ref[...] + a[...].astype(F32) + b[...].astype(F32) + c[...].astype(F32)
    ).astype(BF)
    for k, out in enumerate((out0, out1, out2, out3)):
        out[...] = sum_s[rows_at(sc[0] ^ k)]


def grads_kernel(sc, a_ref, b_ref, oa0, oa1, oa2, oa3, ob0, ob1, ob2, ob3, qkv_ref, out_ref, gains_ref, oa_s, ob_s):
    ix = sc[0]
    share_a = AW // ROWS
    share_b = KV // ROWS
    for k in range(ROWS):
        oa_s[pl.ds(pl.multiple_of((ix ^ k) * share_a, 8), share_a)] = (oa0, oa1, oa2, oa3)[k][...]
        ob_s[pl.ds(pl.multiple_of((ix ^ k) * share_b, 8), share_b)] = (ob0, ob1, ob2, ob3)[k][...]
    live = (ix == sc[2]).astype(F32)
    oa = oa_s[...] * live
    ob = ob_s[...] * live
    qkv_ref[...] = jnp.transpose(
        jnp.concatenate([a_ref[:QW], b_ref[:KV], oa[:QW], ob], axis=0)
    )
    out_ref[...] = jnp.transpose(jnp.concatenate([a_ref[QW:AW], oa[QW:]], axis=0))
    gains_ref[...] = b_ref[KV + share_b : KV + share_b + 8]


def whole(*shape):
    return pl.BlockSpec(shape, lambda *_: (0,) * len(shape))


def per_group(*shape):
    return pl.BlockSpec((1,) + shape, lambda g, *_: (g,) + (0,) * len(shape))


def kv_blocks():
    def spec(k):
        return pl.BlockSpec((1, KV, CP), lambda g, *_: (jnp.where(g < ROWS, g ^ k, g), 0, 0))

    return [spec(k) for k in range(ROWS)]


def sds(shape, dtype):
    return jax.ShapeDtypeStruct(shape, dtype)


def simple(kernel, name, outs, *operands, scalars=None, scratch=(), limit=VMEM_LIMIT):
    specs = [pl.BlockSpec(memory_space=pltpu.VMEM)] * len(operands)
    if scalars is not None:
        specs = [pl.BlockSpec(memory_space=pltpu.SMEM)] + specs
        operands = (scalars,) + operands
    return pl.pallas_call(
        kernel,
        in_specs=specs,
        out_specs=[pl.BlockSpec(memory_space=pltpu.VMEM)] * len(outs),
        out_shape=list(outs),
        scratch_shapes=list(scratch),
        compiler_params=pltpu.CompilerParams(vmem_limit_bytes=limit),
        name=name,
    )(*operands)


def grouped(kernel, name, in_specs, outs, out_specs, scratch, sc, *operands):
    return pl.pallas_call(
        kernel,
        grid_spec=pltpu.PrefetchScalarGridSpec(
            num_scalar_prefetch=1,
            grid=(GROUPS,),
            in_specs=in_specs,
            out_specs=out_specs,
            scratch_shapes=scratch,
        ),
        out_shape=outs,
        compiler_params=pltpu.CompilerParams(vmem_limit_bytes=VMEM_LIMIT),
        name=name,
    )(sc, *operands)


def swap(values, bit):
    return lax.ppermute(values, "gx", [(i, i ^ bit) for i in range(ROWS)])


def row_gather(own):
    far = swap(own, 2)
    mate = swap(own, 1)
    return own, mate, far, swap(far, 1)


def row_terms(blocks):
    far = (blocks[2].astype(F32) + swap(blocks[3], 1).astype(F32)).astype(BF)
    return blocks[0], swap(blocks[1], 1), swap(far, 2)


def row_scatter(blocks):
    a, b, c = row_terms(blocks)
    return (a.astype(F32) + b.astype(F32) + c.astype(F32)).astype(BF)


def ring(values):
    return lax.ppermute(values, "gy", [(i, (i + 1) % ROWS) for i in range(ROWS)])


def ring_scatter(blocks, iy):
    def take(at):
        return lax.dynamic_index_in_dim(blocks, at % ROWS, 0, keepdims=False)

    moving = take(iy + 3)
    for s in range(ROWS - 1):
        moving = (ring(moving).astype(F32) + take(iy + 2 - s).astype(F32)).astype(BF)
    return moving


def dp_sum(values):
    if lax.axis_size("dp") == 2:
        return values.astype(F32) + lax.ppermute(values, "dp", [(0, 1), (1, 0)]).astype(F32)
    return lax.psum(values, "dp").astype(F32)


def to_tokens(pieces):
    out = []
    for k in range(ROWS):
        pairs = [(a * ROWS + b, (b ^ k) * ROWS + SEQ_MAP[a]) for a in range(ROWS) for b in range(ROWS)]
        out.append(lax.ppermute(pieces[k], ("gx", "gy"), pairs))
    return out


def to_features(pieces, sc):
    back = []
    for k in range(ROWS):
        pairs = [(a * ROWS + b, SEQ_BACK[b] * ROWS + (a ^ k)) for a in range(ROWS) for b in range(ROWS)]
        back.append(lax.ppermute(pieces[k], ("gx", "gy"), pairs))
    return simple(merge_kernel, "merge", [sds((FB, L), BF)], *back, scalars=sc)[0]


def per_device(
    tokens, segment_ids, slot_table, w_qkv, w_out, w_gate_up, w_down, gain_attn, gain_mlp, cotangent
):
    ix = lax.axis_index("gx")
    iy = lax.axis_index("gy")
    ff = w_down.shape[1]
    odd_row = jnp.sum(jnp.where(slot_table % 2 == 1, slot_table // 2, 0))

    seg = lax.ppermute(segment_ids, "gy", [(i, SEQ_MAP[i]) for i in range(ROWS)]).reshape(ROWS, CH)
    seg_own = lax.dynamic_index_in_dim(seg, ix, 0, keepdims=False)
    starts = [jnp.sum(seg < s).astype(jnp.int32) for s in range(SEGS)]
    first = sum(jnp.where(seg_own == s, starts[s], 0) for s in range(SEGS))
    at_own = jnp.arange(CP, dtype=jnp.int32)
    position = (ix * CH + at_own - jnp.pad(first, (0, CP - CH))).astype(F32)
    frequency = THETA_BASE ** (-2.0 * jnp.arange(HALF, dtype=F32) / HD)
    angles = frequency[:, None] * position[None, :]
    cos_a = jnp.cos(angles)
    sin_a = jnp.sin(angles)
    query_docs = jnp.pad(seg_own, (0, CP - CH), constant_values=-1)
    biases = []
    flags = []
    for k in range(ROWS):
        seg_k = lax.dynamic_index_in_dim(seg, ix ^ k, 0, keepdims=False)
        key_docs = jnp.pad(seg_k, (0, CP - CH), constant_values=-2)
        allowed = (key_docs[:, None] == query_docs[None, :]) & (
            ((ix ^ k) * CH + at_own)[:, None] <= (ix * CH + at_own)[None, :]
        )
        biases.append(jnp.where(allowed, 0.0, NEGATIVE).astype(F32))
        flags.append(((ix ^ k) <= ix) & (seg_k[CH - 1] >= seg_own[0]))
    bias = jnp.stack(biases)
    at = jnp.stack([ix, iy, odd_row]).astype(jnp.int32)
    sc = jnp.concatenate([at, jnp.stack(flags).astype(jnp.int32)])

    piece = sds((FB, CP), BF)
    pieces = simple(
        functools.partial(split_kernel, True), "split_tokens", [piece] * ROWS,
        tokens, gain_attn[:, None], gain_mlp[:, None], scalars=at,
    )
    toks = to_tokens(pieces)
    moving = jnp.concatenate([w_qkv[:, :SLOT_W], w_out[:, :QW]], axis=1)
    evens = [moving]
    for _ in range(ROWS - 1):
        evens.append(ring(evens[-1]))
    gathered = [row_gather(e) for e in evens]
    odd = jnp.concatenate([w_qkv[:, SLOT_W:], w_out[:, QW:]], axis=1)
    odd = jnp.where(ix == odd_row, odd, jnp.zeros_like(odd))
    quarter = row_scatter([lax.dynamic_slice(odd, (0, ODD * (ix ^ k)), (FB, ODD)) for k in range(ROWS)])
    quarters = [quarter]
    for _ in range(ROWS - 1):
        quarters.append(ring(quarters[-1]))
    odds = row_gather(jnp.concatenate(quarters, axis=0))
    x, n1, r1, gain_one, gain_two, w5, qs, kv = simple(
        qkv_kernel, "qkv",
        [
            sds((D, CP), BF), sds((D, CP), BF), sds((1, CP), F32), sds((D, 1), F32), sds((D, 1), F32),
            sds((GROUPS, D, PACK), BF), sds((GROUPS, QW, CP), BF), sds((GROUPS, KV, CP), BF),
        ],
        *toks, *[gathered[j][k] for k in range(ROWS) for j in range(ROWS)], *odds, cos_a, sin_a,
        scalars=at,
    )

    dy_pieces = simple(
        functools.partial(split_kernel, False), "split_grad", [piece] * ROWS, cotangent, scalars=at
    )
    dy = simple(join_kernel, "join", [sds((D, CP), BF)], *to_tokens(dy_pieces), scalars=at)[0]
    own = jnp.concatenate([w_gate_up[:, 0], w_gate_up[:, 1], w_down], axis=1)
    w_pieces = [own]
    offsets = [FB * iy]
    if lax.axis_size("dp") == 2:
        half = 128
        idp = lax.axis_index("dp")
        moving = lax.dynamic_slice(own, ((FB - half) * idp, 0), (half, 3 * ff))
        for j in range(1, ROWS):
            moving = ring(moving)
            base = FB * ((iy + ROWS - j) % ROWS)
            w_pieces += [moving, lax.ppermute(moving, "dp", [(0, 1), (1, 0)])]
            offsets += [base + (FB - half) * idp, base + (FB - half) * (1 - idp)]
    else:
        moving = own
        for j in range(1, ROWS):
            moving = ring(moving)
            w_pieces.append(moving)
            offsets.append(FB * ((iy + ROWS - j) % ROWS))
    offsets = jnp.stack(offsets).astype(jnp.int32)
    dys = row_gather(dy)

    kvs = row_gather(kv)
    o, lse, h, n2, r2 = grouped(
        attend_kernel, "attend",
        [per_group(QW, CP)] + kv_blocks()
        + [whole(ROWS, CP, CP), per_group(D, PACK), whole(D, CP), whole(D, 1)],
        [
            sds((GROUPS, QW, CP), BF), sds((GROUPS, 8, CP), F32), sds((D, CP), F32), sds((D, CP), BF),
            sds((1, CP), F32),
        ],
        [per_group(QW, CP), per_group(8, CP), whole(D, CP), whole(D, CP), whole(1, CP)],
        [pltpu.VMEM((8, CP), F32), pltpu.VMEM((8, CP), F32), pltpu.VMEM((QW, CP), F32)],
        sc, qs, *kvs, bias, w5, x, gain_two,
    )

    n2s = row_gather(n2)
    per_block = [sds((ff, CP), BF)] * 3 + [sds((D, CP), BF)] * 2
    near = simple(
        functools.partial(mlp_kernel, len(w_pieces), 2, False), "mlp_near",
        [sds((D, 3 * ff), BF)] + per_block * 2, *w_pieces, *n2s[:2], *dys[:2], scalars=offsets,
    )
    w_mlp = near[0]
    near = near[1:]
    far = simple(
        functools.partial(mlp_kernel, 0, 2, True), "mlp_far", per_block * 2, w_mlp, *n2s[2:], *dys[2:]
    )
    blocks = [near[:5], near[5:], far[:5], far[5:]]
    dn2_terms = row_terms([b[4] for b in blocks])
    g_mlp = simple(
        mlp_grad_kernel, "mlp_grad", [sds((ROWS, FB, 3 * ff), BF)],
        *n2s, *dys, *[b[0] for b in blocks], *[b[1] for b in blocks], *[b[2] for b in blocks],
    )[0]

    pack_a = sds((ROWS, AP, FB), BF)
    back = grouped(
        attend_back_kernel, "attend_back",
        [per_group(QW, CP)] + kv_blocks()
        + [whole(ROWS, CP, CP), per_group(D, PACK), per_group(QW, CP), per_group(8, CP), whole(D, CP),
           whole(HALF, CP), whole(HALF, CP)]
        + [whole(D, CP)] * 4 + [whole(1, CP), whole(D, 1), whole(D, CP)],
        [sds((GROUPS, QW, CP), BF), sds((GROUPS, KV, CP), F32)] + [sds((GROUPS, KV, CP), BF)] * 3
        + [sds((D, CP), F32), sds((ROWS, 16, FB), F32)] + [pack_a] * ROWS,
        [per_group(QW, CP)] + kv_blocks() + [whole(D, CP), whole(ROWS, 16, FB)]
        + [whole(ROWS, AP, FB)] * ROWS,
        [pltpu.VMEM((D, CP), BF), pltpu.VMEM((QW, CP), BF), pltpu.VMEM((8, CP), F32), pltpu.VMEM((QW, CP), F32)],
        sc, qs, *kvs, bias, w5, o, lse, n1, cos_a, sin_a, *dn2_terms, h, r2, gain_two, dy,
    )
    dq, dkv, dh, gg, packs_a = back[0], back[1:5], back[5], back[6], back[7:]
    dkv_terms = row_terms(dkv)
    final = grouped(
        final_kernel, "final",
        [per_group(QW, CP)] + [per_group(KV, CP)] * 3
        + [per_group(D, PACK), whole(D, CP), whole(HALF, CP), whole(HALF, CP), whole(D, CP), whole(1, CP),
           whole(D, 1), whole(D, CP), whole(ROWS, 16, FB)],
        [sds((ROWS, BP, FB), BF)] * ROWS + [piece] * ROWS,
        [whole(ROWS, BP, FB)] * ROWS + [whole(FB, CP)] * ROWS,
        [pltpu.VMEM((D, CP), F32), pltpu.VMEM((SLOT_W, CP), BF), pltpu.VMEM((D, CP), BF)],
        sc, dq, *dkv_terms, w5, n1, cos_a, sin_a, x, r1, gain_one, dh, gg,
    )
    packs_b, dx_pieces = final[:ROWS], final[ROWS:]
    input_grad = to_features(dx_pieces, at)

    out_pieces = simple(
        out_kernel, "out", [piece] * ROWS, h, *row_terms([b[3] for b in blocks]), scalars=at,
        scratch=[pltpu.VMEM((D, CP), BF)],
    )
    layer_out = to_features(out_pieces, at)

    g_mlp = dp_sum(ring_scatter(g_mlp, iy))
    g_a = dp_sum(ring_scatter(row_scatter(packs_a), iy))
    g_b = dp_sum(ring_scatter(row_scatter(packs_b), iy))
    grad_qkv, grad_out, grad_gains = simple(
        grads_kernel, "grads",
        [sds((FB, 2 * SLOT_W), F32), sds((FB, 2 * QW), F32), sds((8, FB), F32)],
        g_a[:AW], g_b, *row_gather(g_a[AW:]), *row_gather(g_b[KV : KV + KV // ROWS]), scalars=at,
        scratch=[pltpu.VMEM((AW, FB), F32), pltpu.VMEM((KV, FB), F32)],
    )
    grad_gate_up = jnp.stack([g_mlp[:, :ff], g_mlp[:, ff : 2 * ff]], axis=1)
    grad_down = g_mlp[:, 2 * ff :]
    return (
        layer_out,
        input_grad,
        grad_qkv,
        grad_out,
        grad_gate_up,
        grad_down,
        grad_gains[0],
        grad_gains[1],
    )


def solution(mesh):
    placed = (
        P("gy", ("dp", "gx")),
        P(("dp", "gy"), None),
        P(),
        P("gy", "gx"),
        P("gy", "gx"),
        P("gy", None, "gx"),
        P("gy", "gx"),
        P("gy"),
        P("gy"),
        P("gy", ("dp", "gx")),
    )
    return jax.shard_map(
        per_device,
        mesh=mesh,
        in_specs=placed,
        out_specs=(
            P("gy", ("dp", "gx")),
            P("gy", ("dp", "gx")),
            P("gy", "gx"),
            P("gy", "gx"),
            P("gy", None, "gx"),
            P("gy", "gx"),
            P("gy"),
            P("gy"),
        ),
        check_vma=False,
    )
```

```python
import functools

import jax
import jax.numpy as jnp
from jax import lax
from jax.experimental import pallas as pl
from jax.experimental.pallas import tpu as pltpu
from jax.sharding import PartitionSpec as P

D = 960
HD = 64
QPK = 3
L = 1408
SEGS = 4
QW = QPK * HD
SLOT_W = QW + 2 * HD
PACK = SLOT_W + QW
GROUPS = 5
ROWS = 4
CH = L // ROWS
CP = 384
FB = D // ROWS
ODD = PACK // ROWS

EPSILON = 1e-05
THETA_BASE = 100000.0
NEGATIVE = -1e30
SEQ_MAP = (0, 2, 1, 3)
SEQ_BACK = (0, 2, 1, 3)
BF = jnp.bfloat16
F32 = jnp.float32
VMEM_LIMIT = 58 * 1024 * 1024
HALF = HD // 2
AW = 2 * QW
AP = AW + AW // ROWS
KV = 2 * HD
BP = KV + KV // ROWS + 16


def tn(a, b):
    return lax.dot_general(a, b, (((0,), (0,)), ((), ())), preferred_element_type=F32)


def nn(a, b):
    return lax.dot_general(a, b, (((1,), (0,)), ((), ())), preferred_element_type=F32)


def nt(a, b):
    return lax.dot_general(a, b, (((1,), (1,)), ((), ())), preferred_element_type=F32)


def rows_at(block, size=FB):
    return pl.ds(pl.multiple_of(block * FB, 16), size)


def rope(a, b, cos_a, sin_a):
    return a * cos_a - b * sin_a, b * cos_a + a * sin_a


def split_kernel(with_tail, sc, *refs):
    t_ref = refs[0]
    outs = refs[-ROWS:]
    iy = sc[1]
    if with_tail:
        lane = lax.broadcasted_iota(jnp.int32, (FB, CP - CH), 1)
        tail = jnp.zeros((FB, CP - CH), F32)
        for i in range(2):
            rest = refs[1 + i][...]
            for part in range(3):
                piece = rest.astype(BF).astype(F32)
                rest = rest - piece
                tail = jnp.where(lane == 3 * i + part, piece, tail)
        tail = tail.astype(BF)
    else:
        tail = jnp.zeros((FB, CP - CH), BF)
    for q in range(ROWS):
        block = jnp.concatenate([t_ref[:, q * CH : (q + 1) * CH], tail], axis=1)
        for k in range(ROWS):

            @pl.when((iy ^ k) == q)
            def _(k=k, block=block):
                outs[k][...] = block


def join_kernel(sc, *refs):
    for k in range(ROWS):
        refs[ROWS][rows_at(sc[0] ^ k)] = refs[k][...]


def merge_kernel(sc, *refs):
    iy = sc[1]
    parts = []
    for q in range(ROWS):
        value = refs[0][:, :CH]
        for k in range(1, ROWS):
            value = jnp.where((iy ^ k) == q, refs[k][:, :CH], value)
        parts.append(value)
    refs[ROWS][...] = jnp.concatenate(parts, axis=1)


def qkv_kernel(sc, *refs):
    toks = refs[:4]
    even = refs[4]
    odds = refs[5:9]
    cos_ref, sin_ref = refs[9:11]
    x_ref, n1_ref, r1_ref, g1_ref, g2_ref, w5_ref, qs_ref, kv_ref = refs[11:]
    ix = sc[0]
    iy = sc[1]
    lane = lax.broadcasted_iota(jnp.int32, (FB, CP), 1)
    for k in range(ROWS):
        rows = rows_at(ix ^ k)
        piece = toks[k][...].astype(F32)
        x_ref[rows] = jnp.where(lane < CH, piece, 0.0).astype(BF)
        for i, out in enumerate((g1_ref, g2_ref)):
            here = (lane >= CH + 3 * i) & (lane < CH + 3 * i + 3)
            out[rows] = jnp.sum(jnp.where(here, piece, 0.0), axis=1, keepdims=True)
    x = x_ref[...].astype(F32)
    r1 = lax.rsqrt(jnp.sum(x * x, axis=0, keepdims=True) / D + EPSILON)
    r1_ref[...] = r1
    n1_ref[...] = (x * r1 * g1_ref[...]).astype(BF)
    for k in range(ROWS):
        w5_ref[k] = even[ix ^ k]
    for j in range(ROWS):
        rows = rows_at((iy + ROWS - j) % ROWS)
        for k in range(ROWS):
            lanes = pl.ds(pl.multiple_of((ix ^ k) * ODD, ODD), ODD)
            w5_ref[GROUPS - 1, rows, lanes] = odds[k][j * FB : (j + 1) * FB]
    cos_a = cos_ref[...]
    sin_a = sin_ref[...]
    for g in range(GROUPS):
        p = tn(w5_ref[g, :, :SLOT_W], n1_ref[...])
        for j in range(QPK + 1):
            first, second = rope(
                p[j * HD : j * HD + HALF], p[j * HD + HALF : (j + 1) * HD], cos_a, sin_a
            )
            first = first.astype(BF)
            second = second.astype(BF)
            if j < QPK:
                qs_ref[g, j * HD : j * HD + HALF] = (first.astype(F32) * HD**-0.5).astype(BF)
                qs_ref[g, j * HD + HALF : (j + 1) * HD] = (second.astype(F32) * HD**-0.5).astype(BF)
            else:
                kv_ref[g, :HALF] = first
                kv_ref[g, HALF:HD] = second
        kv_ref[g, HD:] = p[(QPK + 1) * HD :].astype(BF)


def attend_kernel(
    sc, qs_ref, kv0, kv1, kv2, kv3, bias_ref, w_ref, x_ref, gain_ref,
    o_ref, lse_ref, h_ref, n2_ref, r2_ref, m_s, l_s, acc_s,
):
    g = pl.program_id(0)
    kvs = (kv0, kv1, kv2, kv3)

    def fold(k, fresh):
        keys = kvs[k][0, :HD]
        values = kvs[k][0, HD:]
        bias = bias_ref[k]
        for j in range(QPK):
            s = tn(keys, qs_ref[0, j * HD : (j + 1) * HD]) + bias
            top = jnp.max(s, axis=0, keepdims=True)
            if fresh:
                m = top
                e = jnp.exp(s - m)
                l_s[j : j + 1] = jnp.sum(e, axis=0, keepdims=True)
                acc_s[j * HD : (j + 1) * HD] = nn(values, e.astype(BF))
            else:
                old = m_s[j : j + 1]
                m = jnp.maximum(old, top)
                fade = jnp.exp(old - m)
                e = jnp.exp(s - m)
                l_s[j : j + 1] = l_s[j : j + 1] * fade + jnp.sum(e, axis=0, keepdims=True)
                acc_s[j * HD : (j + 1) * HD] = acc_s[j * HD : (j + 1) * HD] * fade + nn(
                    values, e.astype(BF)
                )
            m_s[j : j + 1] = m

    fold(0, True)
    for k in range(1, ROWS):
        pl.when(sc[4 + k] != 0)(functools.partial(fold, k, False))
    for j in range(QPK):
        total = l_s[j : j + 1]
        o_ref[0, j * HD : (j + 1) * HD] = (acc_s[j * HD : (j + 1) * HD] / total).astype(BF)
        lse_ref[0, j : j + 1] = m_s[j : j + 1] + jnp.log(total)
    part = nn(w_ref[0, :, SLOT_W:], o_ref[0])

    @pl.when(g == 0)
    def _():
        h_ref[...] = x_ref[...].astype(F32) + part

    @pl.when(g != 0)
    def _():
        h_ref[...] += part

    @pl.when(g == GROUPS - 1)
    def _():
        h = h_ref[...]
        r2 = lax.rsqrt(jnp.sum(h * h, axis=0, keepdims=True) / D + EPSILON)
        r2_ref[...] = r2
        n2_ref[...] = (h * r2 * gain_ref[...]).astype(BF)


def row_sums(values):
    return lax.dot_general(
        jnp.ones((16, CP), F32), values, (((1,), (1,)), ((), ())),
        precision=lax.Precision.HIGHEST, preferred_element_type=F32,
    )


def attend_back_kernel(
    sc, qs_ref, kv0, kv1, kv2, kv3, bias_ref, w_ref, o_ref, lse_ref, n1_ref, cos_ref, sin_ref,
    dn_a, dn_b, dn_c, h_ref, r2_ref, gain_ref, dy_ref,
    dq_ref, d0, d1, d2, d3, dh_ref, gg_ref, pa0, pa1, pa2, pa3, datt_s, do_s, dl_s, dq_s,
):
    g = pl.program_id(0)
    kvs = (kv0, kv1, kv2, kv3)
    outs = (d0, d1, d2, d3)
    packs = (pa0, pa1, pa2, pa3)

    @pl.when(g == 0)
    def _():
        dn2 = dn_a[...].astype(F32) + dn_b[...].astype(F32) + dn_c[...].astype(F32)
        h = h_ref[...]
        r2 = r2_ref[...]
        weighted = dn2 * gain_ref[...]
        inner = jnp.sum(weighted * h, axis=0, keepdims=True)
        dh = dy_ref[...].astype(F32) + r2 * weighted - h * (r2 * r2 * r2 * inner / D)
        dh_ref[...] = dh
        datt_s[...] = dh.astype(BF)
        for b in range(ROWS):
            rows = slice(b * FB, (b + 1) * FB)
            gg_ref[b] = row_sums(dn2[rows] * h[rows] * r2)

    do_s[...] = tn(w_ref[0, :, SLOT_W:], datt_s[...]).astype(BF)
    for j in range(QPK):
        rows = slice(j * HD, (j + 1) * HD)
        dl_s[j : j + 1] = jnp.sum(
            do_s[rows].astype(F32) * o_ref[0, rows].astype(F32), axis=0, keepdims=True
        )

    def fold(k, fresh):
        keys = kvs[k][0, :HD]
        values = kvs[k][0, HD:]
        bias = bias_ref[k]
        dk = jnp.zeros((HD, CP), F32)
        dv = jnp.zeros((HD, CP), F32)
        for j in range(QPK):
            rows = slice(j * HD, (j + 1) * HD)
            s = tn(keys, qs_ref[0, rows]) + bias
            p = jnp.exp(s - lse_ref[0, j : j + 1])
            do_j = do_s[rows]
            dp = tn(values, do_j)
            ds = (p * (dp - dl_s[j : j + 1])).astype(BF)
            dv = dv + nt(do_j, p.astype(BF))
            dk = dk + nt(qs_ref[0, rows], ds)
            dq = nn(keys, ds)
            if fresh:
                dq_s[rows] = dq
            else:
                dq_s[rows] += dq
        outs[k][0, :HD] = dk.astype(outs[k].dtype)
        outs[k][0, HD:] = dv.astype(outs[k].dtype)

    fold(0, True)
    for k in range(1, ROWS):
        pl.when(sc[4 + k] != 0)(functools.partial(fold, k, False))

        @pl.when(sc[4 + k] == 0)
        def _(k=k):
            outs[k][...] = jnp.zeros(outs[k].shape, outs[k].dtype)

    cos_a = cos_ref[...]
    sin_a = sin_ref[...]
    for j in range(QPK):
        first, second = rope(
            dq_s[j * HD : j * HD + HALF] * HD**-0.5,
            dq_s[j * HD + HALF : (j + 1) * HD] * HD**-0.5,
            cos_a, -sin_a,
        )
        dq_ref[0, j * HD : j * HD + HALF] = first.astype(BF)
        dq_ref[0, j * HD + HALF : (j + 1) * HD] = second.astype(BF)

    for b in range(ROWS):
        rows = slice(b * FB, (b + 1) * FB)
        block = jnp.concatenate(
            [nt(dq_ref[0], n1_ref[rows]).astype(BF), nt(o_ref[0], datt_s[rows]).astype(BF)], axis=0
        )
        for k in range(ROWS):

            @pl.when(g == k)
            def _(k=k, block=block, b=b):
                packs[k][b, :AW] = block

        @pl.when(g == GROUPS - 1)
        def _(block=block, b=b):
            for k in range(ROWS):
                share = AW // ROWS
                for q in range(ROWS):

                    @pl.when((sc[0] ^ k) == q)
                    def _(k=k, q=q):
                        packs[k][b, AW:] = block[q * share : (q + 1) * share]


def final_kernel(
    sc, dq_ref, d0, d1, d2, w_ref, n1_ref, cos_ref, sin_ref, x_ref, r1_ref, gain_ref, dh_ref, gg_ref,
    pb0, pb1, pb2, pb3, out0, out1, out2, out3, dn_s, dpg_s, dx_s,
):
    g = pl.program_id(0)
    packs = (pb0, pb1, pb2, pb3)
    outs = (out0, out1, out2, out3)
    dkv = d0[0] + d1[0].astype(F32) + d2[0].astype(F32)
    first, second = rope(dkv[:HALF], dkv[HALF:HD], cos_ref[...], -sin_ref[...])
    dpg_s[:QW] = dq_ref[0]
    dpg_s[QW : QW + HALF] = first.astype(BF)
    dpg_s[QW + HALF : QW + HD] = second.astype(BF)
    dpg_s[QW + HD :] = dkv[HD:].astype(BF)
    part = nn(w_ref[0, :, :SLOT_W], dpg_s[...])

    @pl.when(g == 0)
    def _():
        dn_s[...] = part

    @pl.when(g != 0)
    def _():
        dn_s[...] += part

    for b in range(ROWS):
        block = nt(dpg_s[QW:], n1_ref[b * FB : (b + 1) * FB]).astype(BF)
        for k in range(ROWS):

            @pl.when(g == k)
            def _(k=k, block=block, b=b):
                packs[k][b, :KV] = block

        @pl.when(g == GROUPS - 1)
        def _(block=block, b=b):
            share = KV // ROWS
            for k in range(ROWS):
                for q in range(ROWS):

                    @pl.when((sc[0] ^ k) == q)
                    def _(k=k, q=q):
                        packs[k][b, KV : KV + share] = block[q * share : (q + 1) * share]

    @pl.when(g == GROUPS - 1)
    def _():
        dn1 = dn_s[...]
        x = x_ref[...].astype(F32)
        r1 = r1_ref[...]
        weighted = dn1 * gain_ref[...]
        inner = jnp.sum(weighted * x, axis=0, keepdims=True)
        dx = dh_ref[...] + r1 * weighted - x * (r1 * r1 * r1 * inner / D)
        dx_s[...] = dx.astype(BF)
        row = lax.broadcasted_iota(jnp.int32, (16, FB), 0)
        for b in range(ROWS):
            rows = slice(b * FB, (b + 1) * FB)
            sums = row_sums(dn1[rows] * x[rows] * r1)
            sums = jnp.where(row == 0, sums, jnp.where(row == 1, gg_ref[b], 0.0)).astype(BF)
            for k in range(ROWS):
                packs[k][b, KV + KV // ROWS :] = sums
        for k in range(ROWS):
            outs[k][...] = dx_s[rows_at(sc[0] ^ k)]


def mlp_kernel(count, halves, sc, *refs):
    if halves:
        w = refs[-1]
        part = refs[0].shape[0] // ROWS
        for h in range(2):
            shift = (FB - part) * (sc[3] if h == 0 else 1 - sc[3])
            for b in range(ROWS):
                w[pl.ds(pl.multiple_of(b * FB + shift, 16), part)] = refs[h][b * part : (b + 1) * part]
        wd = refs[2]
        refs = refs[3:-1]
    else:
        w, wd = refs[:2]
        refs = refs[2:]
    width = wd.shape[1]
    for i in range(count):
        n2 = refs[i]
        dy = refs[count + i]
        a_ref, dg_ref, du_ref, mlp_ref, dn_ref = refs[2 * count + 5 * i : 2 * count + 5 * i + 5]
        step = 128
        for f in range(0, width, step):
            cols = slice(f, f + step)
            gate = tn(w[:, f : f + step], n2[...])
            up = tn(w[:, width + f : width + f + step], n2[...])
            da = tn(wd[:, cols], dy[...])
            sigma = jax.nn.sigmoid(gate)
            silu = gate * sigma
            a_ref[cols] = (silu * up).astype(BF)
            dg_ref[cols] = (da * up * sigma * (1.0 + gate * (1.0 - sigma))).astype(BF)
            du_ref[cols] = (da * silu).astype(BF)
        dn_ref[...] = (nn(w[:, :width], dg_ref[...]) + nn(w[:, width : 2 * width], du_ref[...])).astype(BF)
        mlp_ref[...] = nn(wd[...], a_ref[...]).astype(BF)


def mlp_grad_kernel(*refs):
    n2s, dys, acts, gates, ups = (refs[ROWS * i : ROWS * (i + 1)] for i in range(5))
    out = refs[-1]
    width = acts[0].shape[0]
    step = 128
    for part, (left, right) in enumerate(((n2s, gates), (n2s, ups), (dys, acts))):
        for f in range(0, width, step):
            total = nt(left[0][...], right[0][f : f + step])
            for k in range(1, ROWS):
                total = total + nt(left[k][...], right[k][f : f + step])
            out[:, part * width + f : part * width + f + step] = total.astype(BF)


def out_kernel(sc, h_ref, a, b, c, out0, out1, out2, out3, sum_s):
    sum_s[...] = (
        h_ref[...] + a[...].astype(F32) + b[...].astype(F32) + c[...].astype(F32)
    ).astype(BF)
    for k, out in enumerate((out0, out1, out2, out3)):
        out[...] = sum_s[rows_at(sc[0] ^ k)]


def grads_kernel(sc, a_ref, b_ref, oa0, oa1, oa2, oa3, ob0, ob1, ob2, ob3, qkv_ref, out_ref, gains_ref, oa_s, ob_s):
    ix = sc[0]
    share_a = AW // ROWS
    share_b = KV // ROWS
    for k in range(ROWS):
        oa_s[pl.ds(pl.multiple_of((ix ^ k) * share_a, 8), share_a)] = (oa0, oa1, oa2, oa3)[k][...]
        ob_s[pl.ds(pl.multiple_of((ix ^ k) * share_b, 8), share_b)] = (ob0, ob1, ob2, ob3)[k][...]
    live = (ix == sc[2]).astype(F32)
    oa = oa_s[...] * live
    ob = ob_s[...] * live
    qkv_ref[...] = jnp.transpose(
        jnp.concatenate([a_ref[:QW], b_ref[:KV], oa[:QW], ob], axis=0)
    )
    out_ref[...] = jnp.transpose(jnp.concatenate([a_ref[QW:AW], oa[QW:]], axis=0))
    gains_ref[...] = b_ref[KV + share_b : KV + share_b + 8]


def whole(*shape):
    return pl.BlockSpec(shape, lambda *_: (0,) * len(shape))


def per_group(*shape):
    return pl.BlockSpec((1,) + shape, lambda g, *_: (g,) + (0,) * len(shape))


def kv_blocks():
    def spec(k):
        return pl.BlockSpec((1, KV, CP), lambda g, *_: (jnp.where(g < ROWS, g ^ k, g), 0, 0))

    return [spec(k) for k in range(ROWS)]


def sds(shape, dtype):
    return jax.ShapeDtypeStruct(shape, dtype)


def simple(kernel, name, outs, *operands, scalars=None, scratch=(), limit=VMEM_LIMIT):
    specs = [pl.BlockSpec(memory_space=pltpu.VMEM)] * len(operands)
    if scalars is not None:
        specs = [pl.BlockSpec(memory_space=pltpu.SMEM)] + specs
        operands = (scalars,) + operands
    return pl.pallas_call(
        kernel,
        in_specs=specs,
        out_specs=[pl.BlockSpec(memory_space=pltpu.VMEM)] * len(outs),
        out_shape=list(outs),
        scratch_shapes=list(scratch),
        compiler_params=pltpu.CompilerParams(vmem_limit_bytes=limit),
        name=name,
    )(*operands)


def grouped(kernel, name, in_specs, outs, out_specs, scratch, sc, *operands):
    return pl.pallas_call(
        kernel,
        grid_spec=pltpu.PrefetchScalarGridSpec(
            num_scalar_prefetch=1,
            grid=(GROUPS,),
            in_specs=in_specs,
            out_specs=out_specs,
            scratch_shapes=scratch,
        ),
        out_shape=outs,
        compiler_params=pltpu.CompilerParams(vmem_limit_bytes=VMEM_LIMIT),
        name=name,
    )(sc, *operands)


def swap(values, bit):
    return lax.ppermute(values, "gx", [(i, i ^ bit) for i in range(ROWS)])


def row_gather(own):
    far = swap(own, 2)
    mate = swap(own, 1)
    return own, mate, far, swap(far, 1)


def after(values, *first):
    return lax.optimization_barrier((values,) + first)[0]


def row_terms(blocks, first=()):
    far = (blocks[2].astype(F32) + swap(blocks[3], 1).astype(F32)).astype(BF)
    if first:
        far = after(far, *first)
    return blocks[0], swap(blocks[1], 1), swap(far, 2)


def row_scatter(blocks, first=()):
    a, b, c = row_terms(blocks, first)
    return (a.astype(F32) + b.astype(F32) + c.astype(F32)).astype(BF)


def ring(values):
    return lax.ppermute(values, "gy", [(i, (i + 1) % ROWS) for i in range(ROWS)])


def ring_scatter(blocks, iy):
    def take(at):
        return lax.dynamic_index_in_dim(blocks, at % ROWS, 0, keepdims=False)

    moving = take(iy + 3)
    for s in range(ROWS - 1):
        moving = (ring(moving).astype(F32) + take(iy + 2 - s).astype(F32)).astype(BF)
    return moving


def dp_sum(values):
    if lax.axis_size("dp") == 2:
        return values.astype(F32) + lax.ppermute(values, "dp", [(0, 1), (1, 0)]).astype(F32)
    return lax.psum(values, "dp").astype(F32)


def to_tokens(pieces):
    out = []
    for k in range(ROWS):
        pairs = [(a * ROWS + b, (b ^ k) * ROWS + SEQ_MAP[a]) for a in range(ROWS) for b in range(ROWS)]
        out.append(lax.ppermute(pieces[k], ("gx", "gy"), pairs))
    return out


def to_features(pieces, sc):
    back = []
    for k in range(ROWS):
        pairs = [(a * ROWS + b, SEQ_BACK[b] * ROWS + (a ^ k)) for a in range(ROWS) for b in range(ROWS)]
        back.append(lax.ppermute(pieces[k], ("gx", "gy"), pairs))
    return simple(merge_kernel, "merge", [sds((FB, L), BF)], *back, scalars=sc)[0]


def per_device(
    tokens, segment_ids, slot_table, w_qkv, w_out, w_gate_up, w_down, gain_attn, gain_mlp, cotangent
):
    ix = lax.axis_index("gx")
    iy = lax.axis_index("gy")
    ff = w_down.shape[1]
    odd_row = jnp.sum(jnp.where(slot_table % 2 == 1, slot_table // 2, 0))

    seg = lax.ppermute(segment_ids, "gy", [(i, SEQ_MAP[i]) for i in range(ROWS)]).reshape(ROWS, CH)
    seg_own = lax.dynamic_index_in_dim(seg, ix, 0, keepdims=False)
    starts = [jnp.sum(seg < s).astype(jnp.int32) for s in range(SEGS)]
    first = sum(jnp.where(seg_own == s, starts[s], 0) for s in range(SEGS))
    at_own = jnp.arange(CP, dtype=jnp.int32)
    position = (ix * CH + at_own - jnp.pad(first, (0, CP - CH))).astype(F32)
    frequency = THETA_BASE ** (-2.0 * jnp.arange(HALF, dtype=F32) / HD)
    angles = frequency[:, None] * position[None, :]
    cos_a = jnp.cos(angles)
    sin_a = jnp.sin(angles)
    query_docs = jnp.pad(seg_own, (0, CP - CH), constant_values=-1)
    biases = []
    flags = []
    for k in range(ROWS):
        seg_k = lax.dynamic_index_in_dim(seg, ix ^ k, 0, keepdims=False)
        key_docs = jnp.pad(seg_k, (0, CP - CH), constant_values=-2)
        allowed = (key_docs[:, None] == query_docs[None, :]) & (
            ((ix ^ k) * CH + at_own)[:, None] <= (ix * CH + at_own)[None, :]
        )
        biases.append(jnp.where(allowed, 0.0, NEGATIVE).astype(F32))
        flags.append(((ix ^ k) <= ix) & (seg_k[CH - 1] >= seg_own[0]))
    bias = jnp.stack(biases)
    idp = lax.axis_index("dp")
    at = jnp.stack([ix, iy, odd_row, idp]).astype(jnp.int32)
    sc = jnp.concatenate([at, jnp.stack(flags).astype(jnp.int32)])

    piece = sds((FB, CP), BF)
    pieces = simple(
        functools.partial(split_kernel, True), "split_tokens", [piece] * ROWS,
        tokens, gain_attn[:, None], gain_mlp[:, None], scalars=at,
    )
    toks = to_tokens(pieces)
    even = lax.all_gather(
        jnp.concatenate([w_qkv[:, :SLOT_W], w_out[:, :QW]], axis=1), ("gx", "gy"), axis=0, tiled=True
    ).reshape(ROWS, D, PACK)
    odd = jnp.concatenate([w_qkv[:, SLOT_W:], w_out[:, QW:]], axis=1)
    odd = after(jnp.where(ix == odd_row, odd, jnp.zeros_like(odd)), pieces[0])
    quarter = row_scatter([lax.dynamic_slice(odd, (0, ODD * (ix ^ k)), (FB, ODD)) for k in range(ROWS)])
    quarters = [quarter]
    for _ in range(ROWS - 1):
        quarters.append(ring(quarters[-1]))
    odds = row_gather(jnp.concatenate(quarters, axis=0))
    x, n1, r1, gain_one, gain_two, w5, qs, kv = simple(
        qkv_kernel, "qkv",
        [
            sds((D, CP), BF), sds((D, CP), BF), sds((1, CP), F32), sds((D, 1), F32), sds((D, 1), F32),
            sds((GROUPS, D, PACK), BF), sds((GROUPS, QW, CP), BF), sds((GROUPS, KV, CP), BF),
        ],
        *toks, even, *odds, cos_a, sin_a,
        scalars=at,
    )

    dy_pieces = simple(
        functools.partial(split_kernel, False), "split_grad", [piece] * ROWS,
        after(cotangent, pieces[0]), scalars=at,
    )
    dy = simple(join_kernel, "join", [sds((D, CP), BF)], *to_tokens(dy_pieces), scalars=at)[0]
    w_gu = jnp.concatenate([w_gate_up[:, 0], w_gate_up[:, 1]], axis=1)
    halves = lax.axis_size("dp") == 2
    if halves:
        w_gu = lax.dynamic_slice(w_gu, ((FB - 128) * idp, 0), (128, 2 * ff))
    w_gu = [lax.all_gather(w_gu, "gy", axis=0, tiled=True)]
    if halves:
        w_gu.append(lax.ppermute(w_gu[0], "dp", [(0, 1), (1, 0)]))
    w_d = lax.all_gather(w_down, "gy", axis=0, tiled=True)

    kvs = row_gather(kv)
    dys = row_gather(after(dy, kvs[2]))
    o, lse, h, n2, r2 = grouped(
        attend_kernel, "attend",
        [per_group(QW, CP)] + kv_blocks()
        + [whole(ROWS, CP, CP), per_group(D, PACK), whole(D, CP), whole(D, 1)],
        [
            sds((GROUPS, QW, CP), BF), sds((GROUPS, 8, CP), F32), sds((D, CP), F32), sds((D, CP), BF),
            sds((1, CP), F32),
        ],
        [per_group(QW, CP), per_group(8, CP), whole(D, CP), whole(D, CP), whole(1, CP)],
        [pltpu.VMEM((8, CP), F32), pltpu.VMEM((8, CP), F32), pltpu.VMEM((QW, CP), F32)],
        sc, qs, *kvs, bias, w5, x, gain_two,
    )

    n2s = row_gather(n2)
    per_block = [sds((ff, CP), BF)] * 3 + [sds((D, CP), BF)] * 2
    def feed_forward(name, some_n2, some_dy):
        return simple(
            functools.partial(mlp_kernel, 2, halves), name, per_block * 2, *w_gu, w_d, *some_n2, *some_dy,
            scalars=at, scratch=[pltpu.VMEM((D, 2 * ff), BF)] if halves else [],
        )

    near = feed_forward("mlp_near", n2s[:2], dys[:2])
    far = feed_forward("mlp_far", n2s[2:], dys[2:])
    blocks = [near[:5], near[5:], far[:5], far[5:]]
    dn2_terms = row_terms([b[4] for b in blocks])
    g_mlp = simple(
        mlp_grad_kernel, "mlp_grad", [sds((D, 3 * ff), BF)],
        *n2s, *dys, *[b[0] for b in blocks], *[b[1] for b in blocks], *[b[2] for b in blocks],
    )[0]

    dn2_terms = list(dn2_terms)
    dn2_terms[1] = after(dn2_terms[1], g_mlp)
    pack_a = sds((ROWS, AP, FB), BF)
    back = grouped(
        attend_back_kernel, "attend_back",
        [per_group(QW, CP)] + kv_blocks()
        + [whole(ROWS, CP, CP), per_group(D, PACK), per_group(QW, CP), per_group(8, CP), whole(D, CP),
           whole(HALF, CP), whole(HALF, CP)]
        + [whole(D, CP)] * 4 + [whole(1, CP), whole(D, 1), whole(D, CP)],
        [sds((GROUPS, QW, CP), BF), sds((GROUPS, KV, CP), F32)] + [sds((GROUPS, KV, CP), BF)] * 3
        + [sds((D, CP), F32), sds((ROWS, 16, FB), F32)] + [pack_a] * ROWS,
        [per_group(QW, CP)] + kv_blocks() + [whole(D, CP), whole(ROWS, 16, FB)]
        + [whole(ROWS, AP, FB)] * ROWS,
        [pltpu.VMEM((D, CP), BF), pltpu.VMEM((QW, CP), BF), pltpu.VMEM((8, CP), F32), pltpu.VMEM((QW, CP), F32)],
        sc, qs, *kvs, bias, w5, o, lse, n1, cos_a, sin_a, *dn2_terms, h, r2, gain_two, dy,
    )
    dq, dkv, dh, gg, packs_a = back[0], back[1:5], back[5], back[6], back[7:]
    out_pieces = simple(
        out_kernel, "out", [piece] * ROWS, h, *row_terms([b[3] for b in blocks], (dn2_terms[2],)), scalars=at,
        scratch=[pltpu.VMEM((D, CP), BF)],
    )
    layer_out = to_features(out_pieces, at)

    dkv_terms = list(row_terms(dkv))
    dkv_terms[0] = after(dkv_terms[0], out_pieces[0])
    final = grouped(
        final_kernel, "final",
        [per_group(QW, CP)] + [per_group(KV, CP)] * 3
        + [per_group(D, PACK), whole(D, CP), whole(HALF, CP), whole(HALF, CP), whole(D, CP), whole(1, CP),
           whole(D, 1), whole(D, CP), whole(ROWS, 16, FB)],
        [sds((ROWS, BP, FB), BF)] * ROWS + [piece] * ROWS,
        [whole(ROWS, BP, FB)] * ROWS + [whole(FB, CP)] * ROWS,
        [pltpu.VMEM((D, CP), F32), pltpu.VMEM((SLOT_W, CP), BF), pltpu.VMEM((D, CP), BF)],
        sc, dq, *dkv_terms, w5, n1, cos_a, sin_a, x, r1, gain_one, dh, gg,
    )
    packs_b, dx_pieces = final[:ROWS], final[ROWS:]
    input_grad = to_features(dx_pieces, at)

    g_mlp = dp_sum(lax.psum_scatter(g_mlp, "gy", scatter_dimension=0, tiled=True))
    g_a = dp_sum(ring_scatter(row_scatter(packs_a, (dkv_terms[2],)), iy))
    g_b = dp_sum(ring_scatter(row_scatter(packs_b), iy))
    grad_qkv, grad_out, grad_gains = simple(
        grads_kernel, "grads",
        [sds((FB, 2 * SLOT_W), F32), sds((FB, 2 * QW), F32), sds((8, FB), F32)],
        g_a[:AW], g_b, *row_gather(g_a[AW:]), *row_gather(g_b[KV : KV + KV // ROWS]), scalars=at,
        scratch=[pltpu.VMEM((AW, FB), F32), pltpu.VMEM((KV, FB), F32)],
    )
    grad_gate_up = jnp.stack([g_mlp[:, :ff], g_mlp[:, ff : 2 * ff]], axis=1)
    grad_down = g_mlp[:, 2 * ff :]
    return (
        layer_out,
        input_grad,
        grad_qkv,
        grad_out,
        grad_gate_up,
        grad_down,
        grad_gains[0],
        grad_gains[1],
    )


def solution(mesh):
    placed = (
        P("gy", ("dp", "gx")),
        P(("dp", "gy"), None),
        P(),
        P("gy", "gx"),
        P("gy", "gx"),
        P("gy", None, "gx"),
        P("gy", "gx"),
        P("gy"),
        P("gy"),
        P("gy", ("dp", "gx")),
    )
    return jax.shard_map(
        per_device,
        mesh=mesh,
        in_specs=placed,
        out_specs=(
            P("gy", ("dp", "gx")),
            P("gy", ("dp", "gx")),
            P("gy", "gx"),
            P("gy", "gx"),
            P("gy", None, "gx"),
            P("gy", "gx"),
            P("gy"),
            P("gy"),
        ),
        check_vma=False,
    )
```

```python
import functools

import jax
import jax.numpy as jnp
from jax import lax
from jax.experimental import pallas as pl
from jax.experimental.pallas import tpu as pltpu
from jax.sharding import PartitionSpec as P

D = 960
HD = 64
QPK = 3
L = 1408
SEGS = 4
QW = QPK * HD
SLOT_W = QW + 2 * HD
PACK = SLOT_W + QW
GROUPS = 5
ROWS = 4
CH = L // ROWS
CP = 384
FB = D // ROWS
ODD = PACK // ROWS

EPSILON = 1e-05
THETA_BASE = 100000.0
NEGATIVE = -1e30
SEQ_MAP = (0, 2, 1, 3)
SEQ_BACK = (0, 2, 1, 3)
BF = jnp.bfloat16
F32 = jnp.float32
VMEM_LIMIT = 58 * 1024 * 1024
HALF = HD // 2
AW = 2 * QW
AP = AW + AW // ROWS
KV = 2 * HD
BP = KV + KV // ROWS + 16


def tn(a, b):
    return lax.dot_general(a, b, (((0,), (0,)), ((), ())), preferred_element_type=F32)


def nn(a, b):
    return lax.dot_general(a, b, (((1,), (0,)), ((), ())), preferred_element_type=F32)


def nt(a, b):
    return lax.dot_general(a, b, (((1,), (1,)), ((), ())), preferred_element_type=F32)


def rows_at(block, size=FB):
    return pl.ds(pl.multiple_of(block * FB, 16), size)


def rope(a, b, cos_a, sin_a):
    return a * cos_a - b * sin_a, b * cos_a + a * sin_a


def split_kernel(with_tail, sc, *refs):
    t_ref = refs[0]
    outs = refs[-ROWS:]
    iy = sc[1]
    if with_tail:
        lane = lax.broadcasted_iota(jnp.int32, (FB, CP - CH), 1)
        tail = jnp.zeros((FB, CP - CH), F32)
        for i in range(2):
            rest = refs[1 + i][...]
            for part in range(3):
                piece = rest.astype(BF).astype(F32)
                rest = rest - piece
                tail = jnp.where(lane == 3 * i + part, piece, tail)
        tail = tail.astype(BF)
    else:
        tail = jnp.zeros((FB, CP - CH), BF)
    for q in range(ROWS):
        block = jnp.concatenate([t_ref[:, q * CH : (q + 1) * CH], tail], axis=1)
        for k in range(ROWS):

            @pl.when((iy ^ k) == q)
            def _(k=k, block=block):
                outs[k][...] = block


def join_kernel(sc, *refs):
    for k in range(ROWS):
        refs[ROWS][rows_at(sc[0] ^ k)] = refs[k][...]


def merge_kernel(sc, *refs):
    iy = sc[1]
    for i in range(2):
        rows = slice(i * FB, (i + 1) * FB)
        parts = []
        for q in range(ROWS):
            value = refs[0][rows, :CH]
            for k in range(1, ROWS):
                value = jnp.where((iy ^ k) == q, refs[k][rows, :CH], value)
            parts.append(value)
        refs[ROWS + i][...] = jnp.concatenate(parts, axis=1)


def qkv_kernel(sc, *refs):
    toks = refs[:4]
    w_all = refs[4]
    cos_ref, sin_ref = refs[5:7]
    x_ref, n1_ref, r1_ref, g1_ref, g2_ref, w5_ref, qs_ref, kv_ref = refs[7:]
    ix = sc[0]
    lane = lax.broadcasted_iota(jnp.int32, (FB, CP), 1)
    for k in range(ROWS):
        rows = rows_at(ix ^ k)
        piece = toks[k][...].astype(F32)
        x_ref[rows] = jnp.where(lane < CH, piece, 0.0).astype(BF)
        for i, out in enumerate((g1_ref, g2_ref)):
            here = (lane >= CH + 3 * i) & (lane < CH + 3 * i + 3)
            out[rows] = jnp.sum(jnp.where(here, piece, 0.0), axis=1, keepdims=True)
    x = x_ref[...].astype(F32)
    r1 = lax.rsqrt(jnp.sum(x * x, axis=0, keepdims=True) / D + EPSILON)
    r1_ref[...] = r1
    n1_ref[...] = (x * r1 * g1_ref[...]).astype(BF)
    for k in range(ROWS):
        w5_ref[k] = w_all[ix ^ k, :, :PACK]
        w5_ref[GROUPS - 1, :, k * ODD : (k + 1) * ODD] = w_all[k, :, PACK:]
    cos_a = cos_ref[...]
    sin_a = sin_ref[...]
    for g in range(GROUPS):
        p = tn(w5_ref[g, :, :SLOT_W], n1_ref[...])
        for j in range(QPK + 1):
            first, second = rope(
                p[j * HD : j * HD + HALF], p[j * HD + HALF : (j + 1) * HD], cos_a, sin_a
            )
            first = first.astype(BF)
            second = second.astype(BF)
            if j < QPK:
                qs_ref[g, j * HD : j * HD + HALF] = (first.astype(F32) * HD**-0.5).astype(BF)
                qs_ref[g, j * HD + HALF : (j + 1) * HD] = (second.astype(F32) * HD**-0.5).astype(BF)
            else:
                kv_ref[g, :HALF] = first
                kv_ref[g, HALF:HD] = second
        kv_ref[g, HD:] = p[(QPK + 1) * HD :].astype(BF)


def attend_kernel(
    sc, qs_ref, kv0, kv1, kv2, kv3, bias_ref, w_ref, x_ref, gain_ref,
    o_ref, lse_ref, h_ref, n2_ref, r2_ref, m_s, l_s, acc_s,
):
    g = pl.program_id(0)
    kvs = (kv0, kv1, kv2, kv3)

    def fold(k, fresh):
        keys = kvs[k][0, :HD]
        values = kvs[k][0, HD:]
        bias = bias_ref[k]
        for j in range(QPK):
            s = tn(keys, qs_ref[0, j * HD : (j + 1) * HD]) + bias
            top = jnp.max(s, axis=0, keepdims=True)
            if fresh:
                m = top
                e = jnp.exp(s - m)
                l_s[j : j + 1] = jnp.sum(e, axis=0, keepdims=True)
                acc_s[j * HD : (j + 1) * HD] = nn(values, e.astype(BF))
            else:
                old = m_s[j : j + 1]
                m = jnp.maximum(old, top)
                fade = jnp.exp(old - m)
                e = jnp.exp(s - m)
                l_s[j : j + 1] = l_s[j : j + 1] * fade + jnp.sum(e, axis=0, keepdims=True)
                acc_s[j * HD : (j + 1) * HD] = acc_s[j * HD : (j + 1) * HD] * fade + nn(
                    values, e.astype(BF)
                )
            m_s[j : j + 1] = m

    fold(0, True)
    for k in range(1, ROWS):
        pl.when(sc[4 + k] != 0)(functools.partial(fold, k, False))
    for j in range(QPK):
        total = l_s[j : j + 1]
        o_ref[0, j * HD : (j + 1) * HD] = (acc_s[j * HD : (j + 1) * HD] / total).astype(BF)
        lse_ref[0, j : j + 1] = m_s[j : j + 1] + jnp.log(total)
    part = nn(w_ref[0, :, SLOT_W:], o_ref[0])

    @pl.when(g == 0)
    def _():
        h_ref[...] = x_ref[...].astype(F32) + part

    @pl.when(g != 0)
    def _():
        h_ref[...] += part

    @pl.when(g == GROUPS - 1)
    def _():
        h = h_ref[...]
        r2 = lax.rsqrt(jnp.sum(h * h, axis=0, keepdims=True) / D + EPSILON)
        r2_ref[...] = r2
        n2_ref[...] = (h * r2 * gain_ref[...]).astype(BF)


def row_sums(values):
    return lax.dot_general(
        jnp.ones((16, CP), F32), values, (((1,), (1,)), ((), ())),
        precision=lax.Precision.HIGHEST, preferred_element_type=F32,
    )


def attend_back_kernel(
    sc, qs_ref, kv0, kv1, kv2, kv3, bias_ref, w_ref, o_ref, lse_ref, n1_ref, cos_ref, sin_ref,
    dn_a, dn_b, dn_c, h_ref, r2_ref, gain_ref, dy_ref,
    dq_ref, d0, d1, d2, d3, dh_ref, gg_ref, pa0, pa1, pa2, pa3, datt_s, do_s, dl_s, dq_s,
):
    g = pl.program_id(0)
    kvs = (kv0, kv1, kv2, kv3)
    outs = (d0, d1, d2, d3)
    packs = (pa0, pa1, pa2, pa3)

    @pl.when(g == 0)
    def _():
        dn2 = dn_a[...].astype(F32) + dn_b[...].astype(F32) + dn_c[...].astype(F32)
        h = h_ref[...]
        r2 = r2_ref[...]
        weighted = dn2 * gain_ref[...]
        inner = jnp.sum(weighted * h, axis=0, keepdims=True)
        dh = dy_ref[...].astype(F32) + r2 * weighted - h * (r2 * r2 * r2 * inner / D)
        dh_ref[...] = dh
        datt_s[...] = dh.astype(BF)
        for b in range(ROWS):
            rows = slice(b * FB, (b + 1) * FB)
            gg_ref[b] = row_sums(dn2[rows] * h[rows] * r2)

    do_s[...] = tn(w_ref[0, :, SLOT_W:], datt_s[...]).astype(BF)
    for j in range(QPK):
        rows = slice(j * HD, (j + 1) * HD)
        dl_s[j : j + 1] = jnp.sum(
            do_s[rows].astype(F32) * o_ref[0, rows].astype(F32), axis=0, keepdims=True
        )

    def fold(k, fresh):
        keys = kvs[k][0, :HD]
        values = kvs[k][0, HD:]
        bias = bias_ref[k]
        dk = jnp.zeros((HD, CP), F32)
        dv = jnp.zeros((HD, CP), F32)
        for j in range(QPK):
            rows = slice(j * HD, (j + 1) * HD)
            s = tn(keys, qs_ref[0, rows]) + bias
            p = jnp.exp(s - lse_ref[0, j : j + 1])
            do_j = do_s[rows]
            dp = tn(values, do_j)
            ds = (p * (dp - dl_s[j : j + 1])).astype(BF)
            dv = dv + nt(do_j, p.astype(BF))
            dk = dk + nt(qs_ref[0, rows], ds)
            dq = nn(keys, ds)
            if fresh:
                dq_s[rows] = dq
            else:
                dq_s[rows] += dq
        outs[k][0, :HD] = dk.astype(outs[k].dtype)
        outs[k][0, HD:] = dv.astype(outs[k].dtype)

    fold(0, True)
    for k in range(1, ROWS):
        pl.when(sc[4 + k] != 0)(functools.partial(fold, k, False))

        @pl.when(sc[4 + k] == 0)
        def _(k=k):
            outs[k][...] = jnp.zeros(outs[k].shape, outs[k].dtype)

    cos_a = cos_ref[...]
    sin_a = sin_ref[...]
    for j in range(QPK):
        first, second = rope(
            dq_s[j * HD : j * HD + HALF] * HD**-0.5,
            dq_s[j * HD + HALF : (j + 1) * HD] * HD**-0.5,
            cos_a, -sin_a,
        )
        dq_ref[0, j * HD : j * HD + HALF] = first.astype(BF)
        dq_ref[0, j * HD + HALF : (j + 1) * HD] = second.astype(BF)

    for b in range(ROWS):
        rows = slice(b * FB, (b + 1) * FB)
        block = jnp.concatenate(
            [nt(dq_ref[0], n1_ref[rows]).astype(BF), nt(o_ref[0], datt_s[rows]).astype(BF)], axis=0
        )
        for k in range(ROWS):

            @pl.when(g == k)
            def _(k=k, block=block, b=b):
                packs[k][b, :AW] = block

        @pl.when(g == GROUPS - 1)
        def _(block=block, b=b):
            for k in range(ROWS):
                share = AW // ROWS
                for q in range(ROWS):

                    @pl.when((sc[0] ^ k) == q)
                    def _(k=k, q=q):
                        packs[k][b, AW:] = block[q * share : (q + 1) * share]


def final_kernel(
    sc, dq_ref, d0, d1, d2, w_ref, n1_ref, cos_ref, sin_ref, x_ref, r1_ref, gain_ref, dh_ref, gg_ref,
    h_ref, mlp_a, mlp_b, mlp_c,
    pb0, pb1, pb2, pb3, out0, out1, out2, out3, dn_s, dpg_s, dx_s, lo_s,
):
    g = pl.program_id(0)
    packs = (pb0, pb1, pb2, pb3)
    outs = (out0, out1, out2, out3)
    dkv = d0[0] + d1[0].astype(F32) + d2[0].astype(F32)
    first, second = rope(dkv[:HALF], dkv[HALF:HD], cos_ref[...], -sin_ref[...])
    dpg_s[:QW] = dq_ref[0]
    dpg_s[QW : QW + HALF] = first.astype(BF)
    dpg_s[QW + HALF : QW + HD] = second.astype(BF)
    dpg_s[QW + HD :] = dkv[HD:].astype(BF)
    part = nn(w_ref[0, :, :SLOT_W], dpg_s[...])

    @pl.when(g == 0)
    def _():
        dn_s[...] = part

    @pl.when(g != 0)
    def _():
        dn_s[...] += part

    for b in range(ROWS):
        block = nt(dpg_s[QW:], n1_ref[b * FB : (b + 1) * FB]).astype(BF)
        for k in range(ROWS):

            @pl.when(g == k)
            def _(k=k, block=block, b=b):
                packs[k][b, :KV] = block

        @pl.when(g == GROUPS - 1)
        def _(block=block, b=b):
            share = KV // ROWS
            for k in range(ROWS):
                for q in range(ROWS):

                    @pl.when((sc[0] ^ k) == q)
                    def _(k=k, q=q):
                        packs[k][b, KV : KV + share] = block[q * share : (q + 1) * share]

    @pl.when(g == GROUPS - 1)
    def _():
        dn1 = dn_s[...]
        x = x_ref[...].astype(F32)
        r1 = r1_ref[...]
        weighted = dn1 * gain_ref[...]
        inner = jnp.sum(weighted * x, axis=0, keepdims=True)
        dx = dh_ref[...] + r1 * weighted - x * (r1 * r1 * r1 * inner / D)
        dx_s[...] = dx.astype(BF)
        row = lax.broadcasted_iota(jnp.int32, (16, FB), 0)
        for b in range(ROWS):
            rows = slice(b * FB, (b + 1) * FB)
            sums = row_sums(dn1[rows] * x[rows] * r1)
            sums = jnp.where(row == 0, sums, jnp.where(row == 1, gg_ref[b], 0.0)).astype(BF)
            for k in range(ROWS):
                packs[k][b, KV + KV // ROWS :] = sums
        lo_s[...] = (
            h_ref[...] + mlp_a[...].astype(F32) + mlp_b[...].astype(F32) + mlp_c[...].astype(F32)
        ).astype(BF)
        for k in range(ROWS):
            outs[k][:FB] = lo_s[rows_at(sc[0] ^ k)]
            outs[k][FB:] = dx_s[rows_at(sc[0] ^ k)]


def mlp_kernel(count, halves, sc, *refs):
    if halves:
        w = refs[-1]
        part = refs[0].shape[0] // ROWS
        for h in range(2):
            shift = (FB - part) * (sc[3] if h == 0 else 1 - sc[3])
            for b in range(ROWS):
                w[pl.ds(pl.multiple_of(b * FB + shift, 16), part)] = refs[h][b * part : (b + 1) * part]
        wd = refs[2]
        refs = refs[3:-1]
    else:
        w, wd = refs[:2]
        refs = refs[2:]
    width = wd.shape[1]
    for i in range(count):
        n2 = refs[i]
        dy = refs[count + i]
        a_ref, dg_ref, du_ref, mlp_ref, dn_ref = refs[2 * count + 5 * i : 2 * count + 5 * i + 5]
        step = 128
        for f in range(0, width, step):
            cols = slice(f, f + step)
            gate = tn(w[:, f : f + step], n2[...])
            up = tn(w[:, width + f : width + f + step], n2[...])
            da = tn(wd[:, cols], dy[...])
            sigma = jax.nn.sigmoid(gate)
            silu = gate * sigma
            a_ref[cols] = (silu * up).astype(BF)
            dg_ref[cols] = (da * up * sigma * (1.0 + gate * (1.0 - sigma))).astype(BF)
            du_ref[cols] = (da * silu).astype(BF)
        dn_ref[...] = (nn(w[:, :width], dg_ref[...]) + nn(w[:, width : 2 * width], du_ref[...])).astype(BF)
        mlp_ref[...] = nn(wd[...], a_ref[...]).astype(BF)


def mlp_grad_kernel(*refs):
    n2s, dys, acts, gates, ups = (refs[ROWS * i : ROWS * (i + 1)] for i in range(5))
    out = refs[-1]
    width = acts[0].shape[0]
    step = 128
    for part, (left, right) in enumerate(((n2s, gates), (n2s, ups), (dys, acts))):
        for f in range(0, width, step):
            total = nt(left[0][...], right[0][f : f + step])
            for k in range(1, ROWS):
                total = total + nt(left[k][...], right[k][f : f + step])
            out[:, part * width + f : part * width + f + step] = total.astype(BF)


def grads_kernel(sc, g_ref, o0, o1, o2, o3, qkv_ref, out_ref, gains_ref, oa_s, ob_s):
    ix = sc[0]
    share_a = AW // ROWS
    share_b = KV // ROWS
    for k, odd in enumerate((o0, o1, o2, o3)):
        oa_s[pl.ds(pl.multiple_of((ix ^ k) * share_a, 8), share_a)] = odd[:share_a]
        ob_s[pl.ds(pl.multiple_of((ix ^ k) * share_b, 8), share_b)] = odd[share_a:]
    live = (ix == sc[2]).astype(F32)
    oa = oa_s[...] * live
    ob = ob_s[...] * live
    qkv_ref[...] = jnp.transpose(
        jnp.concatenate([g_ref[:QW], g_ref[AP : AP + KV], oa[:QW], ob], axis=0)
    )
    out_ref[...] = jnp.transpose(jnp.concatenate([g_ref[QW:AW], oa[QW:]], axis=0))
    gains_ref[...] = g_ref[AP + KV + share_b : AP + KV + share_b + 8]


def whole(*shape):
    return pl.BlockSpec(shape, lambda *_: (0,) * len(shape))


def per_group(*shape):
    return pl.BlockSpec((1,) + shape, lambda g, *_: (g,) + (0,) * len(shape))


def kv_blocks():
    def spec(k):
        return pl.BlockSpec((1, KV, CP), lambda g, *_: (jnp.where(g < ROWS, g ^ k, g), 0, 0))

    return [spec(k) for k in range(ROWS)]


def sds(shape, dtype):
    return jax.ShapeDtypeStruct(shape, dtype)


MICROSECONDS = {
    "split_tokens": 3, "split_grad": 3, "join": 2, "qkv": 7, "attend": 18, "mlp_near": 13, "mlp_far": 13,
    "mlp_grad": 18, "attend_back": 30, "final": 19, "merge": 2, "grads": 3,
}


def cost(name):
    return pl.CostEstimate(
        flops=MICROSECONDS[name] * 100 * 10**6, bytes_accessed=MICROSECONDS[name] * 3000 * 100, transcendentals=0
    )


def simple(kernel, name, outs, *operands, scalars=None, scratch=(), limit=VMEM_LIMIT):
    specs = [pl.BlockSpec(memory_space=pltpu.VMEM)] * len(operands)
    if scalars is not None:
        specs = [pl.BlockSpec(memory_space=pltpu.SMEM)] + specs
        operands = (scalars,) + operands
    return pl.pallas_call(
        kernel,
        in_specs=specs,
        out_specs=[pl.BlockSpec(memory_space=pltpu.VMEM)] * len(outs),
        out_shape=list(outs),
        scratch_shapes=list(scratch),
        compiler_params=pltpu.CompilerParams(vmem_limit_bytes=limit),
        cost_estimate=cost(name),
        name=name,
    )(*operands)


def grouped(kernel, name, in_specs, outs, out_specs, scratch, sc, *operands):
    return pl.pallas_call(
        kernel,
        grid_spec=pltpu.PrefetchScalarGridSpec(
            num_scalar_prefetch=1,
            grid=(GROUPS,),
            in_specs=in_specs,
            out_specs=out_specs,
            scratch_shapes=scratch,
        ),
        out_shape=outs,
        compiler_params=pltpu.CompilerParams(vmem_limit_bytes=VMEM_LIMIT),
        cost_estimate=cost(name),
        name=name,
    )(sc, *operands)


def swap(values, bit):
    return lax.ppermute(values, "gx", [(i, i ^ bit) for i in range(ROWS)])


def row_gather(own):
    far = swap(own, 2)
    mate = swap(own, 1)
    return own, mate, far, swap(far, 1)


def after(values, *first):
    return lax.optimization_barrier((values,) + first)[0]


def row_near(blocks):
    far = (blocks[2].astype(F32) + swap(blocks[3], 1).astype(F32)).astype(BF)
    return blocks[0], swap(blocks[1], 1), far


def row_terms(blocks, first=()):
    a, b, far = row_near(blocks)
    if first:
        far = after(far, *first)
    return a, b, swap(far, 2)


def row_scatter(blocks, first=()):
    a, b, c = row_terms(blocks, first)
    return (a.astype(F32) + b.astype(F32) + c.astype(F32)).astype(BF)


def ring(values):
    return lax.ppermute(values, "gy", [(i, (i + 1) % ROWS) for i in range(ROWS)])


def ring_scatter(blocks, iy):
    def take(at):
        return lax.dynamic_index_in_dim(blocks, at % ROWS, 0, keepdims=False)

    moving = take(iy + 3)
    for s in range(ROWS - 1):
        moving = (ring(moving).astype(F32) + take(iy + 2 - s).astype(F32)).astype(BF)
    return moving


def dp_sum(values):
    if lax.axis_size("dp") == 2:
        return values.astype(F32) + lax.ppermute(values, "dp", [(0, 1), (1, 0)]).astype(F32)
    return lax.psum(values, "dp").astype(F32)


def to_tokens(pieces):
    out = []
    for k in range(ROWS):
        pairs = [(a * ROWS + b, (b ^ k) * ROWS + SEQ_MAP[a]) for a in range(ROWS) for b in range(ROWS)]
        out.append(lax.ppermute(pieces[k], ("gx", "gy"), pairs))
    return out


def to_features(pieces):
    back = []
    for k in range(ROWS):
        pairs = [(a * ROWS + b, SEQ_BACK[b] * ROWS + (a ^ k)) for a in range(ROWS) for b in range(ROWS)]
        back.append(lax.ppermute(pieces[k], ("gx", "gy"), pairs))
    return back


def per_device(
    tokens, segment_ids, slot_table, w_qkv, w_out, w_gate_up, w_down, gain_attn, gain_mlp, cotangent
):
    ix = lax.axis_index("gx")
    iy = lax.axis_index("gy")
    ff = w_down.shape[1]
    odd_row = jnp.sum(jnp.where(slot_table % 2 == 1, slot_table // 2, 0))

    seg = lax.ppermute(segment_ids, "gy", [(i, SEQ_MAP[i]) for i in range(ROWS)]).reshape(ROWS, CH)
    seg_own = lax.dynamic_index_in_dim(seg, ix, 0, keepdims=False)
    starts = [jnp.sum(seg < s).astype(jnp.int32) for s in range(SEGS)]
    first = sum(jnp.where(seg_own == s, starts[s], 0) for s in range(SEGS))
    at_own = jnp.arange(CP, dtype=jnp.int32)
    position = (ix * CH + at_own - jnp.pad(first, (0, CP - CH))).astype(F32)
    frequency = THETA_BASE ** (-2.0 * jnp.arange(HALF, dtype=F32) / HD)
    angles = frequency[:, None] * position[None, :]
    cos_a = jnp.cos(angles)
    sin_a = jnp.sin(angles)
    query_docs = jnp.pad(seg_own, (0, CP - CH), constant_values=-1)
    biases = []
    flags = []
    for k in range(ROWS):
        seg_k = lax.dynamic_index_in_dim(seg, ix ^ k, 0, keepdims=False)
        key_docs = jnp.pad(seg_k, (0, CP - CH), constant_values=-2)
        allowed = (key_docs[:, None] == query_docs[None, :]) & (
            ((ix ^ k) * CH + at_own)[:, None] <= (ix * CH + at_own)[None, :]
        )
        biases.append(jnp.where(allowed, 0.0, NEGATIVE).astype(F32))
        flags.append(((ix ^ k) <= ix) & (seg_k[CH - 1] >= seg_own[0]))
    bias = jnp.stack(biases)
    idp = lax.axis_index("dp")
    at = jnp.stack([ix, iy, odd_row, idp]).astype(jnp.int32)
    sc = jnp.concatenate([at, jnp.stack(flags).astype(jnp.int32)])

    piece = sds((FB, CP), BF)
    pieces = simple(
        functools.partial(split_kernel, True), "split_tokens", [piece] * ROWS,
        tokens, gain_attn[:, None], gain_mlp[:, None], scalars=at,
    )
    toks = to_tokens(pieces)
    odd = jnp.concatenate([w_qkv[:, SLOT_W:], w_out[:, QW:]], axis=1)
    odd = jnp.where(ix == odd_row, odd, jnp.zeros_like(odd))
    quarter = row_scatter([lax.dynamic_slice(odd, (0, ODD * (ix ^ k)), (FB, ODD)) for k in range(ROWS)])
    w_all = lax.all_gather(
        jnp.concatenate([w_qkv[:, :SLOT_W], w_out[:, :QW], quarter], axis=1),
        ("gx", "gy"), axis=0, tiled=True,
    ).reshape(ROWS, D, PACK + ODD)
    dy_pieces = simple(
        functools.partial(split_kernel, False), "split_grad", [piece] * ROWS,
        after(cotangent, pieces[0]), scalars=at,
    )
    dy_pieces = to_tokens(dy_pieces)
    toks[0] = after(toks[0], *dy_pieces)
    x, n1, r1, gain_one, gain_two, w5, qs, kv = simple(
        qkv_kernel, "qkv",
        [
            sds((D, CP), BF), sds((D, CP), BF), sds((1, CP), F32), sds((D, 1), F32), sds((D, 1), F32),
            sds((GROUPS, D, PACK), BF), sds((GROUPS, QW, CP), BF), sds((GROUPS, KV, CP), BF),
        ],
        *toks, w_all, cos_a, sin_a,
        scalars=at,
    )

    dy = simple(join_kernel, "join", [sds((D, CP), BF)], *dy_pieces, scalars=at)[0]
    w_gu = jnp.concatenate([w_gate_up[:, 0], w_gate_up[:, 1]], axis=1)
    halves = lax.axis_size("dp") == 2
    if halves:
        w_gu = lax.dynamic_slice(w_gu, ((FB - 128) * idp, 0), (128, 2 * ff))
    w_gu = [lax.all_gather(w_gu, "gy", axis=0, tiled=True)]
    if halves:
        w_gu.append(lax.ppermute(w_gu[0], "dp", [(0, 1), (1, 0)]))
    w_d = lax.all_gather(w_down, "gy", axis=0, tiled=True)

    kvs = row_gather(kv)
    dys = row_gather(after(dy, kvs[2]))
    o, lse, h, n2, r2 = grouped(
        attend_kernel, "attend",
        [per_group(QW, CP)] + kv_blocks()
        + [whole(ROWS, CP, CP), per_group(D, PACK), whole(D, CP), whole(D, 1)],
        [
            sds((GROUPS, QW, CP), BF), sds((GROUPS, 8, CP), F32), sds((D, CP), F32), sds((D, CP), BF),
            sds((1, CP), F32),
        ],
        [per_group(QW, CP), per_group(8, CP), whole(D, CP), whole(D, CP), whole(1, CP)],
        [pltpu.VMEM((8, CP), F32), pltpu.VMEM((8, CP), F32), pltpu.VMEM((QW, CP), F32)],
        sc, after(qs, w_gu[0]), *kvs, bias, w5, x, gain_two,
    )

    n2s = row_gather(n2)
    per_block = [sds((ff, CP), BF)] * 3 + [sds((D, CP), BF)] * 2
    def feed_forward(name, some_n2, some_dy):
        return simple(
            functools.partial(mlp_kernel, 2, halves), name, per_block * 2, *w_gu, w_d, *some_n2, *some_dy,
            scalars=at, scratch=[pltpu.VMEM((D, 2 * ff), BF)] if halves else [],
        )

    near = feed_forward("mlp_near", n2s[:2], dys[:2])
    far = feed_forward("mlp_far", n2s[2:], dys[2:])
    blocks = [near[:5], near[5:], far[:5], far[5:]]
    dn2_terms = list(row_near([b[4] for b in blocks]))
    mlp_terms = list(row_near([b[3] for b in blocks]))

    def beside_dn2(far, *operands):
        return swap(far, 2), simple(
            mlp_grad_kernel, "mlp_grad", [sds((D, 3 * ff), BF)],
            *operands,
        )[0]

    dn2_terms[2], g_mlp = beside_dn2(
        dn2_terms[2], *n2s, *dys, *[b[0] for b in blocks], *[b[1] for b in blocks], *[b[2] for b in blocks]
    )

    pack_a = sds((ROWS, AP, FB), BF)

    def beside_back(far, *operands):
        return swap(far, 2), grouped(
        attend_back_kernel, "attend_back",
        [per_group(QW, CP)] + kv_blocks()
        + [whole(ROWS, CP, CP), per_group(D, PACK), per_group(QW, CP), per_group(8, CP), whole(D, CP),
           whole(HALF, CP), whole(HALF, CP)]
        + [whole(D, CP)] * 4 + [whole(1, CP), whole(D, 1), whole(D, CP)],
        [sds((GROUPS, QW, CP), BF), sds((GROUPS, KV, CP), F32)] + [sds((GROUPS, KV, CP), BF)] * 3
        + [sds((D, CP), F32), sds((ROWS, 16, FB), F32)] + [pack_a] * ROWS,
        [per_group(QW, CP)] + kv_blocks() + [whole(D, CP), whole(ROWS, 16, FB)]
        + [whole(ROWS, AP, FB)] * ROWS,
        [pltpu.VMEM((D, CP), BF), pltpu.VMEM((QW, CP), BF), pltpu.VMEM((8, CP), F32), pltpu.VMEM((QW, CP), F32)],
            *operands,
        )

    g_down = lax.psum_scatter(g_mlp[:, 2 * ff :], "gy", scatter_dimension=0, tiled=True)
    g_gate_up = lax.psum_scatter(g_mlp[:, : 2 * ff], "gy", scatter_dimension=0, tiled=True)
    mlp_terms[2] = after(mlp_terms[2], dn2_terms[2])
    dn2_terms[1] = after(dn2_terms[1], g_mlp, mlp_terms[2])
    mlp_terms[2], back = beside_back(
        mlp_terms[2],
        sc, qs, *kvs, bias, w5, o, lse, n1, cos_a, sin_a, *dn2_terms, h, r2, gain_two, dy,
    )
    dq, dkv, dh, gg, packs_a = back[0], list(back[1:5]), back[5], back[6], back[7:]
    dkv[2] = after(dkv[2], mlp_terms[2], g_down)
    dkv_terms = list(row_terms(dkv))
    a_terms = list(row_near(packs_a))
    a_terms[2] = after(a_terms[2], dkv_terms[2])
    dkv_terms[0] = after(dkv_terms[0], a_terms[2])
    a_terms[2] = swap(a_terms[2], 2)
    final = grouped(
        final_kernel, "final",
        [per_group(QW, CP)] + [per_group(KV, CP)] * 3
        + [per_group(D, PACK), whole(D, CP), whole(HALF, CP), whole(HALF, CP), whole(D, CP), whole(1, CP),
           whole(D, 1), whole(D, CP), whole(ROWS, 16, FB)] + [whole(D, CP)] * 4,
        [sds((ROWS, BP, FB), BF)] * ROWS + [sds((2 * FB, CP), BF)] * ROWS,
        [whole(ROWS, BP, FB)] * ROWS + [whole(2 * FB, CP)] * ROWS,
        [pltpu.VMEM((D, CP), F32), pltpu.VMEM((SLOT_W, CP), BF)] + [pltpu.VMEM((D, CP), BF)] * 2,
        sc, dq, *dkv_terms, w5, n1, cos_a, sin_a, x, r1, gain_one, dh, gg, h, *mlp_terms,
    )
    packs_b, out_pieces = final[:ROWS], final[ROWS:]
    back = to_features(out_pieces)
    layer_out, input_grad = simple(merge_kernel, "merge", [sds((FB, L), BF)] * 2, *back, scalars=at)

    grad_down = dp_sum(g_down)
    g_mlp = dp_sum(g_gate_up)
    g_a = sum(term.astype(F32) for term in a_terms).astype(BF)
    packs_b = list(packs_b)
    packs_b[2] = after(packs_b[2], a_terms[2])
    g_all = jnp.concatenate([g_a, row_scatter(packs_b)], axis=1)
    g_all = ring_scatter(after(g_all, *back[:2]), iy)
    g_all = dp_sum(after(g_all, *back[2:]))
    odds = jnp.concatenate([g_all[AW:AP], g_all[AP + KV : AP + KV + KV // ROWS]], axis=0)
    grad_qkv, grad_out, grad_gains = simple(
        grads_kernel, "grads",
        [sds((FB, 2 * SLOT_W), F32), sds((FB, 2 * QW), F32), sds((8, FB), F32)],
        g_all, *row_gather(odds), scalars=at,
        scratch=[pltpu.VMEM((AW, FB), F32), pltpu.VMEM((KV, FB), F32)],
    )
    grad_gate_up = jnp.stack([g_mlp[:, :ff], g_mlp[:, ff : 2 * ff]], axis=1)
    return (
        layer_out,
        input_grad,
        grad_qkv,
        grad_out,
        grad_gate_up,
        grad_down,
        grad_gains[0],
        grad_gains[1],
    )


def solution(mesh):
    placed = (
        P("gy", ("dp", "gx")),
        P(("dp", "gy"), None),
        P(),
        P("gy", "gx"),
        P("gy", "gx"),
        P("gy", None, "gx"),
        P("gy", "gx"),
        P("gy"),
        P("gy"),
        P("gy", ("dp", "gx")),
    )
    return jax.shard_map(
        per_device,
        mesh=mesh,
        in_specs=placed,
        out_specs=(
            P("gy", ("dp", "gx")),
            P("gy", ("dp", "gx")),
            P("gy", "gx"),
            P("gy", "gx"),
            P("gy", None, "gx"),
            P("gy", "gx"),
            P("gy"),
            P("gy"),
        ),
        check_vma=False,
    )
```

```python
import functools

import jax
import jax.numpy as jnp
from jax import lax
from jax.experimental import pallas as pl
from jax.experimental.pallas import tpu as pltpu
from jax.sharding import PartitionSpec as P

D = 960
HD = 64
QPK = 3
L = 1408
SEGS = 4
QW = QPK * HD
SLOT_W = QW + 2 * HD
PACK = SLOT_W + QW
GROUPS = 5
ROWS = 4
CH = L // ROWS
CP = 384
FB = D // ROWS
ODD = PACK // ROWS

EPSILON = 1e-05
THETA_BASE = 100000.0
NEGATIVE = -1e30
SEQ_MAP = (0, 2, 1, 3)
SEQ_BACK = (0, 2, 1, 3)
BF = jnp.bfloat16
F32 = jnp.float32
VMEM_LIMIT = 58 * 1024 * 1024
HALF = HD // 2
AW = 2 * QW
AP = AW + AW // ROWS
KV = 2 * HD
BP = KV + KV // ROWS + 16


def tn(a, b):
    return lax.dot_general(a, b, (((0,), (0,)), ((), ())), preferred_element_type=F32)


def nn(a, b):
    return lax.dot_general(a, b, (((1,), (0,)), ((), ())), preferred_element_type=F32)


def nt(a, b):
    return lax.dot_general(a, b, (((1,), (1,)), ((), ())), preferred_element_type=F32)


def rows_at(block, size=FB):
    return pl.ds(pl.multiple_of(block * FB, 16), size)


def rope(a, b, cos_a, sin_a):
    return a * cos_a - b * sin_a, b * cos_a + a * sin_a


def split_kernel(with_tail, sc, *refs):
    t_ref = refs[0]
    outs = refs[-ROWS:]
    iy = sc[1]
    if with_tail:
        lane = lax.broadcasted_iota(jnp.int32, (FB, CP - CH), 1)
        tail = jnp.zeros((FB, CP - CH), F32)
        for i in range(2):
            rest = refs[1 + i][...]
            for part in range(3):
                piece = rest.astype(BF).astype(F32)
                rest = rest - piece
                tail = jnp.where(lane == 3 * i + part, piece, tail)
        tail = tail.astype(BF)
    else:
        tail = jnp.zeros((FB, CP - CH), BF)
    for q in range(ROWS):
        block = jnp.concatenate([t_ref[:, q * CH : (q + 1) * CH], tail], axis=1)
        for k in range(ROWS):

            @pl.when((iy ^ k) == q)
            def _(k=k, block=block):
                outs[k][...] = block


def join_kernel(sc, *refs):
    for k in range(ROWS):
        refs[ROWS][rows_at(sc[0] ^ k)] = refs[k][...]


def merge_kernel(sc, *refs):
    iy = sc[1]
    for i in range(2):
        rows = slice(i * FB, (i + 1) * FB)
        parts = []
        for q in range(ROWS):
            value = refs[0][rows, :CH]
            for k in range(1, ROWS):
                value = jnp.where((iy ^ k) == q, refs[k][rows, :CH], value)
            parts.append(value)
        refs[ROWS + i][...] = jnp.concatenate(parts, axis=1)


def qkv_kernel(sc, *refs):
    toks = refs[:4]
    w_rows = refs[4:8]
    cos_ref, sin_ref = refs[8:10]
    x_ref, n1_ref, r1_ref, g1_ref, g2_ref, w5_ref, qs_ref, kv_ref = refs[10:]
    ix = sc[0]
    lane = lax.broadcasted_iota(jnp.int32, (FB, CP), 1)
    for k in range(ROWS):
        rows = rows_at(ix ^ k)
        piece = toks[k][...].astype(F32)
        x_ref[rows] = jnp.where(lane < CH, piece, 0.0).astype(BF)
        for i, out in enumerate((g1_ref, g2_ref)):
            here = (lane >= CH + 3 * i) & (lane < CH + 3 * i + 3)
            out[rows] = jnp.sum(jnp.where(here, piece, 0.0), axis=1, keepdims=True)
    x = x_ref[...].astype(F32)
    r1 = lax.rsqrt(jnp.sum(x * x, axis=0, keepdims=True) / D + EPSILON)
    r1_ref[...] = r1
    n1_ref[...] = (x * r1 * g1_ref[...]).astype(BF)
    for k in range(ROWS):
        w5_ref[k] = w_rows[k][:, :PACK]
        lanes = pl.ds(pl.multiple_of((ix ^ k) * ODD, ODD), ODD)
        w5_ref[GROUPS - 1, :, lanes] = w_rows[k][:, PACK:]
    cos_a = cos_ref[...]
    sin_a = sin_ref[...]
    for g in range(GROUPS):
        p = tn(w5_ref[g, :, :SLOT_W], n1_ref[...])
        for j in range(QPK + 1):
            first, second = rope(
                p[j * HD : j * HD + HALF], p[j * HD + HALF : (j + 1) * HD], cos_a, sin_a
            )
            first = first.astype(BF)
            second = second.astype(BF)
            if j < QPK:
                qs_ref[g, j * HD : j * HD + HALF] = (first.astype(F32) * HD**-0.5).astype(BF)
                qs_ref[g, j * HD + HALF : (j + 1) * HD] = (second.astype(F32) * HD**-0.5).astype(BF)
            else:
                kv_ref[g, :HALF] = first
                kv_ref[g, HALF:HD] = second
        kv_ref[g, HD:] = p[(QPK + 1) * HD :].astype(BF)


def attend_kernel(
    sc, qs_ref, kv0, kv1, kv2, kv3, bias_ref, w_ref, x_ref, gain_ref,
    o_ref, lse_ref, h_ref, n2_ref, r2_ref, m_s, l_s, acc_s,
):
    g = pl.program_id(0)
    kvs = (kv0, kv1, kv2, kv3)

    def fold(k, fresh):
        keys = kvs[k][0, :HD]
        values = kvs[k][0, HD:]
        bias = bias_ref[k]
        for j in range(QPK):
            s = tn(keys, qs_ref[0, j * HD : (j + 1) * HD]) + bias
            top = jnp.max(s, axis=0, keepdims=True)
            if fresh:
                m = top
                e = jnp.exp(s - m)
                l_s[j : j + 1] = jnp.sum(e, axis=0, keepdims=True)
                acc_s[j * HD : (j + 1) * HD] = nn(values, e.astype(BF))
            else:
                old = m_s[j : j + 1]
                m = jnp.maximum(old, top)
                fade = jnp.exp(old - m)
                e = jnp.exp(s - m)
                l_s[j : j + 1] = l_s[j : j + 1] * fade + jnp.sum(e, axis=0, keepdims=True)
                acc_s[j * HD : (j + 1) * HD] = acc_s[j * HD : (j + 1) * HD] * fade + nn(
                    values, e.astype(BF)
                )
            m_s[j : j + 1] = m

    fold(0, True)
    for k in range(1, ROWS):
        pl.when(sc[4 + k] != 0)(functools.partial(fold, k, False))
    for j in range(QPK):
        total = l_s[j : j + 1]
        o_ref[0, j * HD : (j + 1) * HD] = (acc_s[j * HD : (j + 1) * HD] / total).astype(BF)
        lse_ref[0, j : j + 1] = m_s[j : j + 1] + jnp.log(total)
    part = nn(w_ref[0, :, SLOT_W:], o_ref[0])

    @pl.when(g == 0)
    def _():
        h_ref[...] = x_ref[...].astype(F32) + part

    @pl.when(g != 0)
    def _():
        h_ref[...] += part

    @pl.when(g == GROUPS - 1)
    def _():
        h = h_ref[...]
        r2 = lax.rsqrt(jnp.sum(h * h, axis=0, keepdims=True) / D + EPSILON)
        r2_ref[...] = r2
        n2_ref[...] = (h * r2 * gain_ref[...]).astype(BF)


def row_sums(values):
    return lax.dot_general(
        jnp.ones((16, CP), F32), values, (((1,), (1,)), ((), ())),
        precision=lax.Precision.HIGHEST, preferred_element_type=F32,
    )


def attend_back_kernel(
    sc, qs_ref, kv0, kv1, kv2, kv3, bias_ref, w_ref, o_ref, lse_ref, n1_ref, cos_ref, sin_ref,
    dn_a, dn_b, dn_c, h_ref, r2_ref, gain_ref, dy_ref,
    dq_ref, d0, d1, d2, d3, dh_ref, gg_ref, pa0, pa1, pa2, pa3, datt_s, do_s, dl_s, dq_s,
):
    g = pl.program_id(0)
    kvs = (kv0, kv1, kv2, kv3)
    outs = (d0, d1, d2, d3)
    packs = (pa0, pa1, pa2, pa3)

    @pl.when(g == 0)
    def _():
        dn2 = dn_a[...].astype(F32) + dn_b[...].astype(F32) + dn_c[...].astype(F32)
        h = h_ref[...]
        r2 = r2_ref[...]
        weighted = dn2 * gain_ref[...]
        inner = jnp.sum(weighted * h, axis=0, keepdims=True)
        dh = dy_ref[...].astype(F32) + r2 * weighted - h * (r2 * r2 * r2 * inner / D)
        dh_ref[...] = dh
        datt_s[...] = dh.astype(BF)
        for b in range(ROWS):
            rows = slice(b * FB, (b + 1) * FB)
            gg_ref[b] = row_sums(dn2[rows] * h[rows] * r2)

    do_s[...] = tn(w_ref[0, :, SLOT_W:], datt_s[...]).astype(BF)
    for j in range(QPK):
        rows = slice(j * HD, (j + 1) * HD)
        dl_s[j : j + 1] = jnp.sum(
            do_s[rows].astype(F32) * o_ref[0, rows].astype(F32), axis=0, keepdims=True
        )

    def fold(k, fresh):
        keys = kvs[k][0, :HD]
        values = kvs[k][0, HD:]
        bias = bias_ref[k]
        dk = jnp.zeros((HD, CP), F32)
        dv = jnp.zeros((HD, CP), F32)
        for j in range(QPK):
            rows = slice(j * HD, (j + 1) * HD)
            s = tn(keys, qs_ref[0, rows]) + bias
            p = jnp.exp(s - lse_ref[0, j : j + 1])
            do_j = do_s[rows]
            dp = tn(values, do_j)
            ds = (p * (dp - dl_s[j : j + 1])).astype(BF)
            dv = dv + nt(do_j, p.astype(BF))
            dk = dk + nt(qs_ref[0, rows], ds)
            dq = nn(keys, ds)
            if fresh:
                dq_s[rows] = dq
            else:
                dq_s[rows] += dq
        outs[k][0, :HD] = dk.astype(outs[k].dtype)
        outs[k][0, HD:] = dv.astype(outs[k].dtype)

    fold(0, True)
    for k in range(1, ROWS):
        pl.when(sc[4 + k] != 0)(functools.partial(fold, k, False))

        @pl.when(sc[4 + k] == 0)
        def _(k=k):
            outs[k][...] = jnp.zeros(outs[k].shape, outs[k].dtype)

    cos_a = cos_ref[...]
    sin_a = sin_ref[...]
    for j in range(QPK):
        first, second = rope(
            dq_s[j * HD : j * HD + HALF] * HD**-0.5,
            dq_s[j * HD + HALF : (j + 1) * HD] * HD**-0.5,
            cos_a, -sin_a,
        )
        dq_ref[0, j * HD : j * HD + HALF] = first.astype(BF)
        dq_ref[0, j * HD + HALF : (j + 1) * HD] = second.astype(BF)

    for b in range(ROWS):
        rows = slice(b * FB, (b + 1) * FB)
        block = jnp.concatenate(
            [nt(dq_ref[0], n1_ref[rows]).astype(BF), nt(o_ref[0], datt_s[rows]).astype(BF)], axis=0
        )
        for k in range(ROWS):

            @pl.when(g == k)
            def _(k=k, block=block, b=b):
                packs[k][b, :AW] = block

        @pl.when(g == GROUPS - 1)
        def _(block=block, b=b):
            for k in range(ROWS):
                share = AW // ROWS
                for q in range(ROWS):

                    @pl.when((sc[0] ^ k) == q)
                    def _(k=k, q=q):
                        packs[k][b, AW:] = block[q * share : (q + 1) * share]


def final_kernel(
    sc, dq_ref, d0, d1, d2, w_ref, n1_ref, cos_ref, sin_ref, x_ref, r1_ref, gain_ref, dh_ref, gg_ref,
    h_ref, mlp_a, mlp_b, mlp_c,
    pb0, pb1, pb2, pb3, out0, out1, out2, out3, dn_s, dpg_s, dx_s, lo_s,
):
    g = pl.program_id(0)
    packs = (pb0, pb1, pb2, pb3)
    outs = (out0, out1, out2, out3)
    dkv = d0[0] + d1[0].astype(F32) + d2[0].astype(F32)
    first, second = rope(dkv[:HALF], dkv[HALF:HD], cos_ref[...], -sin_ref[...])
    dpg_s[:QW] = dq_ref[0]
    dpg_s[QW : QW + HALF] = first.astype(BF)
    dpg_s[QW + HALF : QW + HD] = second.astype(BF)
    dpg_s[QW + HD :] = dkv[HD:].astype(BF)
    part = nn(w_ref[0, :, :SLOT_W], dpg_s[...])

    @pl.when(g == 0)
    def _():
        dn_s[...] = part

    @pl.when(g != 0)
    def _():
        dn_s[...] += part

    for b in range(ROWS):
        block = nt(dpg_s[QW:], n1_ref[b * FB : (b + 1) * FB]).astype(BF)
        for k in range(ROWS):

            @pl.when(g == k)
            def _(k=k, block=block, b=b):
                packs[k][b, :KV] = block

        @pl.when(g == GROUPS - 1)
        def _(block=block, b=b):
            share = KV // ROWS
            for k in range(ROWS):
                for q in range(ROWS):

                    @pl.when((sc[0] ^ k) == q)
                    def _(k=k, q=q):
                        packs[k][b, KV : KV + share] = block[q * share : (q + 1) * share]

    @pl.when(g == GROUPS - 1)
    def _():
        dn1 = dn_s[...]
        x = x_ref[...].astype(F32)
        r1 = r1_ref[...]
        weighted = dn1 * gain_ref[...]
        inner = jnp.sum(weighted * x, axis=0, keepdims=True)
        dx = dh_ref[...] + r1 * weighted - x * (r1 * r1 * r1 * inner / D)
        dx_s[...] = dx.astype(BF)
        row = lax.broadcasted_iota(jnp.int32, (16, FB), 0)
        for b in range(ROWS):
            rows = slice(b * FB, (b + 1) * FB)
            sums = row_sums(dn1[rows] * x[rows] * r1)
            sums = jnp.where(row == 0, sums, jnp.where(row == 1, gg_ref[b], 0.0)).astype(BF)
            for k in range(ROWS):
                packs[k][b, KV + KV // ROWS :] = sums
        lo_s[...] = (
            h_ref[...] + mlp_a[...].astype(F32) + mlp_b[...].astype(F32) + mlp_c[...].astype(F32)
        ).astype(BF)
        for k in range(ROWS):
            outs[k][:FB] = lo_s[rows_at(sc[0] ^ k)]
            outs[k][FB:] = dx_s[rows_at(sc[0] ^ k)]


def mlp_kernel(count, halves, sc, *refs):
    if halves:
        w = refs[-1]
        part = refs[0].shape[0] // ROWS
        for h in range(2):
            shift = (FB - part) * (sc[3] if h == 0 else 1 - sc[3])
            for b in range(ROWS):
                w[pl.ds(pl.multiple_of(b * FB + shift, 16), part)] = refs[h][b * part : (b + 1) * part]
        wd = refs[2]
        refs = refs[3:-1]
    else:
        w, wd = refs[:2]
        refs = refs[2:]
    width = wd.shape[1]
    for i in range(count):
        n2 = refs[i]
        dy = refs[count + i]
        a_ref, dg_ref, du_ref, mlp_ref, dn_ref = refs[2 * count + 5 * i : 2 * count + 5 * i + 5]
        step = 128
        for f in range(0, width, step):
            cols = slice(f, f + step)
            gate = tn(w[:, f : f + step], n2[...])
            up = tn(w[:, width + f : width + f + step], n2[...])
            da = tn(wd[:, cols], dy[...])
            sigma = jax.nn.sigmoid(gate)
            silu = gate * sigma
            a_ref[cols] = (silu * up).astype(BF)
            dg_ref[cols] = (da * up * sigma * (1.0 + gate * (1.0 - sigma))).astype(BF)
            du_ref[cols] = (da * silu).astype(BF)
        dn_ref[...] = (nn(w[:, :width], dg_ref[...]) + nn(w[:, width : 2 * width], du_ref[...])).astype(BF)
        mlp_ref[...] = nn(wd[...], a_ref[...]).astype(BF)


def mlp_grad_kernel(*refs):
    n2s, dys, acts, gates, ups = (refs[ROWS * i : ROWS * (i + 1)] for i in range(5))
    outs = refs[-2:]
    width = acts[0].shape[0]
    edge = outs[0].shape[1]
    step = 128
    for part, (left, right) in enumerate(((n2s, gates), (n2s, ups), (dys, acts))):
        for f in range(0, width, step):
            total = nt(left[0][...], right[0][f : f + step])
            for k in range(1, ROWS):
                total = total + nt(left[k][...], right[k][f : f + step])
            col = part * width + f
            out = outs[col // edge]
            out[:, col % edge : col % edge + step] = total.astype(BF)


def grads_kernel(sc, g_ref, o0, o1, o2, o3, qkv_ref, out_ref, gains_ref, oa_s, ob_s):
    ix = sc[0]
    share_a = AW // ROWS
    share_b = KV // ROWS
    for k, odd in enumerate((o0, o1, o2, o3)):
        oa_s[pl.ds(pl.multiple_of((ix ^ k) * share_a, 8), share_a)] = odd[:share_a]
        ob_s[pl.ds(pl.multiple_of((ix ^ k) * share_b, 8), share_b)] = odd[share_a:]
    live = (ix == sc[2]).astype(F32)
    oa = oa_s[...] * live
    ob = ob_s[...] * live
    qkv_ref[...] = jnp.transpose(
        jnp.concatenate([g_ref[:QW], g_ref[AP : AP + KV], oa[:QW], ob], axis=0)
    )
    out_ref[...] = jnp.transpose(jnp.concatenate([g_ref[QW:AW], oa[QW:]], axis=0))
    gains_ref[...] = g_ref[AP + KV + share_b : AP + KV + share_b + 8]


def whole(*shape):
    return pl.BlockSpec(shape, lambda *_: (0,) * len(shape))


def per_group(*shape):
    return pl.BlockSpec((1,) + shape, lambda g, *_: (g,) + (0,) * len(shape))


def kv_blocks():
    def spec(k):
        return pl.BlockSpec((1, KV, CP), lambda g, *_: (jnp.where(g < ROWS, g ^ k, g), 0, 0))

    return [spec(k) for k in range(ROWS)]


def sds(shape, dtype):
    return jax.ShapeDtypeStruct(shape, dtype)


MICROSECONDS = {
    "split_tokens": 3, "split_grad": 3, "join": 2, "qkv": 7, "attend": 18, "mlp_near": 13, "mlp_far": 13,
    "mlp_grad": 18, "attend_back": 30, "final": 19, "merge": 2, "grads": 3,
}


def cost(name):
    return pl.CostEstimate(
        flops=MICROSECONDS[name] * 100 * 10**6, bytes_accessed=MICROSECONDS[name] * 3000 * 100, transcendentals=0
    )


def simple(kernel, name, outs, *operands, scalars=None, scratch=(), limit=VMEM_LIMIT):
    specs = [pl.BlockSpec(memory_space=pltpu.VMEM)] * len(operands)
    if scalars is not None:
        specs = [pl.BlockSpec(memory_space=pltpu.SMEM)] + specs
        operands = (scalars,) + operands
    return pl.pallas_call(
        kernel,
        in_specs=specs,
        out_specs=[pl.BlockSpec(memory_space=pltpu.VMEM)] * len(outs),
        out_shape=list(outs),
        scratch_shapes=list(scratch),
        compiler_params=pltpu.CompilerParams(vmem_limit_bytes=limit),
        cost_estimate=cost(name),
        name=name,
    )(*operands)


def grouped(kernel, name, in_specs, outs, out_specs, scratch, sc, *operands):
    return pl.pallas_call(
        kernel,
        grid_spec=pltpu.PrefetchScalarGridSpec(
            num_scalar_prefetch=1,
            grid=(GROUPS,),
            in_specs=in_specs,
            out_specs=out_specs,
            scratch_shapes=scratch,
        ),
        out_shape=outs,
        compiler_params=pltpu.CompilerParams(vmem_limit_bytes=VMEM_LIMIT),
        cost_estimate=cost(name),
        name=name,
    )(sc, *operands)


def swap(values, bit):
    return lax.ppermute(values, "gx", [(i, i ^ bit) for i in range(ROWS)])


def row_gather(own):
    far = swap(own, 2)
    mate = swap(own, 1)
    return own, mate, far, swap(far, 1)


def after(values, *first):
    return lax.optimization_barrier((values,) + first)[0]


def row_near(blocks):
    far = (blocks[2].astype(F32) + swap(blocks[3], 1).astype(F32)).astype(BF)
    return blocks[0], swap(blocks[1], 1), far


def row_terms(blocks, first=()):
    a, b, far = row_near(blocks)
    if first:
        far = after(far, *first)
    return a, b, swap(far, 2)


def row_scatter(blocks, first=()):
    a, b, c = row_terms(blocks, first)
    return (a.astype(F32) + b.astype(F32) + c.astype(F32)).astype(BF)


def ring(values):
    return lax.ppermute(values, "gy", [(i, (i + 1) % ROWS) for i in range(ROWS)])


def ring_scatter(blocks, iy):
    def take(at):
        return lax.dynamic_index_in_dim(blocks, at % ROWS, 0, keepdims=False)

    moving = take(iy + 3)
    for s in range(ROWS - 1):
        moving = (ring(moving).astype(F32) + take(iy + 2 - s).astype(F32)).astype(BF)
    return moving


def dp_sum(values):
    if lax.axis_size("dp") == 2:
        return values.astype(F32) + lax.ppermute(values, "dp", [(0, 1), (1, 0)]).astype(F32)
    return lax.psum(values, "dp").astype(F32)


def to_tokens(pieces):
    out = []
    for k in range(ROWS):
        pairs = [(a * ROWS + b, (b ^ k) * ROWS + SEQ_MAP[a]) for a in range(ROWS) for b in range(ROWS)]
        out.append(lax.ppermute(pieces[k], ("gx", "gy"), pairs))
    return out


def to_features(pieces):
    back = []
    for k in range(ROWS):
        pairs = [(a * ROWS + b, SEQ_BACK[b] * ROWS + (a ^ k)) for a in range(ROWS) for b in range(ROWS)]
        back.append(lax.ppermute(pieces[k], ("gx", "gy"), pairs))
    return back


def per_device(
    tokens, segment_ids, slot_table, w_qkv, w_out, w_gate_up, w_down, gain_attn, gain_mlp, cotangent
):
    ix = lax.axis_index("gx")
    iy = lax.axis_index("gy")
    ff = w_down.shape[1]
    odd_row = jnp.sum(jnp.where(slot_table % 2 == 1, slot_table // 2, 0))

    seg = lax.ppermute(segment_ids, "gy", [(i, SEQ_MAP[i]) for i in range(ROWS)]).reshape(ROWS, CH)
    seg_own = lax.dynamic_index_in_dim(seg, ix, 0, keepdims=False)
    starts = [jnp.sum(seg < s).astype(jnp.int32) for s in range(SEGS)]
    first = sum(jnp.where(seg_own == s, starts[s], 0) for s in range(SEGS))
    at_own = jnp.arange(CP, dtype=jnp.int32)
    position = (ix * CH + at_own - jnp.pad(first, (0, CP - CH))).astype(F32)
    frequency = THETA_BASE ** (-2.0 * jnp.arange(HALF, dtype=F32) / HD)
    angles = frequency[:, None] * position[None, :]
    cos_a = jnp.cos(angles)
    sin_a = jnp.sin(angles)
    query_docs = jnp.pad(seg_own, (0, CP - CH), constant_values=-1)
    biases = []
    flags = []
    for k in range(ROWS):
        seg_k = lax.dynamic_index_in_dim(seg, ix ^ k, 0, keepdims=False)
        key_docs = jnp.pad(seg_k, (0, CP - CH), constant_values=-2)
        allowed = (key_docs[:, None] == query_docs[None, :]) & (
            ((ix ^ k) * CH + at_own)[:, None] <= (ix * CH + at_own)[None, :]
        )
        biases.append(jnp.where(allowed, 0.0, NEGATIVE).astype(F32))
        flags.append(((ix ^ k) <= ix) & (seg_k[CH - 1] >= seg_own[0]))
    bias = jnp.stack(biases)
    idp = lax.axis_index("dp")
    at = jnp.stack([ix, iy, odd_row, idp]).astype(jnp.int32)
    sc = jnp.concatenate([at, jnp.stack(flags).astype(jnp.int32)])

    piece = sds((FB, CP), BF)
    pieces = simple(
        functools.partial(split_kernel, True), "split_tokens", [piece] * ROWS,
        tokens, gain_attn[:, None], gain_mlp[:, None], scalars=at,
    )
    toks = to_tokens(pieces)
    odd = jnp.concatenate([w_qkv[:, SLOT_W:], w_out[:, QW:]], axis=1)
    odd = jnp.where(ix == odd_row, odd, jnp.zeros_like(odd))
    quarter = row_scatter([lax.dynamic_slice(odd, (0, ODD * (ix ^ k)), (FB, ODD)) for k in range(ROWS)])
    w_own = lax.all_gather(
        jnp.concatenate([w_qkv[:, :SLOT_W], w_out[:, :QW], quarter], axis=1), "gy", axis=0, tiled=True
    )
    dy_pieces = simple(
        functools.partial(split_kernel, False), "split_grad", [piece] * ROWS,
        after(cotangent, pieces[0]), scalars=at,
    )
    dy_pieces = to_tokens(dy_pieces)
    w_own = after(w_own, *toks)
    w_far = after(swap(w_own, 2), *dy_pieces)
    w_rows = [w_own, swap(w_own, 1), w_far, swap(w_far, 1)]
    w_gu = jnp.concatenate([w_gate_up[:, 0], w_gate_up[:, 1]], axis=1)
    halves = lax.axis_size("dp") == 2
    if halves:
        w_gu = lax.dynamic_slice(w_gu, ((FB - 128) * idp, 0), (128, 2 * ff))
    w_gu = [lax.all_gather(w_gu, "gy", axis=0, tiled=True)]
    if halves:
        w_gu.append(lax.ppermute(w_gu[0], "dp", [(0, 1), (1, 0)]))
    x, n1, r1, gain_one, gain_two, w5, qs, kv = simple(
        qkv_kernel, "qkv",
        [
            sds((D, CP), BF), sds((D, CP), BF), sds((1, CP), F32), sds((D, 1), F32), sds((D, 1), F32),
            sds((GROUPS, D, PACK), BF), sds((GROUPS, QW, CP), BF), sds((GROUPS, KV, CP), BF),
        ],
        *toks, *w_rows, cos_a, sin_a,
        scalars=at,
    )

    dy = simple(join_kernel, "join", [sds((D, CP), BF)], *dy_pieces, scalars=at)[0]
    w_d = lax.all_gather(w_down, "gy", axis=0, tiled=True)

    kvs = row_gather(kv)
    dys = row_gather(after(dy, kvs[2]))
    o, lse, h, n2, r2 = grouped(
        attend_kernel, "attend",
        [per_group(QW, CP)] + kv_blocks()
        + [whole(ROWS, CP, CP), per_group(D, PACK), whole(D, CP), whole(D, 1)],
        [
            sds((GROUPS, QW, CP), BF), sds((GROUPS, 8, CP), F32), sds((D, CP), F32), sds((D, CP), BF),
            sds((1, CP), F32),
        ],
        [per_group(QW, CP), per_group(8, CP), whole(D, CP), whole(D, CP), whole(1, CP)],
        [pltpu.VMEM((8, CP), F32), pltpu.VMEM((8, CP), F32), pltpu.VMEM((QW, CP), F32)],
        sc, qs, *kvs, bias, w5, x, gain_two,
    )

    n2s = row_gather(n2)
    per_block = [sds((ff, CP), BF)] * 3 + [sds((D, CP), BF)] * 2
    def feed_forward(name, some_n2, some_dy):
        return simple(
            functools.partial(mlp_kernel, 2, halves), name, per_block * 2, *w_gu, w_d, *some_n2, *some_dy,
            scalars=at, scratch=[pltpu.VMEM((D, 2 * ff), BF)] if halves else [],
        )

    far = feed_forward("mlp_far", n2s[2:], dys[2:])
    near = feed_forward("mlp_near", [after(n2s[0], far[9]), n2s[1]], dys[:2])
    blocks = [near[:5], near[5:], far[:5], far[5:]]
    dn2_terms = list(row_near([b[4] for b in blocks]))
    mlp_terms = list(row_near([b[3] for b in blocks]))

    dn2_terms[2] = swap(dn2_terms[2], 2)
    wide = (3 * ff // 2 + 127) // 128 * 128
    g_mlp = simple(
        mlp_grad_kernel, "mlp_grad", [sds((D, wide), BF), sds((D, 3 * ff - wide), BF)],
        after(n2s[0], dn2_terms[2]), *n2s[1:], *dys,
        *[b[0] for b in blocks], *[b[1] for b in blocks], *[b[2] for b in blocks],
    )

    pack_a = sds((ROWS, AP, FB), BF)

    def beside_back(far, *operands):
        return swap(far, 2), grouped(
        attend_back_kernel, "attend_back",
        [per_group(QW, CP)] + kv_blocks()
        + [whole(ROWS, CP, CP), per_group(D, PACK), per_group(QW, CP), per_group(8, CP), whole(D, CP),
           whole(HALF, CP), whole(HALF, CP)]
        + [whole(D, CP)] * 4 + [whole(1, CP), whole(D, 1), whole(D, CP)],
        [sds((GROUPS, QW, CP), BF), sds((GROUPS, KV, CP), F32)] + [sds((GROUPS, KV, CP), BF)] * 3
        + [sds((D, CP), F32), sds((ROWS, 16, FB), F32)] + [pack_a] * ROWS,
        [per_group(QW, CP)] + kv_blocks() + [whole(D, CP), whole(ROWS, 16, FB)]
        + [whole(ROWS, AP, FB)] * ROWS,
        [pltpu.VMEM((D, CP), BF), pltpu.VMEM((QW, CP), BF), pltpu.VMEM((8, CP), F32), pltpu.VMEM((QW, CP), F32)],
            *operands,
        )

    mlp_terms[2] = after(mlp_terms[2], dn2_terms[2])
    dn2_terms[1] = after(dn2_terms[1], g_mlp[0], mlp_terms[2])
    mlp_terms[2], back = beside_back(
        mlp_terms[2],
        sc, qs, *kvs, bias, w5, o, lse, n1, cos_a, sin_a, *dn2_terms, h, r2, gain_two, dy,
    )
    dq, dkv, dh, gg, packs_a = back[0], list(back[1:5]), back[5], back[6], back[7:]
    g_mlp = [lax.psum_scatter(g, "gy", scatter_dimension=0, tiled=True) for g in g_mlp]
    dkv[2] = after(dkv[2], mlp_terms[2], g_mlp[0])
    dkv_terms = list(row_terms(dkv))
    a_terms = list(row_near(packs_a))
    a_terms[2] = after(a_terms[2], dkv_terms[2])
    dkv_terms[0] = after(dkv_terms[0], a_terms[2])
    a_terms[2] = swap(a_terms[2], 2)
    final = grouped(
        final_kernel, "final",
        [per_group(QW, CP)] + [per_group(KV, CP)] * 3
        + [per_group(D, PACK), whole(D, CP), whole(HALF, CP), whole(HALF, CP), whole(D, CP), whole(1, CP),
           whole(D, 1), whole(D, CP), whole(ROWS, 16, FB)] + [whole(D, CP)] * 4,
        [sds((ROWS, BP, FB), BF)] * ROWS + [sds((2 * FB, CP), BF)] * ROWS,
        [whole(ROWS, BP, FB)] * ROWS + [whole(2 * FB, CP)] * ROWS,
        [pltpu.VMEM((D, CP), F32), pltpu.VMEM((SLOT_W, CP), BF)] + [pltpu.VMEM((D, CP), BF)] * 2,
        sc, dq, *dkv_terms, w5, n1, cos_a, sin_a, x, r1, gain_one, dh, gg, h, *mlp_terms,
    )
    packs_b, out_pieces = final[:ROWS], final[ROWS:]
    back = to_features(out_pieces)
    layer_out, input_grad = simple(merge_kernel, "merge", [sds((FB, L), BF)] * 2, *back, scalars=at)

    g_mlp = jnp.concatenate([dp_sum(g) for g in g_mlp], axis=1)
    grad_down = g_mlp[:, 2 * ff :]
    g_a = sum(term.astype(F32) for term in a_terms).astype(BF)
    packs_b = list(packs_b)
    packs_b[2] = after(packs_b[2], a_terms[2])
    g_all = jnp.concatenate([g_a, row_scatter(packs_b)], axis=1)
    g_all = ring_scatter(after(g_all, *back[:2]), iy)
    g_all = dp_sum(after(g_all, *back[2:]))
    odds = jnp.concatenate([g_all[AW:AP], g_all[AP + KV : AP + KV + KV // ROWS]], axis=0)
    grad_qkv, grad_out, grad_gains = simple(
        grads_kernel, "grads",
        [sds((FB, 2 * SLOT_W), F32), sds((FB, 2 * QW), F32), sds((8, FB), F32)],
        g_all, *row_gather(odds), scalars=at,
        scratch=[pltpu.VMEM((AW, FB), F32), pltpu.VMEM((KV, FB), F32)],
    )
    grad_gate_up = jnp.stack([g_mlp[:, :ff], g_mlp[:, ff : 2 * ff]], axis=1)
    return (
        layer_out,
        input_grad,
        grad_qkv,
        grad_out,
        grad_gate_up,
        grad_down,
        grad_gains[0],
        grad_gains[1],
    )


def solution(mesh):
    placed = (
        P("gy", ("dp", "gx")),
        P(("dp", "gy"), None),
        P(),
        P("gy", "gx"),
        P("gy", "gx"),
        P("gy", None, "gx"),
        P("gy", "gx"),
        P("gy"),
        P("gy"),
        P("gy", ("dp", "gx")),
    )
    return jax.shard_map(
        per_device,
        mesh=mesh,
        in_specs=placed,
        out_specs=(
            P("gy", ("dp", "gx")),
            P("gy", ("dp", "gx")),
            P("gy", "gx"),
            P("gy", "gx"),
            P("gy", None, "gx"),
            P("gy", "gx"),
            P("gy"),
            P("gy"),
        ),
        check_vma=False,
    )
```

```python
import functools

import jax
import jax.numpy as jnp
from jax import lax
from jax.experimental import pallas as pl
from jax.experimental.pallas import tpu as pltpu
from jax.sharding import PartitionSpec as P

D = 960
HD = 64
QPK = 3
L = 1408
SEGS = 4
QW = QPK * HD
SLOT_W = QW + 2 * HD
PACK = SLOT_W + QW
GROUPS = 5
ROWS = 4
CH = L // ROWS
CP = 384
FB = D // ROWS
ODD = PACK // ROWS

EPSILON = 1e-05
THETA_BASE = 100000.0
NEGATIVE = -1e30
SEQ_MAP = (0, 2, 1, 3)
SEQ_BACK = (0, 2, 1, 3)
BF = jnp.bfloat16
F32 = jnp.float32
VMEM_LIMIT = 58 * 1024 * 1024
HALF = HD // 2
AW = 2 * QW
AP = AW + AW // ROWS
KV = 2 * HD
BP = KV + KV // ROWS + 16


def tn(a, b):
    return lax.dot_general(a, b, (((0,), (0,)), ((), ())), preferred_element_type=F32)


def nn(a, b):
    return lax.dot_general(a, b, (((1,), (0,)), ((), ())), preferred_element_type=F32)


def nt(a, b):
    return lax.dot_general(a, b, (((1,), (1,)), ((), ())), preferred_element_type=F32)


def rows_at(block, size=FB):
    return pl.ds(pl.multiple_of(block * FB, 16), size)


def rope(a, b, cos_a, sin_a):
    return a * cos_a - b * sin_a, b * cos_a + a * sin_a


def split_kernel(sc, t_ref, dy_ref, gain_one, gain_two, *outs):
    iy = sc[1]
    lane = lax.broadcasted_iota(jnp.int32, (FB, CP - CH), 1)
    tail = jnp.zeros((FB, CP - CH), F32)
    for i, gain in enumerate((gain_one, gain_two)):
        rest = gain[...]
        for part in range(3):
            piece = rest.astype(BF).astype(F32)
            rest = rest - piece
            tail = jnp.where(lane == 3 * i + part, piece, tail)
    tail = tail.astype(BF)
    blank = jnp.zeros((FB, CP - CH), BF)
    for q in range(ROWS):
        cols = slice(q * CH, (q + 1) * CH)
        block = jnp.concatenate([t_ref[:, cols], tail], axis=1)
        below = jnp.concatenate([dy_ref[:, cols], blank], axis=1)
        for k in range(ROWS):

            @pl.when((iy ^ k) == q)
            def _(k=k, block=block, below=below):
                outs[k][:FB] = block
                outs[k][FB:] = below


def merge_kernel(sc, *refs):
    iy = sc[1]
    for i in range(2):
        rows = slice(i * FB, (i + 1) * FB)
        parts = []
        for q in range(ROWS):
            value = refs[0][rows, :CH]
            for k in range(1, ROWS):
                value = jnp.where((iy ^ k) == q, refs[k][rows, :CH], value)
            parts.append(value)
        refs[ROWS + i][...] = jnp.concatenate(parts, axis=1)


def qkv_kernel(sc, *refs):
    toks = refs[:4]
    w_rows = refs[4:8]
    cos_ref, sin_ref = refs[8:10]
    x_ref, dy_ref, n1_ref, r1_ref, g1_ref, g2_ref, w5_ref, qs_ref, kv_ref = refs[10:]
    ix = sc[0]
    lane = lax.broadcasted_iota(jnp.int32, (FB, CP), 1)
    for k in range(ROWS):
        rows = rows_at(ix ^ k)
        piece = toks[k][:FB].astype(F32)
        dy_ref[rows] = toks[k][FB:]
        x_ref[rows] = jnp.where(lane < CH, piece, 0.0).astype(BF)
        for i, out in enumerate((g1_ref, g2_ref)):
            here = (lane >= CH + 3 * i) & (lane < CH + 3 * i + 3)
            out[rows] = jnp.sum(jnp.where(here, piece, 0.0), axis=1, keepdims=True)
    x = x_ref[...].astype(F32)
    r1 = lax.rsqrt(jnp.sum(x * x, axis=0, keepdims=True) / D + EPSILON)
    r1_ref[...] = r1
    n1_ref[...] = (x * r1 * g1_ref[...]).astype(BF)
    for k in range(ROWS):
        lanes = pl.ds(pl.multiple_of((ix ^ k) * ODD, ODD), ODD)
        for j in range(ROWS):
            rows = rows_at((sc[1] + ROWS - j) % ROWS)
            w5_ref[k, rows] = w_rows[k][j * FB : (j + 1) * FB, :PACK]
            w5_ref[GROUPS - 1, rows, lanes] = w_rows[k][j * FB : (j + 1) * FB, PACK:]
    cos_a = cos_ref[...]
    sin_a = sin_ref[...]
    for g in range(GROUPS):
        p = tn(w5_ref[g, :, :SLOT_W], n1_ref[...])
        for j in range(QPK + 1):
            first, second = rope(
                p[j * HD : j * HD + HALF], p[j * HD + HALF : (j + 1) * HD], cos_a, sin_a
            )
            first = first.astype(BF)
            second = second.astype(BF)
            if j < QPK:
                qs_ref[g, j * HD : j * HD + HALF] = (first.astype(F32) * HD**-0.5).astype(BF)
                qs_ref[g, j * HD + HALF : (j + 1) * HD] = (second.astype(F32) * HD**-0.5).astype(BF)
            else:
                kv_ref[g, :HALF] = first
                kv_ref[g, HALF:HD] = second
        kv_ref[g, HD:] = p[(QPK + 1) * HD :].astype(BF)


def attend_kernel(
    sc, qs_ref, kv0, kv1, kv2, kv3, bias_ref, w_ref, x_ref, gain_ref,
    o_ref, lse_ref, h_ref, n2_ref, r2_ref, m_s, l_s, acc_s,
):
    g = pl.program_id(0)
    kvs = (kv0, kv1, kv2, kv3)

    def fold(k, fresh):
        keys = kvs[k][0, :HD]
        values = kvs[k][0, HD:]
        bias = bias_ref[k]
        for j in range(QPK):
            s = tn(keys, qs_ref[0, j * HD : (j + 1) * HD]) + bias
            top = jnp.max(s, axis=0, keepdims=True)
            if fresh:
                m = top
                e = jnp.exp(s - m)
                l_s[j : j + 1] = jnp.sum(e, axis=0, keepdims=True)
                acc_s[j * HD : (j + 1) * HD] = nn(values, e.astype(BF))
            else:
                old = m_s[j : j + 1]
                m = jnp.maximum(old, top)
                fade = jnp.exp(old - m)
                e = jnp.exp(s - m)
                l_s[j : j + 1] = l_s[j : j + 1] * fade + jnp.sum(e, axis=0, keepdims=True)
                acc_s[j * HD : (j + 1) * HD] = acc_s[j * HD : (j + 1) * HD] * fade + nn(
                    values, e.astype(BF)
                )
            m_s[j : j + 1] = m

    fold(0, True)
    for k in range(1, ROWS):
        pl.when(sc[4 + k] != 0)(functools.partial(fold, k, False))
    for j in range(QPK):
        total = l_s[j : j + 1]
        o_ref[0, j * HD : (j + 1) * HD] = (acc_s[j * HD : (j + 1) * HD] / total).astype(BF)
        lse_ref[0, j : j + 1] = m_s[j : j + 1] + jnp.log(total)
    part = nn(w_ref[0, :, SLOT_W:], o_ref[0])

    @pl.when(g == 0)
    def _():
        h_ref[...] = x_ref[...].astype(F32) + part

    @pl.when(g != 0)
    def _():
        h_ref[...] += part

    @pl.when(g == GROUPS - 1)
    def _():
        h = h_ref[...]
        r2 = lax.rsqrt(jnp.sum(h * h, axis=0, keepdims=True) / D + EPSILON)
        r2_ref[...] = r2
        n2_ref[...] = (h * r2 * gain_ref[...]).astype(BF)


def row_sums(values):
    return lax.dot_general(
        jnp.ones((16, CP), F32), values, (((1,), (1,)), ((), ())),
        precision=lax.Precision.HIGHEST, preferred_element_type=F32,
    )


def attend_back_kernel(
    sc, qs_ref, kv0, kv1, kv2, kv3, bias_ref, w_ref, o_ref, lse_ref, n1_ref, cos_ref, sin_ref,
    dn_a, dn_b, dn_c, h_ref, r2_ref, gain_ref, dy_ref,
    dq_ref, d0, d1, d2, d3, dh_ref, gg_ref, pa0, pa1, pa2, pa3, datt_s, do_s, dl_s, dq_s,
):
    g = pl.program_id(0)
    kvs = (kv0, kv1, kv2, kv3)
    outs = (d0, d1, d2, d3)
    packs = (pa0, pa1, pa2, pa3)

    @pl.when(g == 0)
    def _():
        dn2 = dn_a[...].astype(F32) + dn_b[...].astype(F32) + dn_c[...].astype(F32)
        h = h_ref[...]
        r2 = r2_ref[...]
        weighted = dn2 * gain_ref[...]
        inner = jnp.sum(weighted * h, axis=0, keepdims=True)
        dh = dy_ref[...].astype(F32) + r2 * weighted - h * (r2 * r2 * r2 * inner / D)
        dh_ref[...] = dh
        datt_s[...] = dh.astype(BF)
        for b in range(ROWS):
            rows = slice(b * FB, (b + 1) * FB)
            gg_ref[b] = row_sums(dn2[rows] * h[rows] * r2)

    do_s[...] = tn(w_ref[0, :, SLOT_W:], datt_s[...]).astype(BF)
    for j in range(QPK):
        rows = slice(j * HD, (j + 1) * HD)
        dl_s[j : j + 1] = jnp.sum(
            do_s[rows].astype(F32) * o_ref[0, rows].astype(F32), axis=0, keepdims=True
        )

    def fold(k, fresh):
        keys = kvs[k][0, :HD]
        values = kvs[k][0, HD:]
        bias = bias_ref[k]
        dk = jnp.zeros((HD, CP), F32)
        dv = jnp.zeros((HD, CP), F32)
        for j in range(QPK):
            rows = slice(j * HD, (j + 1) * HD)
            s = tn(keys, qs_ref[0, rows]) + bias
            p = jnp.exp(s - lse_ref[0, j : j + 1])
            do_j = do_s[rows]
            dp = tn(values, do_j)
            ds = (p * (dp - dl_s[j : j + 1])).astype(BF)
            dv = dv + nt(do_j, p.astype(BF))
            dk = dk + nt(qs_ref[0, rows], ds)
            dq = nn(keys, ds)
            if fresh:
                dq_s[rows] = dq
            else:
                dq_s[rows] += dq
        outs[k][0, :HD] = dk.astype(outs[k].dtype)
        outs[k][0, HD:] = dv.astype(outs[k].dtype)

    fold(0, True)
    for k in range(1, ROWS):
        pl.when(sc[4 + k] != 0)(functools.partial(fold, k, False))

        @pl.when(sc[4 + k] == 0)
        def _(k=k):
            outs[k][...] = jnp.zeros(outs[k].shape, outs[k].dtype)

    cos_a = cos_ref[...]
    sin_a = sin_ref[...]
    for j in range(QPK):
        first, second = rope(
            dq_s[j * HD : j * HD + HALF] * HD**-0.5,
            dq_s[j * HD + HALF : (j + 1) * HD] * HD**-0.5,
            cos_a, -sin_a,
        )
        dq_ref[0, j * HD : j * HD + HALF] = first.astype(BF)
        dq_ref[0, j * HD + HALF : (j + 1) * HD] = second.astype(BF)

    for b in range(ROWS):
        rows = slice(b * FB, (b + 1) * FB)
        block = jnp.concatenate(
            [nt(dq_ref[0], n1_ref[rows]).astype(BF), nt(o_ref[0], datt_s[rows]).astype(BF)], axis=0
        )
        for k in range(ROWS):

            @pl.when(g == k)
            def _(k=k, block=block, b=b):
                packs[k][b, :AW] = block

        @pl.when(g == GROUPS - 1)
        def _(block=block, b=b):
            for k in range(ROWS):
                share = AW // ROWS
                for q in range(ROWS):

                    @pl.when((sc[0] ^ k) == q)
                    def _(k=k, q=q):
                        packs[k][b, AW:] = block[q * share : (q + 1) * share]


def final_kernel(
    sc, dq_ref, d0, d1, d2, w_ref, n1_ref, cos_ref, sin_ref, x_ref, r1_ref, gain_ref, dh_ref, gg_ref,
    h_ref, mlp_a, mlp_b, mlp_c,
    pb0, pb1, pb2, pb3, out0, out1, out2, out3, dn_s, dpg_s, dx_s, lo_s,
):
    g = pl.program_id(0)
    packs = (pb0, pb1, pb2, pb3)
    outs = (out0, out1, out2, out3)
    dkv = d0[0] + d1[0].astype(F32) + d2[0].astype(F32)
    first, second = rope(dkv[:HALF], dkv[HALF:HD], cos_ref[...], -sin_ref[...])
    dpg_s[:QW] = dq_ref[0]
    dpg_s[QW : QW + HALF] = first.astype(BF)
    dpg_s[QW + HALF : QW + HD] = second.astype(BF)
    dpg_s[QW + HD :] = dkv[HD:].astype(BF)
    part = nn(w_ref[0, :, :SLOT_W], dpg_s[...])

    @pl.when(g == 0)
    def _():
        dn_s[...] = part

    @pl.when(g != 0)
    def _():
        dn_s[...] += part

    for b in range(ROWS):
        block = nt(dpg_s[QW:], n1_ref[b * FB : (b + 1) * FB]).astype(BF)
        for k in range(ROWS):

            @pl.when(g == k)
            def _(k=k, block=block, b=b):
                packs[k][b, :KV] = block

        @pl.when(g == GROUPS - 1)
        def _(block=block, b=b):
            share = KV // ROWS
            for k in range(ROWS):
                for q in range(ROWS):

                    @pl.when((sc[0] ^ k) == q)
                    def _(k=k, q=q):
                        packs[k][b, KV : KV + share] = block[q * share : (q + 1) * share]

    @pl.when(g == GROUPS - 1)
    def _():
        dn1 = dn_s[...]
        x = x_ref[...].astype(F32)
        r1 = r1_ref[...]
        weighted = dn1 * gain_ref[...]
        inner = jnp.sum(weighted * x, axis=0, keepdims=True)
        dx = dh_ref[...] + r1 * weighted - x * (r1 * r1 * r1 * inner / D)
        dx_s[...] = dx.astype(BF)
        row = lax.broadcasted_iota(jnp.int32, (16, FB), 0)
        for b in range(ROWS):
            rows = slice(b * FB, (b + 1) * FB)
            sums = row_sums(dn1[rows] * x[rows] * r1)
            sums = jnp.where(row == 0, sums, jnp.where(row == 1, gg_ref[b], 0.0)).astype(BF)
            for k in range(ROWS):
                packs[k][b, KV + KV // ROWS :] = sums
        lo_s[...] = (
            h_ref[...] + mlp_a[...].astype(F32) + mlp_b[...].astype(F32) + mlp_c[...].astype(F32)
        ).astype(BF)
        for k in range(ROWS):
            outs[k][:FB] = lo_s[rows_at(sc[0] ^ k)]
            outs[k][FB:] = dx_s[rows_at(sc[0] ^ k)]


def mlp_kernel(count, halves, sc, *refs):
    if halves:
        w = refs[-1]
        part = refs[0].shape[0] // ROWS
        for h in range(2):
            shift = (FB - part) * (sc[3] if h == 0 else 1 - sc[3])
            for b in range(ROWS):
                w[pl.ds(pl.multiple_of(b * FB + shift, 16), part)] = refs[h][b * part : (b + 1) * part]
        wd = refs[2]
        refs = refs[3:-1]
    else:
        w, wd = refs[:2]
        refs = refs[2:]
    width = wd.shape[1]
    for i in range(count):
        n2 = refs[i]
        dy = refs[count + i]
        a_ref, dg_ref, du_ref, mlp_ref, dn_ref = refs[2 * count + 5 * i : 2 * count + 5 * i + 5]
        step = 128
        for f in range(0, width, step):
            cols = slice(f, f + step)
            gate = tn(w[:, f : f + step], n2[...])
            up = tn(w[:, width + f : width + f + step], n2[...])
            da = tn(wd[:, cols], dy[...])
            sigma = jax.nn.sigmoid(gate)
            silu = gate * sigma
            a_ref[cols] = (silu * up).astype(BF)
            dg_ref[cols] = (da * up * sigma * (1.0 + gate * (1.0 - sigma))).astype(BF)
            du_ref[cols] = (da * silu).astype(BF)
        dn_ref[...] = (nn(w[:, :width], dg_ref[...]) + nn(w[:, width : 2 * width], du_ref[...])).astype(BF)
        mlp_ref[...] = nn(wd[...], a_ref[...]).astype(BF)


def mlp_grad_kernel(*refs):
    n2s, dys, acts, gates, ups = (refs[ROWS * i : ROWS * (i + 1)] for i in range(5))
    outs = refs[-2:]
    width = acts[0].shape[0]
    edge = outs[0].shape[1]
    step = 128
    for part, (left, right) in enumerate(((n2s, gates), (n2s, ups), (dys, acts))):
        for f in range(0, width, step):
            total = nt(left[0][...], right[0][f : f + step])
            for k in range(1, ROWS):
                total = total + nt(left[k][...], right[k][f : f + step])
            col = part * width + f
            out = outs[col // edge]
            out[:, col % edge : col % edge + step] = total.astype(BF)


def grads_kernel(sc, g_ref, o0, o1, o2, o3, qkv_ref, out_ref, gains_ref, oa_s, ob_s):
    ix = sc[0]
    share_a = AW // ROWS
    share_b = KV // ROWS
    for k, odd in enumerate((o0, o1, o2, o3)):
        oa_s[pl.ds(pl.multiple_of((ix ^ k) * share_a, 8), share_a)] = odd[:share_a]
        ob_s[pl.ds(pl.multiple_of((ix ^ k) * share_b, 8), share_b)] = odd[share_a:]
    live = (ix == sc[2]).astype(F32)
    oa = oa_s[...] * live
    ob = ob_s[...] * live
    qkv_ref[...] = jnp.transpose(
        jnp.concatenate([g_ref[:QW], g_ref[AP : AP + KV], oa[:QW], ob], axis=0)
    )
    out_ref[...] = jnp.transpose(jnp.concatenate([g_ref[QW:AW], oa[QW:]], axis=0))
    gains_ref[...] = g_ref[AP + KV + share_b : AP + KV + share_b + 8]


def whole(*shape):
    return pl.BlockSpec(shape, lambda *_: (0,) * len(shape))


def per_group(*shape):
    return pl.BlockSpec((1,) + shape, lambda g, *_: (g,) + (0,) * len(shape))


def kv_blocks():
    def spec(k):
        return pl.BlockSpec((1, KV, CP), lambda g, *_: (jnp.where(g < ROWS, g ^ k, g), 0, 0))

    return [spec(k) for k in range(ROWS)]


def sds(shape, dtype):
    return jax.ShapeDtypeStruct(shape, dtype)


MICROSECONDS = {
    "split": 5, "qkv": 7, "attend": 18, "mlp_near": 13, "mlp_far": 13,
    "mlp_grad": 18, "attend_back": 30, "final": 19, "merge": 2, "grads": 3,
}


def cost(name):
    return pl.CostEstimate(
        flops=MICROSECONDS[name] * 100 * 10**6, bytes_accessed=MICROSECONDS[name] * 3000 * 100, transcendentals=0
    )


def simple(kernel, name, outs, *operands, scalars=None, scratch=(), limit=VMEM_LIMIT):
    specs = [pl.BlockSpec(memory_space=pltpu.VMEM)] * len(operands)
    if scalars is not None:
        specs = [pl.BlockSpec(memory_space=pltpu.SMEM)] + specs
        operands = (scalars,) + operands
    return pl.pallas_call(
        kernel,
        in_specs=specs,
        out_specs=[pl.BlockSpec(memory_space=pltpu.VMEM)] * len(outs),
        out_shape=list(outs),
        scratch_shapes=list(scratch),
        compiler_params=pltpu.CompilerParams(vmem_limit_bytes=limit),
        cost_estimate=cost(name),
        name=name,
    )(*operands)


def grouped(kernel, name, in_specs, outs, out_specs, scratch, sc, *operands):
    return pl.pallas_call(
        kernel,
        grid_spec=pltpu.PrefetchScalarGridSpec(
            num_scalar_prefetch=1,
            grid=(GROUPS,),
            in_specs=in_specs,
            out_specs=out_specs,
            scratch_shapes=scratch,
        ),
        out_shape=outs,
        compiler_params=pltpu.CompilerParams(vmem_limit_bytes=VMEM_LIMIT),
        cost_estimate=cost(name),
        name=name,
    )(sc, *operands)


def swap(values, bit):
    return lax.ppermute(values, "gx", [(i, i ^ bit) for i in range(ROWS)])


def row_gather(own):
    far = swap(own, 2)
    mate = swap(own, 1)
    return own, mate, far, swap(far, 1)


def after(values, *first):
    return lax.optimization_barrier((values,) + first)[0]


def row_near(blocks):
    far = (blocks[2].astype(F32) + swap(blocks[3], 1).astype(F32)).astype(BF)
    return blocks[0], swap(blocks[1], 1), far


def row_terms(blocks, first=()):
    a, b, far = row_near(blocks)
    if first:
        far = after(far, *first)
    return a, b, swap(far, 2)


def row_scatter(blocks, first=()):
    a, b, c = row_terms(blocks, first)
    return (a.astype(F32) + b.astype(F32) + c.astype(F32)).astype(BF)


def ring(values):
    return lax.ppermute(values, "gy", [(i, (i + 1) % ROWS) for i in range(ROWS)])


def ring_scatter(blocks, iy):
    def take(at):
        return lax.dynamic_index_in_dim(blocks, at % ROWS, 0, keepdims=False)

    moving = take(iy + 3)
    for s in range(ROWS - 1):
        moving = (ring(moving).astype(F32) + take(iy + 2 - s).astype(F32)).astype(BF)
    return moving


def dp_sum(values):
    if lax.axis_size("dp") == 2:
        return values.astype(F32) + lax.ppermute(values, "dp", [(0, 1), (1, 0)]).astype(F32)
    return lax.psum(values, "dp").astype(F32)


def to_tokens(pieces):
    out = []
    for k in range(ROWS):
        pairs = [(a * ROWS + b, (b ^ k) * ROWS + SEQ_MAP[a]) for a in range(ROWS) for b in range(ROWS)]
        out.append(lax.ppermute(pieces[k], ("gx", "gy"), pairs))
    return out


def to_features(pieces):
    back = []
    for k in range(ROWS):
        pairs = [(a * ROWS + b, SEQ_BACK[b] * ROWS + (a ^ k)) for a in range(ROWS) for b in range(ROWS)]
        back.append(lax.ppermute(pieces[k], ("gx", "gy"), pairs))
    return back


def per_device(
    tokens, segment_ids, slot_table, w_qkv, w_out, w_gate_up, w_down, gain_attn, gain_mlp, cotangent
):
    ix = lax.axis_index("gx")
    iy = lax.axis_index("gy")
    ff = w_down.shape[1]
    odd_row = jnp.sum(jnp.where(slot_table % 2 == 1, slot_table // 2, 0))

    seg = lax.ppermute(segment_ids, "gy", [(i, SEQ_MAP[i]) for i in range(ROWS)]).reshape(ROWS, CH)
    seg_own = lax.dynamic_index_in_dim(seg, ix, 0, keepdims=False)
    starts = [jnp.sum(seg < s).astype(jnp.int32) for s in range(SEGS)]
    first = sum(jnp.where(seg_own == s, starts[s], 0) for s in range(SEGS))
    at_own = jnp.arange(CP, dtype=jnp.int32)
    position = (ix * CH + at_own - jnp.pad(first, (0, CP - CH))).astype(F32)
    frequency = THETA_BASE ** (-2.0 * jnp.arange(HALF, dtype=F32) / HD)
    angles = frequency[:, None] * position[None, :]
    cos_a = jnp.cos(angles)
    sin_a = jnp.sin(angles)
    query_docs = jnp.pad(seg_own, (0, CP - CH), constant_values=-1)
    biases = []
    flags = []
    for k in range(ROWS):
        seg_k = lax.dynamic_index_in_dim(seg, ix ^ k, 0, keepdims=False)
        key_docs = jnp.pad(seg_k, (0, CP - CH), constant_values=-2)
        allowed = (key_docs[:, None] == query_docs[None, :]) & (
            ((ix ^ k) * CH + at_own)[:, None] <= (ix * CH + at_own)[None, :]
        )
        biases.append(jnp.where(allowed, 0.0, NEGATIVE).astype(F32))
        flags.append(((ix ^ k) <= ix) & (seg_k[CH - 1] >= seg_own[0]))
    bias = jnp.stack(biases)
    idp = lax.axis_index("dp")
    at = jnp.stack([ix, iy, odd_row, idp]).astype(jnp.int32)
    sc = jnp.concatenate([at, jnp.stack(flags).astype(jnp.int32)])

    pieces = simple(
        split_kernel, "split", [sds((2 * FB, CP), BF)] * ROWS,
        tokens, cotangent, gain_attn[:, None], gain_mlp[:, None], scalars=at,
    )
    odd = jnp.concatenate([w_qkv[:, SLOT_W:], w_out[:, QW:]], axis=1)
    odd = jnp.where(ix == odd_row, odd, jnp.zeros_like(odd))
    quarter = row_scatter([lax.dynamic_slice(odd, (0, ODD * (ix ^ k)), (FB, ODD)) for k in range(ROWS)])
    w_pieces = [after(jnp.concatenate([w_qkv[:, :SLOT_W], w_out[:, :QW], quarter], axis=1), pieces[0])]
    toks = to_tokens(pieces)
    for _ in range(ROWS - 1):
        w_pieces.append(ring(w_pieces[-1]))
    w_own = jnp.concatenate(w_pieces, axis=0)
    w_far = jnp.concatenate([swap(w, 2) for w in w_pieces], axis=0)
    w_rows = [w_own, swap(w_own, 1), w_far, swap(w_far, 1)]
    w_gu = jnp.concatenate([w_gate_up[:, 0], w_gate_up[:, 1]], axis=1)
    halves = lax.axis_size("dp") == 2
    if halves:
        w_gu = lax.dynamic_slice(w_gu, ((FB - 128) * idp, 0), (128, 2 * ff))
    w_gu = [lax.all_gather(after(w_gu, *toks), "gy", axis=0, tiled=True)]
    if halves:
        w_gu.append(lax.ppermute(w_gu[0], "dp", [(0, 1), (1, 0)]))
    x, dy, n1, r1, gain_one, gain_two, w5, qs, kv = simple(
        qkv_kernel, "qkv",
        [
            sds((D, CP), BF), sds((D, CP), BF), sds((D, CP), BF), sds((1, CP), F32), sds((D, 1), F32), sds((D, 1), F32),
            sds((GROUPS, D, PACK), BF), sds((GROUPS, QW, CP), BF), sds((GROUPS, KV, CP), BF),
        ],
        *toks, *w_rows, cos_a, sin_a,
        scalars=at,
    )

    w_d = lax.all_gather(w_down, "gy", axis=0, tiled=True)

    kvs = row_gather(kv)
    dys = row_gather(after(dy, kvs[2]))
    o, lse, h, n2, r2 = grouped(
        attend_kernel, "attend",
        [per_group(QW, CP)] + kv_blocks()
        + [whole(ROWS, CP, CP), per_group(D, PACK), whole(D, CP), whole(D, 1)],
        [
            sds((GROUPS, QW, CP), BF), sds((GROUPS, 8, CP), F32), sds((D, CP), F32), sds((D, CP), BF),
            sds((1, CP), F32),
        ],
        [per_group(QW, CP), per_group(8, CP), whole(D, CP), whole(D, CP), whole(1, CP)],
        [pltpu.VMEM((8, CP), F32), pltpu.VMEM((8, CP), F32), pltpu.VMEM((QW, CP), F32)],
        sc, after(qs, w_gu[0]), *kvs, bias, w5, x, gain_two,
    )

    n2s = row_gather(n2)
    per_block = [sds((ff, CP), BF)] * 3 + [sds((D, CP), BF)] * 2
    def feed_forward(name, some_n2, some_dy):
        return simple(
            functools.partial(mlp_kernel, 2, halves), name, per_block * 2, *w_gu, w_d, *some_n2, *some_dy,
            scalars=at, scratch=[pltpu.VMEM((D, 2 * ff), BF)] if halves else [],
        )

    far = feed_forward("mlp_far", n2s[2:], dys[2:])
    near = feed_forward("mlp_near", [after(n2s[0], far[9]), n2s[1]], dys[:2])
    blocks = [near[:5], near[5:], far[:5], far[5:]]
    dn2_terms = list(row_near([b[4] for b in blocks]))
    mlp_terms = list(row_near([b[3] for b in blocks]))

    dn2_terms[2] = swap(dn2_terms[2], 2)
    wide = (3 * ff // 2 + 127) // 128 * 128
    g_mlp = simple(
        mlp_grad_kernel, "mlp_grad", [sds((D, wide), BF), sds((D, 3 * ff - wide), BF)],
        after(n2s[0], dn2_terms[2]), *n2s[1:], *dys,
        *[b[0] for b in blocks], *[b[1] for b in blocks], *[b[2] for b in blocks],
    )

    pack_a = sds((ROWS, AP, FB), BF)

    def beside_back(far, *operands):
        return swap(far, 2), grouped(
        attend_back_kernel, "attend_back",
        [per_group(QW, CP)] + kv_blocks()
        + [whole(ROWS, CP, CP), per_group(D, PACK), per_group(QW, CP), per_group(8, CP), whole(D, CP),
           whole(HALF, CP), whole(HALF, CP)]
        + [whole(D, CP)] * 4 + [whole(1, CP), whole(D, 1), whole(D, CP)],
        [sds((GROUPS, QW, CP), BF), sds((GROUPS, KV, CP), F32)] + [sds((GROUPS, KV, CP), BF)] * 3
        + [sds((D, CP), F32), sds((ROWS, 16, FB), F32)] + [pack_a] * ROWS,
        [per_group(QW, CP)] + kv_blocks() + [whole(D, CP), whole(ROWS, 16, FB)]
        + [whole(ROWS, AP, FB)] * ROWS,
        [pltpu.VMEM((D, CP), BF), pltpu.VMEM((QW, CP), BF), pltpu.VMEM((8, CP), F32), pltpu.VMEM((QW, CP), F32)],
            *operands,
        )

    mlp_terms[2] = after(mlp_terms[2], dn2_terms[2])
    dn2_terms[1] = after(dn2_terms[1], g_mlp[0], mlp_terms[2])
    mlp_terms[2], back = beside_back(
        mlp_terms[2],
        sc, qs, *kvs, bias, w5, o, lse, n1, cos_a, sin_a, *dn2_terms, h, r2, gain_two, dy,
    )
    dq, dkv, dh, gg, packs_a = back[0], list(back[1:5]), back[5], back[6], back[7:]
    g_mlp = [lax.psum_scatter(g, "gy", scatter_dimension=0, tiled=True) for g in g_mlp]
    dkv[2] = after(dkv[2], mlp_terms[2], g_mlp[0])
    dkv_terms = list(row_terms(dkv))
    a_terms = list(row_near(packs_a))
    a_terms[2] = after(a_terms[2], dkv_terms[2])
    dkv_terms[0] = after(dkv_terms[0], a_terms[2])
    a_terms[2] = swap(a_terms[2], 2)
    final = grouped(
        final_kernel, "final",
        [per_group(QW, CP)] + [per_group(KV, CP)] * 3
        + [per_group(D, PACK), whole(D, CP), whole(HALF, CP), whole(HALF, CP), whole(D, CP), whole(1, CP),
           whole(D, 1), whole(D, CP), whole(ROWS, 16, FB)] + [whole(D, CP)] * 4,
        [sds((ROWS, BP, FB), BF)] * ROWS + [sds((2 * FB, CP), BF)] * ROWS,
        [whole(ROWS, BP, FB)] * ROWS + [whole(2 * FB, CP)] * ROWS,
        [pltpu.VMEM((D, CP), F32), pltpu.VMEM((SLOT_W, CP), BF)] + [pltpu.VMEM((D, CP), BF)] * 2,
        sc, dq, *dkv_terms, w5, n1, cos_a, sin_a, x, r1, gain_one, dh, gg, h, *mlp_terms,
    )
    packs_b, out_pieces = final[:ROWS], final[ROWS:]
    back = to_features(out_pieces)
    layer_out, input_grad = simple(merge_kernel, "merge", [sds((FB, L), BF)] * 2, *back, scalars=at)

    g_mlp = jnp.concatenate([dp_sum(g) for g in g_mlp], axis=1)
    grad_down = g_mlp[:, 2 * ff :]
    g_a = sum(term.astype(F32) for term in a_terms).astype(BF)
    packs_b = list(packs_b)
    packs_b[2] = after(packs_b[2], a_terms[2])
    g_a = lax.psum_scatter(g_a.reshape(ROWS * AP, FB), "gy", scatter_dimension=0, tiled=True)
    g_b = after(row_scatter(packs_b).reshape(ROWS * BP, FB), *back)
    g_b = lax.psum_scatter(g_b, "gy", scatter_dimension=0, tiled=True)
    g_all = dp_sum(jnp.concatenate([g_a, g_b], axis=0))
    odds = jnp.concatenate([g_all[AW:AP], g_all[AP + KV : AP + KV + KV // ROWS]], axis=0)
    grad_qkv, grad_out, grad_gains = simple(
        grads_kernel, "grads",
        [sds((FB, 2 * SLOT_W), F32), sds((FB, 2 * QW), F32), sds((8, FB), F32)],
        g_all, *row_gather(odds), scalars=at,
        scratch=[pltpu.VMEM((AW, FB), F32), pltpu.VMEM((KV, FB), F32)],
    )
    grad_gate_up = jnp.stack([g_mlp[:, :ff], g_mlp[:, ff : 2 * ff]], axis=1)
    return (
        layer_out,
        input_grad,
        grad_qkv,
        grad_out,
        grad_gate_up,
        grad_down,
        grad_gains[0],
        grad_gains[1],
    )


def solution(mesh):
    placed = (
        P("gy", ("dp", "gx")),
        P(("dp", "gy"), None),
        P(),
        P("gy", "gx"),
        P("gy", "gx"),
        P("gy", None, "gx"),
        P("gy", "gx"),
        P("gy"),
        P("gy"),
        P("gy", ("dp", "gx")),
    )
    return jax.shard_map(
        per_device,
        mesh=mesh,
        in_specs=placed,
        out_specs=(
            P("gy", ("dp", "gx")),
            P("gy", ("dp", "gx")),
            P("gy", "gx"),
            P("gy", "gx"),
            P("gy", None, "gx"),
            P("gy", "gx"),
            P("gy"),
            P("gy"),
        ),
        check_vma=False,
    )
```

```python
import functools

import jax
import jax.numpy as jnp
from jax import lax
from jax.experimental import pallas as pl
from jax.experimental.pallas import tpu as pltpu
from jax.sharding import PartitionSpec as P

D = 960
HD = 64
QPK = 3
L = 1408
SEGS = 4
QW = QPK * HD
SLOT_W = QW + 2 * HD
PACK = SLOT_W + QW
GROUPS = 5
ROWS = 4
CH = L // ROWS
CP = 384
FB = D // ROWS
ODD = PACK // ROWS

EPSILON = 1e-05
THETA_BASE = 100000.0
NEGATIVE = -1e30
SEQ_MAP = (0, 2, 1, 3)
SEQ_BACK = (0, 2, 1, 3)
BF = jnp.bfloat16
F32 = jnp.float32
VMEM_LIMIT = 58 * 1024 * 1024
HALF = HD // 2
AW = 2 * QW
AP = AW + AW // ROWS
KV = 2 * HD
BP = KV + KV // ROWS + 16


def tn(a, b):
    return lax.dot_general(a, b, (((0,), (0,)), ((), ())), preferred_element_type=F32)


def nn(a, b):
    return lax.dot_general(a, b, (((1,), (0,)), ((), ())), preferred_element_type=F32)


def nt(a, b):
    return lax.dot_general(a, b, (((1,), (1,)), ((), ())), preferred_element_type=F32)


def rows_at(block, size=FB):
    return pl.ds(pl.multiple_of(block * FB, 16), size)


def rope(a, b, cos_a, sin_a):
    return a * cos_a - b * sin_a, b * cos_a + a * sin_a


def split_kernel(sc, t_ref, dy_ref, gain_one, gain_two, *outs):
    iy = sc[1]
    lane = lax.broadcasted_iota(jnp.int32, (FB, CP - CH), 1)
    tail = jnp.zeros((FB, CP - CH), F32)
    for i, gain in enumerate((gain_one, gain_two)):
        rest = gain[...]
        for part in range(3):
            piece = rest.astype(BF).astype(F32)
            rest = rest - piece
            tail = jnp.where(lane == 3 * i + part, piece, tail)
    tail = tail.astype(BF)
    blank = jnp.zeros((FB, CP - CH), BF)
    for q in range(ROWS):
        cols = slice(q * CH, (q + 1) * CH)
        block = jnp.concatenate([t_ref[:, cols], tail], axis=1)
        below = jnp.concatenate([dy_ref[:, cols], blank], axis=1)
        for k in range(ROWS):

            @pl.when((iy ^ k) == q)
            def _(k=k, block=block, below=below):
                outs[k][:FB] = block
                outs[k][FB:] = below


def merge_kernel(sc, *refs):
    iy = sc[1]
    for i in range(2):
        rows = slice(i * FB, (i + 1) * FB)
        parts = []
        for q in range(ROWS):
            value = refs[0][rows, :CH]
            for k in range(1, ROWS):
                value = jnp.where((iy ^ k) == q, refs[k][rows, :CH], value)
            parts.append(value)
        refs[ROWS + i][...] = jnp.concatenate(parts, axis=1)


def qkv_kernel(sc, *refs):
    toks = refs[:4]
    w_rows = refs[4:8]
    cos_ref, sin_ref = refs[8:10]
    x_ref, dy_ref, n1_ref, r1_ref, g1_ref, g2_ref, w5_ref, qs_ref, kv_ref = refs[10:]
    ix = sc[0]
    lane = lax.broadcasted_iota(jnp.int32, (FB, CP), 1)
    for k in range(ROWS):
        rows = rows_at(ix ^ k)
        piece = toks[k][:FB].astype(F32)
        dy_ref[rows] = toks[k][FB:]
        x_ref[rows] = jnp.where(lane < CH, piece, 0.0).astype(BF)
        for i, out in enumerate((g1_ref, g2_ref)):
            here = (lane >= CH + 3 * i) & (lane < CH + 3 * i + 3)
            out[rows] = jnp.sum(jnp.where(here, piece, 0.0), axis=1, keepdims=True)
    x = x_ref[...].astype(F32)
    r1 = lax.rsqrt(jnp.sum(x * x, axis=0, keepdims=True) / D + EPSILON)
    r1_ref[...] = r1
    n1_ref[...] = (x * r1 * g1_ref[...]).astype(BF)
    for k in range(ROWS):
        lanes = pl.ds(pl.multiple_of((ix ^ k) * ODD, ODD), ODD)
        for j in range(ROWS):
            rows = rows_at((sc[1] + ROWS - j) % ROWS)
            w5_ref[k, rows] = w_rows[k][j * FB : (j + 1) * FB, :PACK]
            w5_ref[GROUPS - 1, rows, lanes] = w_rows[k][j * FB : (j + 1) * FB, PACK:]
    cos_a = cos_ref[...]
    sin_a = sin_ref[...]
    for g in range(GROUPS):
        p = tn(w5_ref[g, :, :SLOT_W], n1_ref[...])
        for j in range(QPK + 1):
            first, second = rope(
                p[j * HD : j * HD + HALF], p[j * HD + HALF : (j + 1) * HD], cos_a, sin_a
            )
            first = first.astype(BF)
            second = second.astype(BF)
            if j < QPK:
                qs_ref[g, j * HD : j * HD + HALF] = (first.astype(F32) * HD**-0.5).astype(BF)
                qs_ref[g, j * HD + HALF : (j + 1) * HD] = (second.astype(F32) * HD**-0.5).astype(BF)
            else:
                kv_ref[g, :HALF] = first
                kv_ref[g, HALF:HD] = second
        kv_ref[g, HD:] = p[(QPK + 1) * HD :].astype(BF)


def attend_kernel(
    sc, qs_ref, kv0, kv1, kv2, kv3, bias_ref, w_ref, x_ref, gain_ref,
    o_ref, lse_ref, h_ref, n2_ref, r2_ref, m_s, l_s, acc_s,
):
    g = pl.program_id(0)
    kvs = (kv0, kv1, kv2, kv3)

    def fold(k, fresh):
        keys = kvs[k][0, :HD]
        values = kvs[k][0, HD:]
        bias = bias_ref[k]
        for j in range(QPK):
            s = tn(keys, qs_ref[0, j * HD : (j + 1) * HD]) + bias
            top = jnp.max(s, axis=0, keepdims=True)
            if fresh:
                m = top
                e = jnp.exp(s - m)
                l_s[j : j + 1] = jnp.sum(e, axis=0, keepdims=True)
                acc_s[j * HD : (j + 1) * HD] = nn(values, e.astype(BF))
            else:
                old = m_s[j : j + 1]
                m = jnp.maximum(old, top)
                fade = jnp.exp(old - m)
                e = jnp.exp(s - m)
                l_s[j : j + 1] = l_s[j : j + 1] * fade + jnp.sum(e, axis=0, keepdims=True)
                acc_s[j * HD : (j + 1) * HD] = acc_s[j * HD : (j + 1) * HD] * fade + nn(
                    values, e.astype(BF)
                )
            m_s[j : j + 1] = m

    fold(0, True)
    for k in range(1, ROWS):
        pl.when(sc[4 + k] != 0)(functools.partial(fold, k, False))
    for j in range(QPK):
        total = l_s[j : j + 1]
        o_ref[0, j * HD : (j + 1) * HD] = (acc_s[j * HD : (j + 1) * HD] / total).astype(BF)
        lse_ref[0, j : j + 1] = m_s[j : j + 1] + jnp.log(total)
    part = nn(w_ref[0, :, SLOT_W:], o_ref[0])

    @pl.when(g == 0)
    def _():
        h_ref[...] = x_ref[...].astype(F32) + part

    @pl.when(g != 0)
    def _():
        h_ref[...] += part

    @pl.when(g == GROUPS - 1)
    def _():
        h = h_ref[...]
        r2 = lax.rsqrt(jnp.sum(h * h, axis=0, keepdims=True) / D + EPSILON)
        r2_ref[...] = r2
        n2_ref[...] = (h * r2 * gain_ref[...]).astype(BF)


def row_sums(values):
    return lax.dot_general(
        jnp.ones((16, CP), F32), values, (((1,), (1,)), ((), ())),
        precision=lax.Precision.HIGHEST, preferred_element_type=F32,
    )


def attend_back_kernel(
    sc, qs_ref, kv0, kv1, kv2, kv3, bias_ref, w_ref, o_ref, lse_ref, n1_ref, cos_ref, sin_ref,
    dn_a, dn_b, dn_c, h_ref, r2_ref, gain_ref, dy_ref,
    dq_ref, d0, d1, d2, d3, dh_ref, gg_ref, pa0, pa1, pa2, pa3, datt_s, do_s, dl_s, dq_s,
):
    g = pl.program_id(0)
    kvs = (kv0, kv1, kv2, kv3)
    outs = (d0, d1, d2, d3)
    packs = (pa0, pa1, pa2, pa3)

    @pl.when(g == 0)
    def _():
        dn2 = dn_a[...].astype(F32) + dn_b[...].astype(F32) + dn_c[...].astype(F32)
        h = h_ref[...]
        r2 = r2_ref[...]
        weighted = dn2 * gain_ref[...]
        inner = jnp.sum(weighted * h, axis=0, keepdims=True)
        dh = dy_ref[...].astype(F32) + r2 * weighted - h * (r2 * r2 * r2 * inner / D)
        dh_ref[...] = dh
        datt_s[...] = dh.astype(BF)
        for b in range(ROWS):
            rows = slice(b * FB, (b + 1) * FB)
            gg_ref[b] = row_sums(dn2[rows] * h[rows] * r2)

    do_s[...] = tn(w_ref[0, :, SLOT_W:], datt_s[...]).astype(BF)
    for j in range(QPK):
        rows = slice(j * HD, (j + 1) * HD)
        dl_s[j : j + 1] = jnp.sum(
            do_s[rows].astype(F32) * o_ref[0, rows].astype(F32), axis=0, keepdims=True
        )

    def fold(k, fresh):
        keys = kvs[k][0, :HD]
        values = kvs[k][0, HD:]
        bias = bias_ref[k]
        dk = jnp.zeros((HD, CP), F32)
        dv = jnp.zeros((HD, CP), F32)
        for j in range(QPK):
            rows = slice(j * HD, (j + 1) * HD)
            s = tn(keys, qs_ref[0, rows]) + bias
            p = jnp.exp(s - lse_ref[0, j : j + 1])
            do_j = do_s[rows]
            dp = tn(values, do_j)
            ds = (p * (dp - dl_s[j : j + 1])).astype(BF)
            dv = dv + nt(do_j, p.astype(BF))
            dk = dk + nt(qs_ref[0, rows], ds)
            dq = nn(keys, ds)
            if fresh:
                dq_s[rows] = dq
            else:
                dq_s[rows] += dq
        outs[k][0, :HD] = dk.astype(outs[k].dtype)
        outs[k][0, HD:] = dv.astype(outs[k].dtype)

    fold(0, True)
    for k in range(1, ROWS):
        pl.when(sc[4 + k] != 0)(functools.partial(fold, k, False))

        @pl.when(sc[4 + k] == 0)
        def _(k=k):
            outs[k][...] = jnp.zeros(outs[k].shape, outs[k].dtype)

    cos_a = cos_ref[...]
    sin_a = sin_ref[...]
    for j in range(QPK):
        first, second = rope(
            dq_s[j * HD : j * HD + HALF] * HD**-0.5,
            dq_s[j * HD + HALF : (j + 1) * HD] * HD**-0.5,
            cos_a, -sin_a,
        )
        dq_ref[0, j * HD : j * HD + HALF] = first.astype(BF)
        dq_ref[0, j * HD + HALF : (j + 1) * HD] = second.astype(BF)

    for b in range(ROWS):
        rows = slice(b * FB, (b + 1) * FB)
        block = jnp.concatenate(
            [nt(dq_ref[0], n1_ref[rows]).astype(BF), nt(o_ref[0], datt_s[rows]).astype(BF)], axis=0
        )
        for k in range(ROWS):

            @pl.when(g == k)
            def _(k=k, block=block, b=b):
                packs[k][b, :AW] = block

        @pl.when(g == GROUPS - 1)
        def _(block=block, b=b):
            for k in range(ROWS):
                share = AW // ROWS
                for q in range(ROWS):

                    @pl.when((sc[0] ^ k) == q)
                    def _(k=k, q=q):
                        packs[k][b, AW:] = block[q * share : (q + 1) * share]


def final_kernel(
    sc, dq_ref, d0, d1, d2, w_ref, n1_ref, cos_ref, sin_ref, x_ref, r1_ref, gain_ref, dh_ref, gg_ref,
    h_ref, mlp_a, mlp_b, mlp_c,
    pb0, pb1, pb2, pb3, out0, out1, out2, out3, dn_s, dpg_s, dx_s, lo_s,
):
    g = pl.program_id(0)
    packs = (pb0, pb1, pb2, pb3)
    outs = (out0, out1, out2, out3)
    dkv = d0[0] + d1[0].astype(F32) + d2[0].astype(F32)
    first, second = rope(dkv[:HALF], dkv[HALF:HD], cos_ref[...], -sin_ref[...])
    dpg_s[:QW] = dq_ref[0]
    dpg_s[QW : QW + HALF] = first.astype(BF)
    dpg_s[QW + HALF : QW + HD] = second.astype(BF)
    dpg_s[QW + HD :] = dkv[HD:].astype(BF)
    part = nn(w_ref[0, :, :SLOT_W], dpg_s[...])

    @pl.when(g == 0)
    def _():
        dn_s[...] = part

    @pl.when(g != 0)
    def _():
        dn_s[...] += part

    for b in range(ROWS):
        block = nt(dpg_s[QW:], n1_ref[b * FB : (b + 1) * FB]).astype(BF)
        for k in range(ROWS):

            @pl.when(g == k)
            def _(k=k, block=block, b=b):
                packs[k][b, :KV] = block

        @pl.when(g == GROUPS - 1)
        def _(block=block, b=b):
            share = KV // ROWS
            for k in range(ROWS):
                for q in range(ROWS):

                    @pl.when((sc[0] ^ k) == q)
                    def _(k=k, q=q):
                        packs[k][b, KV : KV + share] = block[q * share : (q + 1) * share]

    @pl.when(g == GROUPS - 1)
    def _():
        dn1 = dn_s[...]
        x = x_ref[...].astype(F32)
        r1 = r1_ref[...]
        weighted = dn1 * gain_ref[...]
        inner = jnp.sum(weighted * x, axis=0, keepdims=True)
        dx = dh_ref[...] + r1 * weighted - x * (r1 * r1 * r1 * inner / D)
        dx_s[...] = dx.astype(BF)
        row = lax.broadcasted_iota(jnp.int32, (16, FB), 0)
        for b in range(ROWS):
            rows = slice(b * FB, (b + 1) * FB)
            sums = row_sums(dn1[rows] * x[rows] * r1)
            sums = jnp.where(row == 0, sums, jnp.where(row == 1, gg_ref[b], 0.0)).astype(BF)
            for k in range(ROWS):
                packs[k][b, KV + KV // ROWS :] = sums
        lo_s[...] = (
            h_ref[...] + mlp_a[...].astype(F32) + mlp_b[...].astype(F32) + mlp_c[...].astype(F32)
        ).astype(BF)
        for k in range(ROWS):
            outs[k][:FB] = lo_s[rows_at(sc[0] ^ k)]
            outs[k][FB:] = dx_s[rows_at(sc[0] ^ k)]


def mlp_kernel(count, halves, sc, *refs):
    if halves:
        w = refs[-1]
        part = refs[0].shape[0] // ROWS
        for h in range(2):
            shift = (FB - part) * (sc[3] if h == 0 else 1 - sc[3])
            for b in range(ROWS):
                w[pl.ds(pl.multiple_of(b * FB + shift, 16), part)] = refs[h][b * part : (b + 1) * part]
        wd = refs[2]
        refs = refs[3:-1]
    else:
        w, wd = refs[:2]
        refs = refs[2:]
    width = wd.shape[1]
    for i in range(count):
        n2 = refs[i]
        dy = refs[count + i]
        a_ref, dg_ref, du_ref, mlp_ref, dn_ref = refs[2 * count + 5 * i : 2 * count + 5 * i + 5]
        step = width
        for f in range(0, width, step):
            cols = slice(f, f + step)
            gate = tn(w[:, f : f + step], n2[...])
            up = tn(w[:, width + f : width + f + step], n2[...])
            da = tn(wd[:, cols], dy[...])
            sigma = jax.nn.sigmoid(gate)
            silu = gate * sigma
            a_ref[cols] = (silu * up).astype(BF)
            dg_ref[cols] = (da * up * sigma * (1.0 + gate * (1.0 - sigma))).astype(BF)
            du_ref[cols] = (da * silu).astype(BF)
        dn_ref[...] = (nn(w[:, :width], dg_ref[...]) + nn(w[:, width : 2 * width], du_ref[...])).astype(BF)
        mlp_ref[...] = nn(wd[...], a_ref[...]).astype(BF)


def mlp_grad_kernel(*refs):
    n2s, dys, acts, gates, ups = (refs[ROWS * i : ROWS * (i + 1)] for i in range(5))
    outs = refs[-2:]
    width = acts[0].shape[0]
    edge = outs[0].shape[1]
    for part, (left, right) in enumerate(((n2s, gates), (n2s, ups), (dys, acts))):
        begin = part * width
        cuts = [begin] + ([edge] if begin < edge < begin + width else []) + [begin + width]
        for low, high in zip(cuts[:-1], cuts[1:]):
            total = nt(left[0][...], right[0][low - begin : high - begin])
            for k in range(1, ROWS):
                total = total + nt(left[k][...], right[k][low - begin : high - begin])
            outs[low // edge][:, low % edge : low % edge + high - low] = total.astype(BF)


def grads_kernel(sc, g_ref, o0, o1, o2, o3, qkv_ref, out_ref, gains_ref, oa_s, ob_s):
    ix = sc[0]
    share_a = AW // ROWS
    share_b = KV // ROWS
    for k, odd in enumerate((o0, o1, o2, o3)):
        oa_s[pl.ds(pl.multiple_of((ix ^ k) * share_a, 8), share_a)] = odd[:share_a]
        ob_s[pl.ds(pl.multiple_of((ix ^ k) * share_b, 8), share_b)] = odd[share_a:]
    live = (ix == sc[2]).astype(F32)
    oa = oa_s[...] * live
    ob = ob_s[...] * live
    qkv_ref[...] = jnp.transpose(
        jnp.concatenate([g_ref[:QW], g_ref[AP : AP + KV], oa[:QW], ob], axis=0)
    )
    out_ref[...] = jnp.transpose(jnp.concatenate([g_ref[QW:AW], oa[QW:]], axis=0))
    gains_ref[...] = g_ref[AP + KV + share_b : AP + KV + share_b + 8]


def whole(*shape):
    return pl.BlockSpec(shape, lambda *_: (0,) * len(shape))


def per_group(*shape):
    return pl.BlockSpec((1,) + shape, lambda g, *_: (g,) + (0,) * len(shape))


def kv_blocks():
    def spec(k):
        return pl.BlockSpec((1, KV, CP), lambda g, *_: (jnp.where(g < ROWS, g ^ k, g), 0, 0))

    return [spec(k) for k in range(ROWS)]


def sds(shape, dtype):
    return jax.ShapeDtypeStruct(shape, dtype)


MICROSECONDS = {
    "split": 5, "qkv": 7, "attend": 18, "mlp_near": 13, "mlp_far": 13,
    "mlp_grad": 18, "attend_back": 30, "final": 19, "merge": 2, "grads": 3,
}


def cost(name):
    return pl.CostEstimate(
        flops=MICROSECONDS[name] * 100 * 10**6, bytes_accessed=MICROSECONDS[name] * 3000 * 100, transcendentals=0
    )


def simple(kernel, name, outs, *operands, scalars=None, scratch=(), limit=VMEM_LIMIT):
    specs = [pl.BlockSpec(memory_space=pltpu.VMEM)] * len(operands)
    if scalars is not None:
        specs = [pl.BlockSpec(memory_space=pltpu.SMEM)] + specs
        operands = (scalars,) + operands
    return pl.pallas_call(
        kernel,
        in_specs=specs,
        out_specs=[pl.BlockSpec(memory_space=pltpu.VMEM)] * len(outs),
        out_shape=list(outs),
        scratch_shapes=list(scratch),
        compiler_params=pltpu.CompilerParams(vmem_limit_bytes=limit),
        cost_estimate=cost(name),
        name=name,
    )(*operands)


def grouped(kernel, name, in_specs, outs, out_specs, scratch, sc, *operands):
    return pl.pallas_call(
        kernel,
        grid_spec=pltpu.PrefetchScalarGridSpec(
            num_scalar_prefetch=1,
            grid=(GROUPS,),
            in_specs=in_specs,
            out_specs=out_specs,
            scratch_shapes=scratch,
        ),
        out_shape=outs,
        compiler_params=pltpu.CompilerParams(vmem_limit_bytes=VMEM_LIMIT),
        cost_estimate=cost(name),
        name=name,
    )(sc, *operands)


def swap(values, bit):
    return lax.ppermute(values, "gx", [(i, i ^ bit) for i in range(ROWS)])


def row_gather(own):
    far = swap(own, 2)
    mate = swap(own, 1)
    return own, mate, far, swap(far, 1)


def after(values, *first):
    return lax.optimization_barrier((values,) + first)[0]


def row_near(blocks):
    far = (blocks[2].astype(F32) + swap(blocks[3], 1).astype(F32)).astype(BF)
    return blocks[0], swap(blocks[1], 1), far


def row_terms(blocks, first=()):
    a, b, far = row_near(blocks)
    if first:
        far = after(far, *first)
    return a, b, swap(far, 2)


def row_scatter(blocks, first=()):
    a, b, c = row_terms(blocks, first)
    return (a.astype(F32) + b.astype(F32) + c.astype(F32)).astype(BF)


def ring(values):
    return lax.ppermute(values, "gy", [(i, (i + 1) % ROWS) for i in range(ROWS)])


def ring_scatter(blocks, iy):
    def take(at):
        return lax.dynamic_index_in_dim(blocks, at % ROWS, 0, keepdims=False)

    moving = take(iy + 3)
    for s in range(ROWS - 1):
        moving = (ring(moving).astype(F32) + take(iy + 2 - s).astype(F32)).astype(BF)
    return moving


def dp_sum(values):
    if lax.axis_size("dp") == 2:
        return values.astype(F32) + lax.ppermute(values, "dp", [(0, 1), (1, 0)]).astype(F32)
    return lax.psum(values, "dp").astype(F32)


def to_token(k, piece):
    pairs = [(a * ROWS + b, (b ^ k) * ROWS + SEQ_MAP[a]) for a in range(ROWS) for b in range(ROWS)]
    return lax.ppermute(piece, ("gx", "gy"), pairs)


def to_features(pieces):
    back = []
    for k in range(ROWS):
        pairs = [(a * ROWS + b, SEQ_BACK[b] * ROWS + (a ^ k)) for a in range(ROWS) for b in range(ROWS)]
        back.append(lax.ppermute(pieces[k], ("gx", "gy"), pairs))
    return back


def per_device(
    tokens, segment_ids, slot_table, w_qkv, w_out, w_gate_up, w_down, gain_attn, gain_mlp, cotangent
):
    ix = lax.axis_index("gx")
    iy = lax.axis_index("gy")
    ff = w_down.shape[1]
    odd_row = jnp.sum(jnp.where(slot_table % 2 == 1, slot_table // 2, 0))

    seg = lax.ppermute(segment_ids, "gy", [(i, SEQ_MAP[i]) for i in range(ROWS)]).reshape(ROWS, CH)
    seg_own = lax.dynamic_index_in_dim(seg, ix, 0, keepdims=False)
    starts = [jnp.sum(seg < s).astype(jnp.int32) for s in range(SEGS)]
    first = sum(jnp.where(seg_own == s, starts[s], 0) for s in range(SEGS))
    at_own = jnp.arange(CP, dtype=jnp.int32)
    position = (ix * CH + at_own - jnp.pad(first, (0, CP - CH))).astype(F32)
    frequency = THETA_BASE ** (-2.0 * jnp.arange(HALF, dtype=F32) / HD)
    angles = frequency[:, None] * position[None, :]
    cos_a = jnp.cos(angles)
    sin_a = jnp.sin(angles)
    query_docs = jnp.pad(seg_own, (0, CP - CH), constant_values=-1)
    biases = []
    flags = []
    for k in range(ROWS):
        seg_k = lax.dynamic_index_in_dim(seg, ix ^ k, 0, keepdims=False)
        key_docs = jnp.pad(seg_k, (0, CP - CH), constant_values=-2)
        allowed = (key_docs[:, None] == query_docs[None, :]) & (
            ((ix ^ k) * CH + at_own)[:, None] <= (ix * CH + at_own)[None, :]
        )
        biases.append(jnp.where(allowed, 0.0, NEGATIVE).astype(F32))
        flags.append(((ix ^ k) <= ix) & (seg_k[CH - 1] >= seg_own[0]))
    bias = jnp.stack(biases)
    idp = lax.axis_index("dp")
    at = jnp.stack([ix, iy, odd_row, idp]).astype(jnp.int32)
    sc = jnp.concatenate([at, jnp.stack(flags).astype(jnp.int32)])

    pieces = simple(
        split_kernel, "split", [sds((2 * FB, CP), BF)] * ROWS,
        tokens, cotangent, gain_attn[:, None], gain_mlp[:, None], scalars=at,
    )
    odd = jnp.concatenate([w_qkv[:, SLOT_W:], w_out[:, QW:]], axis=1)
    odd = jnp.where(ix == odd_row, odd, jnp.zeros_like(odd))
    quarter = row_scatter([lax.dynamic_slice(odd, (0, ODD * (ix ^ k)), (FB, ODD)) for k in range(ROWS)])
    w_pieces = [after(jnp.concatenate([w_qkv[:, :SLOT_W], w_out[:, :QW], quarter], axis=1), pieces[0])]
    toks = []
    for k in range(ROWS):
        toks.append(to_token(k, after(pieces[k], *w_pieces[1:])))
        if k < ROWS - 1:
            w_pieces.append(ring(after(w_pieces[-1], *toks[:k])))
    w_own = jnp.concatenate(w_pieces, axis=0)
    w_far = jnp.concatenate([swap(w, 2) for w in w_pieces], axis=0)
    w_rows = [w_own, swap(after(w_own, toks[2]), 1), w_far, swap(after(w_far, toks[2], toks[3]), 1)]
    w_gu = jnp.concatenate([w_gate_up[:, 0], w_gate_up[:, 1]], axis=1)
    halves = lax.axis_size("dp") == 2
    if halves:
        w_gu = lax.dynamic_slice(w_gu, ((FB - 128) * idp, 0), (128, 2 * ff))
    w_gu = [lax.all_gather(after(w_gu, *toks), "gy", axis=0, tiled=True)]
    if halves:
        w_gu.append(lax.ppermute(w_gu[0], "dp", [(0, 1), (1, 0)]))
    x, dy, n1, r1, gain_one, gain_two, w5, qs, kv = simple(
        qkv_kernel, "qkv",
        [
            sds((D, CP), BF), sds((D, CP), BF), sds((D, CP), BF), sds((1, CP), F32), sds((D, 1), F32), sds((D, 1), F32),
            sds((GROUPS, D, PACK), BF), sds((GROUPS, QW, CP), BF), sds((GROUPS, KV, CP), BF),
        ],
        *toks, *w_rows, cos_a, sin_a,
        scalars=at,
    )

    w_d = lax.all_gather(w_down, "gy", axis=0, tiled=True)

    kvs = row_gather(kv)
    dys = row_gather(after(dy, kvs[2]))
    o, lse, h, n2, r2 = grouped(
        attend_kernel, "attend",
        [per_group(QW, CP)] + kv_blocks()
        + [whole(ROWS, CP, CP), per_group(D, PACK), whole(D, CP), whole(D, 1)],
        [
            sds((GROUPS, QW, CP), BF), sds((GROUPS, 8, CP), F32), sds((D, CP), F32), sds((D, CP), BF),
            sds((1, CP), F32),
        ],
        [per_group(QW, CP), per_group(8, CP), whole(D, CP), whole(D, CP), whole(1, CP)],
        [pltpu.VMEM((8, CP), F32), pltpu.VMEM((8, CP), F32), pltpu.VMEM((QW, CP), F32)],
        sc, after(qs, w_gu[0]), *kvs, bias, w5, x, gain_two,
    )

    n2s = row_gather(n2)
    per_block = [sds((ff, CP), BF)] * 3 + [sds((D, CP), BF)] * 2
    def feed_forward(name, some_n2, some_dy):
        return simple(
            functools.partial(mlp_kernel, 2, halves), name, per_block * 2, *w_gu, w_d, *some_n2, *some_dy,
            scalars=at, scratch=[pltpu.VMEM((D, 2 * ff), BF)] if halves else [],
        )

    far = feed_forward("mlp_far", n2s[2:], dys[2:])
    near = feed_forward("mlp_near", [after(n2s[0], far[9]), n2s[1]], dys[:2])
    blocks = [near[:5], near[5:], far[:5], far[5:]]
    dn2_terms = list(row_near([b[4] for b in blocks]))
    mlp_terms = list(row_near([b[3] for b in blocks]))

    dn2_terms[2] = swap(dn2_terms[2], 2)
    wide = (3 * ff // 2 + 127) // 128 * 128
    g_mlp = simple(
        mlp_grad_kernel, "mlp_grad", [sds((D, wide), BF), sds((D, 3 * ff - wide), BF)],
        after(n2s[0], dn2_terms[2]), *n2s[1:], *dys,
        *[b[0] for b in blocks], *[b[1] for b in blocks], *[b[2] for b in blocks],
    )

    pack_a = sds((ROWS, AP, FB), BF)

    def beside_back(far, *operands):
        return swap(far, 2), grouped(
        attend_back_kernel, "attend_back",
        [per_group(QW, CP)] + kv_blocks()
        + [whole(ROWS, CP, CP), per_group(D, PACK), per_group(QW, CP), per_group(8, CP), whole(D, CP),
           whole(HALF, CP), whole(HALF, CP)]
        + [whole(D, CP)] * 4 + [whole(1, CP), whole(D, 1), whole(D, CP)],
        [sds((GROUPS, QW, CP), BF), sds((GROUPS, KV, CP), F32)] + [sds((GROUPS, KV, CP), BF)] * 3
        + [sds((D, CP), F32), sds((ROWS, 16, FB), F32)] + [pack_a] * ROWS,
        [per_group(QW, CP)] + kv_blocks() + [whole(D, CP), whole(ROWS, 16, FB)]
        + [whole(ROWS, AP, FB)] * ROWS,
        [pltpu.VMEM((D, CP), BF), pltpu.VMEM((QW, CP), BF), pltpu.VMEM((8, CP), F32), pltpu.VMEM((QW, CP), F32)],
            *operands,
        )

    mlp_terms[2] = after(mlp_terms[2], dn2_terms[2])
    dn2_terms[1] = after(dn2_terms[1], g_mlp[0], mlp_terms[2])
    mlp_terms[2], back = beside_back(
        mlp_terms[2],
        sc, qs, *kvs, bias, w5, o, lse, n1, cos_a, sin_a, *dn2_terms, h, r2, gain_two, dy,
    )
    dq, dkv, dh, gg, packs_a = back[0], list(back[1:5]), back[5], back[6], back[7:]
    g_mlp = [lax.psum_scatter(g, "gy", scatter_dimension=0, tiled=True) for g in g_mlp]
    dkv[2] = after(dkv[2], mlp_terms[2], g_mlp[0])
    dkv_terms = list(row_terms(dkv))
    a_terms = list(row_near(packs_a))
    a_terms[2] = after(a_terms[2], dkv_terms[2])
    dkv_terms[0] = after(dkv_terms[0], a_terms[2])
    a_terms[2] = swap(a_terms[2], 2)
    final = grouped(
        final_kernel, "final",
        [per_group(QW, CP)] + [per_group(KV, CP)] * 3
        + [per_group(D, PACK), whole(D, CP), whole(HALF, CP), whole(HALF, CP), whole(D, CP), whole(1, CP),
           whole(D, 1), whole(D, CP), whole(ROWS, 16, FB)] + [whole(D, CP)] * 4,
        [sds((ROWS, BP, FB), BF)] * ROWS + [sds((2 * FB, CP), BF)] * ROWS,
        [whole(ROWS, BP, FB)] * ROWS + [whole(2 * FB, CP)] * ROWS,
        [pltpu.VMEM((D, CP), F32), pltpu.VMEM((SLOT_W, CP), BF)] + [pltpu.VMEM((D, CP), BF)] * 2,
        sc, dq, *dkv_terms, w5, n1, cos_a, sin_a, x, r1, gain_one, dh, gg, h, *mlp_terms,
    )
    packs_b, out_pieces = final[:ROWS], final[ROWS:]
    back = to_features(out_pieces)
    layer_out, input_grad = simple(merge_kernel, "merge", [sds((FB, L), BF)] * 2, *back, scalars=at)

    g_mlp = jnp.concatenate([dp_sum(g) for g in g_mlp], axis=1)
    grad_down = g_mlp[:, 2 * ff :]
    a_terms[0] = after(a_terms[0], packs_b[0])
    g_a = (
        (a_terms[0].astype(F32) + a_terms[1].astype(F32)) + a_terms[2].astype(F32)
    ).astype(BF)
    packs_b = list(packs_b)
    packs_b[3] = after(packs_b[3], g_a)
    g_a = lax.psum_scatter(g_a.reshape(ROWS * AP, FB), "gy", scatter_dimension=0, tiled=True)
    g_b = row_scatter(packs_b).reshape(ROWS * BP, FB)
    g_b = lax.psum_scatter(g_b, "gy", scatter_dimension=0, tiled=True)
    g_all = dp_sum(after(jnp.concatenate([g_a, g_b], axis=0), *back))
    odds = jnp.concatenate([g_all[AW:AP], g_all[AP + KV : AP + KV + KV // ROWS]], axis=0)
    grad_qkv, grad_out, grad_gains = simple(
        grads_kernel, "grads",
        [sds((FB, 2 * SLOT_W), F32), sds((FB, 2 * QW), F32), sds((8, FB), F32)],
        g_all, *row_gather(odds), scalars=at,
        scratch=[pltpu.VMEM((AW, FB), F32), pltpu.VMEM((KV, FB), F32)],
    )
    grad_gate_up = jnp.stack([g_mlp[:, :ff], g_mlp[:, ff : 2 * ff]], axis=1)
    return (
        layer_out,
        input_grad,
        grad_qkv,
        grad_out,
        grad_gate_up,
        grad_down,
        grad_gains[0],
        grad_gains[1],
    )


def solution(mesh):
    placed = (
        P("gy", ("dp", "gx")),
        P(("dp", "gy"), None),
        P(),
        P("gy", "gx"),
        P("gy", "gx"),
        P("gy", None, "gx"),
        P("gy", "gx"),
        P("gy"),
        P("gy"),
        P("gy", ("dp", "gx")),
    )
    return jax.shard_map(
        per_device,
        mesh=mesh,
        in_specs=placed,
        out_specs=(
            P("gy", ("dp", "gx")),
            P("gy", ("dp", "gx")),
            P("gy", "gx"),
            P("gy", "gx"),
            P("gy", None, "gx"),
            P("gy", "gx"),
            P("gy"),
            P("gy"),
        ),
        check_vma=False,
    )
```

```python
import functools

import jax
import jax.numpy as jnp
from jax import lax
from jax.experimental import pallas as pl
from jax.experimental.pallas import tpu as pltpu
from jax.sharding import PartitionSpec as P

D = 960
HD = 64
QPK = 3
L = 1408
SEGS = 4
QW = QPK * HD
SLOT_W = QW + 2 * HD
PACK = SLOT_W + QW
GROUPS = 5
ROWS = 4
CH = L // ROWS
CP = 384
FB = D // ROWS
ODD = PACK // ROWS

EPSILON = 1e-05
THETA_BASE = 100000.0
NEGATIVE = -1e30
SEQ_MAP = (0, 2, 1, 3)
SEQ_BACK = (0, 2, 1, 3)
BF = jnp.bfloat16
F32 = jnp.float32
VMEM_LIMIT = 58 * 1024 * 1024
HALF = HD // 2
AW = 2 * QW
AP = AW + AW // ROWS
KV = 2 * HD
BP = KV + KV // ROWS + 16


def tn(a, b):
    return lax.dot_general(a, b, (((0,), (0,)), ((), ())), preferred_element_type=F32)


def nn(a, b):
    return lax.dot_general(a, b, (((1,), (0,)), ((), ())), preferred_element_type=F32)


def nt(a, b):
    return lax.dot_general(a, b, (((1,), (1,)), ((), ())), preferred_element_type=F32)


def rows_at(block, size=FB):
    return pl.ds(pl.multiple_of(block * FB, 16), size)


def rope(a, b, cos_a, sin_a):
    return a * cos_a - b * sin_a, b * cos_a + a * sin_a


def split_kernel(sc, t_ref, dy_ref, gain_one, gain_two, *outs):
    iy = sc[1]
    lane = lax.broadcasted_iota(jnp.int32, (FB, CP - CH), 1)
    tail = jnp.zeros((FB, CP - CH), F32)
    for i, gain in enumerate((gain_one, gain_two)):
        rest = gain[...]
        for part in range(3):
            piece = rest.astype(BF).astype(F32)
            rest = rest - piece
            tail = jnp.where(lane == 3 * i + part, piece, tail)
    tail = tail.astype(BF)
    blank = jnp.zeros((FB, CP - CH), BF)
    for q in range(ROWS):
        cols = slice(q * CH, (q + 1) * CH)
        block = jnp.concatenate([t_ref[:, cols], tail], axis=1)
        below = jnp.concatenate([dy_ref[:, cols], blank], axis=1)
        for k in range(ROWS):

            @pl.when((iy ^ k) == q)
            def _(k=k, block=block, below=below):
                outs[k][:FB] = block
                outs[k][FB:] = below


def merge_kernel(sc, *refs):
    iy = sc[1]
    for i in range(2):
        rows = slice(i * FB, (i + 1) * FB)
        parts = []
        for q in range(ROWS):
            value = refs[0][rows, :CH]
            for k in range(1, ROWS):
                value = jnp.where((iy ^ k) == q, refs[k][rows, :CH], value)
            parts.append(value)
        refs[ROWS + i][...] = jnp.concatenate(parts, axis=1)


def qkv_kernel(sc, *refs):
    toks = refs[:4]
    w_rows = refs[4:8]
    cos_ref, sin_ref = refs[8:10]
    x_ref, dy_ref, n1_ref, r1_ref, g1_ref, g2_ref, w5_ref, qs_ref, kv_ref = refs[10:]
    ix = sc[0]
    lane = lax.broadcasted_iota(jnp.int32, (FB, CP), 1)
    for k in range(ROWS):
        rows = rows_at(ix ^ k)
        piece = toks[k][:FB].astype(F32)
        dy_ref[rows] = toks[k][FB:]
        x_ref[rows] = jnp.where(lane < CH, piece, 0.0).astype(BF)
        for i, out in enumerate((g1_ref, g2_ref)):
            here = (lane >= CH + 3 * i) & (lane < CH + 3 * i + 3)
            out[rows] = jnp.sum(jnp.where(here, piece, 0.0), axis=1, keepdims=True)
    x = x_ref[...].astype(F32)
    r1 = lax.rsqrt(jnp.sum(x * x, axis=0, keepdims=True) / D + EPSILON)
    r1_ref[...] = r1
    n1_ref[...] = (x * r1 * g1_ref[...]).astype(BF)
    for k in range(ROWS):
        lanes = pl.ds(pl.multiple_of((ix ^ k) * ODD, ODD), ODD)
        for j in range(ROWS):
            rows = rows_at((sc[1] + ROWS - j) % ROWS)
            w5_ref[k, rows] = w_rows[k][j * FB : (j + 1) * FB, :PACK]
            w5_ref[GROUPS - 1, rows, lanes] = w_rows[k][j * FB : (j + 1) * FB, PACK:]
    cos_a = cos_ref[...]
    sin_a = sin_ref[...]
    for g in range(GROUPS):
        p = tn(w5_ref[g, :, :SLOT_W], n1_ref[...])
        for j in range(QPK + 1):
            first, second = rope(
                p[j * HD : j * HD + HALF], p[j * HD + HALF : (j + 1) * HD], cos_a, sin_a
            )
            first = first.astype(BF)
            second = second.astype(BF)
            if j < QPK:
                qs_ref[g, j * HD : j * HD + HALF] = (first.astype(F32) * HD**-0.5).astype(BF)
                qs_ref[g, j * HD + HALF : (j + 1) * HD] = (second.astype(F32) * HD**-0.5).astype(BF)
            else:
                kv_ref[g, :HALF] = first
                kv_ref[g, HALF:HD] = second
        kv_ref[g, HD:] = p[(QPK + 1) * HD :].astype(BF)


def attend_kernel(
    sc, qs_ref, kv0, kv1, kv2, kv3, bias_ref, w_ref, x_ref, gain_ref,
    o_ref, lse_ref, h_ref, n2_ref, r2_ref, m_s, l_s, acc_s,
):
    g = pl.program_id(0)
    kvs = (kv0, kv1, kv2, kv3)

    def fold(k, fresh):
        keys = kvs[k][0, :HD]
        values = kvs[k][0, HD:]
        bias = bias_ref[k]
        for j in range(QPK):
            s = tn(keys, qs_ref[0, j * HD : (j + 1) * HD]) + bias
            top = jnp.max(s, axis=0, keepdims=True)
            if fresh:
                m = top
                e = jnp.exp(s - m)
                l_s[j : j + 1] = jnp.sum(e, axis=0, keepdims=True)
                acc_s[j * HD : (j + 1) * HD] = nn(values, e.astype(BF))
            else:
                old = m_s[j : j + 1]
                m = jnp.maximum(old, top)
                fade = jnp.exp(old - m)
                e = jnp.exp(s - m)
                l_s[j : j + 1] = l_s[j : j + 1] * fade + jnp.sum(e, axis=0, keepdims=True)
                acc_s[j * HD : (j + 1) * HD] = acc_s[j * HD : (j + 1) * HD] * fade + nn(
                    values, e.astype(BF)
                )
            m_s[j : j + 1] = m

    fold(0, True)
    for k in range(1, ROWS):
        pl.when(sc[4 + k] != 0)(functools.partial(fold, k, False))
    for j in range(QPK):
        total = l_s[j : j + 1]
        o_ref[0, j * HD : (j + 1) * HD] = (acc_s[j * HD : (j + 1) * HD] / total).astype(BF)
        lse_ref[0, j : j + 1] = m_s[j : j + 1] + jnp.log(total)
    part = nn(w_ref[0, :, SLOT_W:], o_ref[0])

    @pl.when(g == 0)
    def _():
        h_ref[...] = x_ref[...].astype(F32) + part

    @pl.when(g != 0)
    def _():
        h_ref[...] += part

    @pl.when(g == GROUPS - 1)
    def _():
        h = h_ref[...]
        r2 = lax.rsqrt(jnp.sum(h * h, axis=0, keepdims=True) / D + EPSILON)
        r2_ref[...] = r2
        n2_ref[...] = (h * r2 * gain_ref[...]).astype(BF)


def row_sums(values):
    return lax.dot_general(
        jnp.ones((16, CP), F32), values, (((1,), (1,)), ((), ())),
        precision=lax.Precision.HIGHEST, preferred_element_type=F32,
    )


def attend_back_kernel(
    sc, qs_ref, kv0, kv1, kv2, kv3, bias_ref, w_ref, o_ref, lse_ref, n1_ref, cos_ref, sin_ref,
    dn_a, dn_b, dn_c, h_ref, r2_ref, gain_ref, dy_ref,
    dq_ref, d0, d1, d2, d3, dh_ref, gg_ref, pa0, pa1, pa2, pa3, datt_s, do_s, dl_s, dq_s,
):
    g = pl.program_id(0)
    kvs = (kv0, kv1, kv2, kv3)
    outs = (d0, d1, d2, d3)
    packs = (pa0, pa1, pa2, pa3)

    @pl.when(g == 0)
    def _():
        dn2 = dn_a[...].astype(F32) + dn_b[...].astype(F32) + dn_c[...].astype(F32)
        h = h_ref[...]
        r2 = r2_ref[...]
        weighted = dn2 * gain_ref[...]
        inner = jnp.sum(weighted * h, axis=0, keepdims=True)
        dh = dy_ref[...].astype(F32) + r2 * weighted - h * (r2 * r2 * r2 * inner / D)
        dh_ref[...] = dh
        datt_s[...] = dh.astype(BF)
        for b in range(ROWS):
            rows = slice(b * FB, (b + 1) * FB)
            gg_ref[b] = row_sums(dn2[rows] * h[rows] * r2)

    do_s[...] = tn(w_ref[0, :, SLOT_W:], datt_s[...]).astype(BF)
    for j in range(QPK):
        rows = slice(j * HD, (j + 1) * HD)
        dl_s[j : j + 1] = jnp.sum(
            do_s[rows].astype(F32) * o_ref[0, rows].astype(F32), axis=0, keepdims=True
        )

    def fold(k, fresh):
        keys = kvs[k][0, :HD]
        values = kvs[k][0, HD:]
        bias = bias_ref[k]
        dk = jnp.zeros((HD, CP), F32)
        dv = jnp.zeros((HD, CP), F32)
        for j in range(QPK):
            rows = slice(j * HD, (j + 1) * HD)
            s = tn(keys, qs_ref[0, rows]) + bias
            p = jnp.exp(s - lse_ref[0, j : j + 1])
            do_j = do_s[rows]
            dp = tn(values, do_j)
            ds = (p * (dp - dl_s[j : j + 1])).astype(BF)
            dv = dv + nt(do_j, p.astype(BF))
            dk = dk + nt(qs_ref[0, rows], ds)
            dq = nn(keys, ds)
            if fresh:
                dq_s[rows] = dq
            else:
                dq_s[rows] += dq
        outs[k][0, :HD] = dk.astype(outs[k].dtype)
        outs[k][0, HD:] = dv.astype(outs[k].dtype)

    fold(0, True)
    for k in range(1, ROWS):
        pl.when(sc[4 + k] != 0)(functools.partial(fold, k, False))

        @pl.when(sc[4 + k] == 0)
        def _(k=k):
            outs[k][...] = jnp.zeros(outs[k].shape, outs[k].dtype)

    cos_a = cos_ref[...]
    sin_a = sin_ref[...]
    for j in range(QPK):
        first, second = rope(
            dq_s[j * HD : j * HD + HALF] * HD**-0.5,
            dq_s[j * HD + HALF : (j + 1) * HD] * HD**-0.5,
            cos_a, -sin_a,
        )
        dq_ref[0, j * HD : j * HD + HALF] = first.astype(BF)
        dq_ref[0, j * HD + HALF : (j + 1) * HD] = second.astype(BF)

    for b in range(ROWS):
        rows = slice(b * FB, (b + 1) * FB)
        block = jnp.concatenate(
            [nt(dq_ref[0], n1_ref[rows]).astype(BF), nt(o_ref[0], datt_s[rows]).astype(BF)], axis=0
        )
        for k in range(ROWS):

            @pl.when(g == k)
            def _(k=k, block=block, b=b):
                packs[k][b, :AW] = block

        @pl.when(g == GROUPS - 1)
        def _(block=block, b=b):
            for k in range(ROWS):
                share = AW // ROWS
                for q in range(ROWS):

                    @pl.when((sc[0] ^ k) == q)
                    def _(k=k, q=q):
                        packs[k][b, AW:] = block[q * share : (q + 1) * share]


def final_kernel(
    sc, dq_ref, d0, d1, d2, w_ref, n1_ref, cos_ref, sin_ref, x_ref, r1_ref, gain_ref, dh_ref, gg_ref,
    h_ref, mlp_a, mlp_b, mlp_c,
    pb0, pb1, pb2, pb3, out0, out1, out2, out3, dn_s, dpg_s, dx_s, lo_s,
):
    g = pl.program_id(0)
    packs = (pb0, pb1, pb2, pb3)
    outs = (out0, out1, out2, out3)
    dkv = d0[0] + d1[0].astype(F32) + d2[0].astype(F32)
    first, second = rope(dkv[:HALF], dkv[HALF:HD], cos_ref[...], -sin_ref[...])
    dpg_s[:QW] = dq_ref[0]
    dpg_s[QW : QW + HALF] = first.astype(BF)
    dpg_s[QW + HALF : QW + HD] = second.astype(BF)
    dpg_s[QW + HD :] = dkv[HD:].astype(BF)
    part = nn(w_ref[0, :, :SLOT_W], dpg_s[...])

    @pl.when(g == 0)
    def _():
        dn_s[...] = part

    @pl.when(g != 0)
    def _():
        dn_s[...] += part

    for b in range(ROWS):
        block = nt(dpg_s[QW:], n1_ref[b * FB : (b + 1) * FB]).astype(BF)
        for k in range(ROWS):

            @pl.when(g == k)
            def _(k=k, block=block, b=b):
                packs[k][b, :KV] = block

        @pl.when(g == GROUPS - 1)
        def _(block=block, b=b):
            share = KV // ROWS
            for k in range(ROWS):
                for q in range(ROWS):

                    @pl.when((sc[0] ^ k) == q)
                    def _(k=k, q=q):
                        packs[k][b, KV : KV + share] = block[q * share : (q + 1) * share]

    @pl.when(g == GROUPS - 1)
    def _():
        dn1 = dn_s[...]
        x = x_ref[...].astype(F32)
        r1 = r1_ref[...]
        weighted = dn1 * gain_ref[...]
        inner = jnp.sum(weighted * x, axis=0, keepdims=True)
        dx = dh_ref[...] + r1 * weighted - x * (r1 * r1 * r1 * inner / D)
        dx_s[...] = dx.astype(BF)
        row = lax.broadcasted_iota(jnp.int32, (16, FB), 0)
        for b in range(ROWS):
            rows = slice(b * FB, (b + 1) * FB)
            sums = row_sums(dn1[rows] * x[rows] * r1)
            sums = jnp.where(row == 0, sums, jnp.where(row == 1, gg_ref[b], 0.0)).astype(BF)
            for k in range(ROWS):
                packs[k][b, KV + KV // ROWS :] = sums
        lo_s[...] = (
            h_ref[...] + mlp_a[...].astype(F32) + mlp_b[...].astype(F32) + mlp_c[...].astype(F32)
        ).astype(BF)
        for k in range(ROWS):
            outs[k][:FB] = lo_s[rows_at(sc[0] ^ k)]
            outs[k][FB:] = dx_s[rows_at(sc[0] ^ k)]


def mlp_kernel(count, halves, sc, *refs):
    if halves:
        w = refs[-1]
        part = refs[0].shape[0] // ROWS
        wd = refs[3]
        width = wd.shape[1]
        for b in range(ROWS):
            rows = slice(b * part, (b + 1) * part)
            mine = pl.ds(pl.multiple_of(b * FB + (FB - part) * sc[3], 16), part)
            theirs = pl.ds(pl.multiple_of(b * FB + (FB - part) * (1 - sc[3]), 16), part)
            w[mine] = refs[0][rows]
            w[theirs, :width] = refs[1][rows]
            w[theirs, width:] = refs[2][rows]
        refs = refs[4:-1]
    else:
        w, wd = refs[:2]
        refs = refs[2:]
    width = wd.shape[1]
    for i in range(count):
        n2 = refs[i]
        dy = refs[count + i]
        a_ref, dg_ref, du_ref, mlp_ref, dn_ref = refs[2 * count + 5 * i : 2 * count + 5 * i + 5]
        step = width
        for f in range(0, width, step):
            cols = slice(f, f + step)
            gate = tn(w[:, f : f + step], n2[...])
            up = tn(w[:, width + f : width + f + step], n2[...])
            da = tn(wd[:, cols], dy[...])
            sigma = jax.nn.sigmoid(gate)
            silu = gate * sigma
            a_ref[cols] = (silu * up).astype(BF)
            dg_ref[cols] = (da * up * sigma * (1.0 + gate * (1.0 - sigma))).astype(BF)
            du_ref[cols] = (da * silu).astype(BF)
        dn_ref[...] = (nn(w[:, :width], dg_ref[...]) + nn(w[:, width : 2 * width], du_ref[...])).astype(BF)
        mlp_ref[...] = nn(wd[...], a_ref[...]).astype(BF)


def mlp_grad_kernel(*refs):
    n2s, dys, acts, gates, ups = (refs[ROWS * i : ROWS * (i + 1)] for i in range(5))
    outs = refs[-2:]
    width = acts[0].shape[0]
    edge = outs[0].shape[1]
    for part, (left, right) in enumerate(((n2s, gates), (n2s, ups), (dys, acts))):
        begin = part * width
        cuts = [begin] + ([edge] if begin < edge < begin + width else []) + [begin + width]
        for low, high in zip(cuts[:-1], cuts[1:]):
            total = nt(left[0][...], right[0][low - begin : high - begin])
            for k in range(1, ROWS):
                total = total + nt(left[k][...], right[k][low - begin : high - begin])
            outs[low // edge][:, low % edge : low % edge + high - low] = total.astype(BF)


def grads_kernel(sc, g_ref, o0, o1, o2, o3, qkv_ref, out_ref, gains_ref, oa_s, ob_s):
    ix = sc[0]
    share_a = AW // ROWS
    share_b = KV // ROWS
    for k, odd in enumerate((o0, o1, o2, o3)):
        oa_s[pl.ds(pl.multiple_of((ix ^ k) * share_a, 8), share_a)] = odd[:share_a]
        ob_s[pl.ds(pl.multiple_of((ix ^ k) * share_b, 8), share_b)] = odd[share_a:]
    live = (ix == sc[2]).astype(F32)
    oa = oa_s[...] * live
    ob = ob_s[...] * live
    qkv_ref[...] = jnp.transpose(
        jnp.concatenate([g_ref[:QW], g_ref[AP : AP + KV], oa[:QW], ob], axis=0)
    )
    out_ref[...] = jnp.transpose(jnp.concatenate([g_ref[QW:AW], oa[QW:]], axis=0))
    gains_ref[...] = g_ref[AP + KV + share_b : AP + KV + share_b + 8]


def whole(*shape):
    return pl.BlockSpec(shape, lambda *_: (0,) * len(shape))


def per_group(*shape):
    return pl.BlockSpec((1,) + shape, lambda g, *_: (g,) + (0,) * len(shape))


def kv_blocks():
    def spec(k):
        return pl.BlockSpec((1, KV, CP), lambda g, *_: (jnp.where(g < ROWS, g ^ k, g), 0, 0))

    return [spec(k) for k in range(ROWS)]


def sds(shape, dtype):
    return jax.ShapeDtypeStruct(shape, dtype)


MICROSECONDS = {
    "split": 5, "qkv": 7, "attend": 18, "mlp_near": 13, "mlp_far": 13,
    "mlp_grad": 18, "attend_back": 30, "final": 19, "merge": 2, "grads": 3,
}


def cost(name):
    return pl.CostEstimate(
        flops=MICROSECONDS[name] * 100 * 10**6, bytes_accessed=MICROSECONDS[name] * 3000 * 100, transcendentals=0
    )


def simple(kernel, name, outs, *operands, scalars=None, scratch=(), limit=VMEM_LIMIT):
    specs = [pl.BlockSpec(memory_space=pltpu.VMEM)] * len(operands)
    if scalars is not None:
        specs = [pl.BlockSpec(memory_space=pltpu.SMEM)] + specs
        operands = (scalars,) + operands
    return pl.pallas_call(
        kernel,
        in_specs=specs,
        out_specs=[pl.BlockSpec(memory_space=pltpu.VMEM)] * len(outs),
        out_shape=list(outs),
        scratch_shapes=list(scratch),
        compiler_params=pltpu.CompilerParams(vmem_limit_bytes=limit),
        cost_estimate=cost(name),
        name=name,
    )(*operands)


def grouped(kernel, name, in_specs, outs, out_specs, scratch, sc, *operands):
    return pl.pallas_call(
        kernel,
        grid_spec=pltpu.PrefetchScalarGridSpec(
            num_scalar_prefetch=1,
            grid=(GROUPS,),
            in_specs=in_specs,
            out_specs=out_specs,
            scratch_shapes=scratch,
        ),
        out_shape=outs,
        compiler_params=pltpu.CompilerParams(vmem_limit_bytes=VMEM_LIMIT),
        cost_estimate=cost(name),
        name=name,
    )(sc, *operands)


def swap(values, bit):
    return lax.ppermute(values, "gx", [(i, i ^ bit) for i in range(ROWS)])


def row_gather(own):
    far = swap(own, 2)
    mate = swap(own, 1)
    return own, mate, far, swap(far, 1)


def after(values, *first):
    return lax.optimization_barrier((values,) + first)[0]


def row_near(blocks):
    far = (blocks[2].astype(F32) + swap(blocks[3], 1).astype(F32)).astype(BF)
    return blocks[0], swap(blocks[1], 1), far


def row_terms(blocks, first=()):
    a, b, far = row_near(blocks)
    if first:
        far = after(far, *first)
    return a, b, swap(far, 2)


def row_scatter(blocks, first=()):
    a, b, c = row_terms(blocks, first)
    return (a.astype(F32) + b.astype(F32) + c.astype(F32)).astype(BF)


def ring(values):
    return lax.ppermute(values, "gy", [(i, (i + 1) % ROWS) for i in range(ROWS)])


def ring_scatter(blocks, iy):
    def take(at):
        return lax.dynamic_index_in_dim(blocks, at % ROWS, 0, keepdims=False)

    moving = take(iy + 3)
    for s in range(ROWS - 1):
        moving = (ring(moving).astype(F32) + take(iy + 2 - s).astype(F32)).astype(BF)
    return moving


def dp_sum(values):
    if lax.axis_size("dp") == 2:
        return values.astype(F32) + lax.ppermute(values, "dp", [(0, 1), (1, 0)]).astype(F32)
    return lax.psum(values, "dp").astype(F32)


def to_token(k, piece):
    pairs = [(a * ROWS + b, (b ^ k) * ROWS + SEQ_MAP[a]) for a in range(ROWS) for b in range(ROWS)]
    return lax.ppermute(piece, ("gx", "gy"), pairs)


def to_features(pieces):
    back = []
    for k in range(ROWS):
        pairs = [(a * ROWS + b, SEQ_BACK[b] * ROWS + (a ^ k)) for a in range(ROWS) for b in range(ROWS)]
        back.append(lax.ppermute(pieces[k], ("gx", "gy"), pairs))
    return back


def per_device(
    tokens, segment_ids, slot_table, w_qkv, w_out, w_gate_up, w_down, gain_attn, gain_mlp, cotangent
):
    ix = lax.axis_index("gx")
    iy = lax.axis_index("gy")
    ff = w_down.shape[1]
    odd_row = jnp.sum(jnp.where(slot_table % 2 == 1, slot_table // 2, 0))

    seg = lax.ppermute(segment_ids, "gy", [(i, SEQ_MAP[i]) for i in range(ROWS)]).reshape(ROWS, CH)
    seg_own = lax.dynamic_index_in_dim(seg, ix, 0, keepdims=False)
    starts = [jnp.sum(seg < s).astype(jnp.int32) for s in range(SEGS)]
    first = sum(jnp.where(seg_own == s, starts[s], 0) for s in range(SEGS))
    at_own = jnp.arange(CP, dtype=jnp.int32)
    position = (ix * CH + at_own - jnp.pad(first, (0, CP - CH))).astype(F32)
    frequency = THETA_BASE ** (-2.0 * jnp.arange(HALF, dtype=F32) / HD)
    angles = frequency[:, None] * position[None, :]
    cos_a = jnp.cos(angles)
    sin_a = jnp.sin(angles)
    query_docs = jnp.pad(seg_own, (0, CP - CH), constant_values=-1)
    biases = []
    flags = []
    for k in range(ROWS):
        seg_k = lax.dynamic_index_in_dim(seg, ix ^ k, 0, keepdims=False)
        key_docs = jnp.pad(seg_k, (0, CP - CH), constant_values=-2)
        allowed = (key_docs[:, None] == query_docs[None, :]) & (
            ((ix ^ k) * CH + at_own)[:, None] <= (ix * CH + at_own)[None, :]
        )
        biases.append(jnp.where(allowed, 0.0, NEGATIVE).astype(F32))
        flags.append(((ix ^ k) <= ix) & (seg_k[CH - 1] >= seg_own[0]))
    bias = jnp.stack(biases)
    idp = lax.axis_index("dp")
    at = jnp.stack([ix, iy, odd_row, idp]).astype(jnp.int32)
    sc = jnp.concatenate([at, jnp.stack(flags).astype(jnp.int32)])

    pieces = simple(
        split_kernel, "split", [sds((2 * FB, CP), BF)] * ROWS,
        tokens, cotangent, gain_attn[:, None], gain_mlp[:, None], scalars=at,
    )
    odd = jnp.concatenate([w_qkv[:, SLOT_W:], w_out[:, QW:]], axis=1)
    odd = jnp.where(ix == odd_row, odd, jnp.zeros_like(odd))
    quarter = row_scatter([lax.dynamic_slice(odd, (0, ODD * (ix ^ k)), (FB, ODD)) for k in range(ROWS)])
    w_pieces = [after(jnp.concatenate([w_qkv[:, :SLOT_W], w_out[:, :QW], quarter], axis=1), pieces[0])]
    toks = []
    for k in range(ROWS):
        toks.append(to_token(k, after(pieces[k], *w_pieces[1:])))
        if k < ROWS - 1:
            w_pieces.append(ring(after(w_pieces[-1], *toks[:k])))
    w_own = jnp.concatenate(w_pieces, axis=0)
    w_far = jnp.concatenate([swap(w, 2) for w in w_pieces], axis=0)
    w_rows = [w_own, swap(after(w_own, toks[2]), 1), w_far, swap(after(w_far, toks[2], toks[3]), 1)]
    w_gu = jnp.concatenate([w_gate_up[:, 0], w_gate_up[:, 1]], axis=1)
    halves = lax.axis_size("dp") == 2
    if halves:
        w_gu = lax.dynamic_slice(w_gu, ((FB - 128) * idp, 0), (128, 2 * ff))
    w_gu = [lax.all_gather(after(w_gu, *toks), "gy", axis=0, tiled=True)]
    if halves:
        w_gu += [lax.ppermute(w_gu[0][:, at : at + ff], "dp", [(0, 1), (1, 0)]) for at in (0, ff)]
    x, dy, n1, r1, gain_one, gain_two, w5, qs, kv = simple(
        qkv_kernel, "qkv",
        [
            sds((D, CP), BF), sds((D, CP), BF), sds((D, CP), BF), sds((1, CP), F32), sds((D, 1), F32), sds((D, 1), F32),
            sds((GROUPS, D, PACK), BF), sds((GROUPS, QW, CP), BF), sds((GROUPS, KV, CP), BF),
        ],
        *toks, *w_rows, cos_a, sin_a,
        scalars=at,
    )

    w_d = lax.all_gather(w_down, "gy", axis=0, tiled=True)

    kvs = row_gather(kv)
    dys = row_gather(after(dy, kvs[2]))
    o, lse, h, n2, r2 = grouped(
        attend_kernel, "attend",
        [per_group(QW, CP)] + kv_blocks()
        + [whole(ROWS, CP, CP), per_group(D, PACK), whole(D, CP), whole(D, 1)],
        [
            sds((GROUPS, QW, CP), BF), sds((GROUPS, 8, CP), F32), sds((D, CP), F32), sds((D, CP), BF),
            sds((1, CP), F32),
        ],
        [per_group(QW, CP), per_group(8, CP), whole(D, CP), whole(D, CP), whole(1, CP)],
        [pltpu.VMEM((8, CP), F32), pltpu.VMEM((8, CP), F32), pltpu.VMEM((QW, CP), F32)],
        sc, after(qs, *w_gu[:2]), *kvs, bias, w5, x, gain_two,
    )

    n2s = row_gather(n2)
    per_block = [sds((ff, CP), BF)] * 3 + [sds((D, CP), BF)] * 2
    def feed_forward(name, some_n2, some_dy):
        return simple(
            functools.partial(mlp_kernel, 2, halves), name, per_block * 2, *w_gu, w_d, *some_n2, *some_dy,
            scalars=at, scratch=[pltpu.VMEM((D, 2 * ff), BF)] if halves else [],
        )

    far = feed_forward("mlp_far", n2s[2:], dys[2:])
    near = feed_forward("mlp_near", [after(n2s[0], far[9]), n2s[1]], dys[:2])
    blocks = [near[:5], near[5:], far[:5], far[5:]]
    dn2_terms = list(row_near([b[4] for b in blocks]))
    mlp_terms = list(row_near([b[3] for b in blocks]))

    dn2_terms[2] = swap(dn2_terms[2], 2)
    wide = (3 * ff // 2 + 127) // 128 * 128
    g_mlp = simple(
        mlp_grad_kernel, "mlp_grad", [sds((D, wide), BF), sds((D, 3 * ff - wide), BF)],
        after(n2s[0], dn2_terms[2]), *n2s[1:], *dys,
        *[b[0] for b in blocks], *[b[1] for b in blocks], *[b[2] for b in blocks],
    )

    pack_a = sds((ROWS, AP, FB), BF)

    def beside_back(far, *operands):
        return swap(far, 2), grouped(
        attend_back_kernel, "attend_back",
        [per_group(QW, CP)] + kv_blocks()
        + [whole(ROWS, CP, CP), per_group(D, PACK), per_group(QW, CP), per_group(8, CP), whole(D, CP),
           whole(HALF, CP), whole(HALF, CP)]
        + [whole(D, CP)] * 4 + [whole(1, CP), whole(D, 1), whole(D, CP)],
        [sds((GROUPS, QW, CP), BF), sds((GROUPS, KV, CP), F32)] + [sds((GROUPS, KV, CP), BF)] * 3
        + [sds((D, CP), F32), sds((ROWS, 16, FB), F32)] + [pack_a] * ROWS,
        [per_group(QW, CP)] + kv_blocks() + [whole(D, CP), whole(ROWS, 16, FB)]
        + [whole(ROWS, AP, FB)] * ROWS,
        [pltpu.VMEM((D, CP), BF), pltpu.VMEM((QW, CP), BF), pltpu.VMEM((8, CP), F32), pltpu.VMEM((QW, CP), F32)],
            *operands,
        )

    mlp_terms[2] = after(mlp_terms[2], dn2_terms[2])
    dn2_terms[1] = after(dn2_terms[1], g_mlp[0], mlp_terms[2])
    mlp_terms[2], back = beside_back(
        mlp_terms[2],
        sc, qs, *kvs, bias, w5, o, lse, n1, cos_a, sin_a, *dn2_terms, h, r2, gain_two, dy,
    )
    dq, dkv, dh, gg, packs_a = back[0], list(back[1:5]), back[5], back[6], back[7:]
    g_mlp = [lax.psum_scatter(g, "gy", scatter_dimension=0, tiled=True) for g in g_mlp]
    dkv[2] = after(dkv[2], mlp_terms[2], g_mlp[0])
    dkv_terms = list(row_terms(dkv))
    a_terms = list(row_near(packs_a))
    a_terms[2] = after(a_terms[2], dkv_terms[2])
    dkv_terms[0] = after(dkv_terms[0], a_terms[2])
    a_terms[2] = swap(a_terms[2], 2)
    final = grouped(
        final_kernel, "final",
        [per_group(QW, CP)] + [per_group(KV, CP)] * 3
        + [per_group(D, PACK), whole(D, CP), whole(HALF, CP), whole(HALF, CP), whole(D, CP), whole(1, CP),
           whole(D, 1), whole(D, CP), whole(ROWS, 16, FB)] + [whole(D, CP)] * 4,
        [sds((ROWS, BP, FB), BF)] * ROWS + [sds((2 * FB, CP), BF)] * ROWS,
        [whole(ROWS, BP, FB)] * ROWS + [whole(2 * FB, CP)] * ROWS,
        [pltpu.VMEM((D, CP), F32), pltpu.VMEM((SLOT_W, CP), BF)] + [pltpu.VMEM((D, CP), BF)] * 2,
        sc, dq, *dkv_terms, w5, n1, cos_a, sin_a, x, r1, gain_one, dh, gg, h, *mlp_terms,
    )
    packs_b, out_pieces = final[:ROWS], final[ROWS:]
    back = to_features(out_pieces)
    layer_out, input_grad = simple(merge_kernel, "merge", [sds((FB, L), BF)] * 2, *back, scalars=at)

    g_mlp = jnp.concatenate([dp_sum(g) for g in g_mlp], axis=1)
    grad_down = g_mlp[:, 2 * ff :]
    a_terms[0] = after(a_terms[0], packs_b[0])
    g_a = (
        (a_terms[0].astype(F32) + a_terms[1].astype(F32)) + a_terms[2].astype(F32)
    ).astype(BF)
    packs_b = list(packs_b)
    packs_b[3] = after(packs_b[3], g_a)
    g_all = jnp.concatenate([g_a, row_scatter(packs_b)], axis=1).reshape(ROWS * (AP + BP), FB)
    g_all = lax.psum_scatter(g_all, "gy", scatter_dimension=0, tiled=True)
    g_all = dp_sum(after(g_all, *back))
    odds = jnp.concatenate([g_all[AW:AP], g_all[AP + KV : AP + KV + KV // ROWS]], axis=0)
    grad_qkv, grad_out, grad_gains = simple(
        grads_kernel, "grads",
        [sds((FB, 2 * SLOT_W), F32), sds((FB, 2 * QW), F32), sds((8, FB), F32)],
        g_all, *row_gather(odds), scalars=at,
        scratch=[pltpu.VMEM((AW, FB), F32), pltpu.VMEM((KV, FB), F32)],
    )
    grad_gate_up = jnp.stack([g_mlp[:, :ff], g_mlp[:, ff : 2 * ff]], axis=1)
    return (
        layer_out,
        input_grad,
        grad_qkv,
        grad_out,
        grad_gate_up,
        grad_down,
        grad_gains[0],
        grad_gains[1],
    )


def solution(mesh):
    placed = (
        P("gy", ("dp", "gx")),
        P(("dp", "gy"), None),
        P(),
        P("gy", "gx"),
        P("gy", "gx"),
        P("gy", None, "gx"),
        P("gy", "gx"),
        P("gy"),
        P("gy"),
        P("gy", ("dp", "gx")),
    )
    return jax.shard_map(
        per_device,
        mesh=mesh,
        in_specs=placed,
        out_specs=(
            P("gy", ("dp", "gx")),
            P("gy", ("dp", "gx")),
            P("gy", "gx"),
            P("gy", "gx"),
            P("gy", None, "gx"),
            P("gy", "gx"),
            P("gy"),
            P("gy"),
        ),
        check_vma=False,
    )
```

```python
import functools

import jax
import jax.numpy as jnp
from jax import lax
from jax.experimental import pallas as pl
from jax.experimental.pallas import tpu as pltpu
from jax.sharding import PartitionSpec as P

D = 960
HD = 64
QPK = 3
L = 1408
SEGS = 4
QW = QPK * HD
SLOT_W = QW + 2 * HD
PACK = SLOT_W + QW
GROUPS = 5
ROWS = 4
CH = L // ROWS
CP = 384
FB = D // ROWS
ODD = PACK // ROWS

EPSILON = 1e-05
THETA_BASE = 100000.0
NEGATIVE = -1e30
SEQ_MAP = (0, 2, 1, 3)
SEQ_BACK = (0, 2, 1, 3)
BF = jnp.bfloat16
F32 = jnp.float32
VMEM_LIMIT = 58 * 1024 * 1024
HALF = HD // 2
AW = 2 * QW
AP = AW + AW // ROWS
KV = 2 * HD
BP = KV + KV // ROWS + 16


def tn(a, b):
    return lax.dot_general(a, b, (((0,), (0,)), ((), ())), preferred_element_type=F32)


def nn(a, b):
    return lax.dot_general(a, b, (((1,), (0,)), ((), ())), preferred_element_type=F32)


def nt(a, b):
    return lax.dot_general(a, b, (((1,), (1,)), ((), ())), preferred_element_type=F32)


def rows_at(block, size=FB):
    return pl.ds(pl.multiple_of(block * FB, 16), size)


def rope(a, b, cos_a, sin_a):
    return a * cos_a - b * sin_a, b * cos_a + a * sin_a


def split_kernel(sc, t_ref, dy_ref, gain_one, gain_two, *outs):
    iy = sc[1]
    lane = lax.broadcasted_iota(jnp.int32, (FB, CP - CH), 1)
    tail = jnp.zeros((FB, CP - CH), F32)
    for i, gain in enumerate((gain_one, gain_two)):
        rest = gain[...]
        for part in range(3):
            piece = rest.astype(BF).astype(F32)
            rest = rest - piece
            tail = jnp.where(lane == 3 * i + part, piece, tail)
    tail = tail.astype(BF)
    blank = jnp.zeros((FB, CP - CH), BF)
    for q in range(ROWS):
        cols = slice(q * CH, (q + 1) * CH)
        block = jnp.concatenate([t_ref[:, cols], tail], axis=1)
        below = jnp.concatenate([dy_ref[:, cols], blank], axis=1)
        for k in range(ROWS):

            @pl.when((iy ^ k) == q)
            def _(k=k, block=block, below=below):
                outs[k][:FB] = block
                outs[k][FB:] = below


def merge_kernel(sc, *refs):
    iy = sc[1]
    for i in range(2):
        rows = slice(i * FB, (i + 1) * FB)
        parts = []
        for q in range(ROWS):
            value = refs[0][rows, :CH]
            for k in range(1, ROWS):
                value = jnp.where((iy ^ k) == q, refs[k][rows, :CH], value)
            parts.append(value)
        refs[ROWS + i][...] = jnp.concatenate(parts, axis=1)


def qkv_kernel(sc, *refs):
    toks = refs[:4]
    w_rows = refs[4:8]
    cos_ref, sin_ref = refs[8:10]
    x_ref, dy_ref, n1_ref, r1_ref, g1_ref, g2_ref, w5_ref, qs_ref, kv_ref = refs[10:]
    ix = sc[0]
    lane = lax.broadcasted_iota(jnp.int32, (FB, CP), 1)
    for k in range(ROWS):
        rows = rows_at(ix ^ k)
        piece = toks[k][:FB].astype(F32)
        dy_ref[rows] = toks[k][FB:]
        x_ref[rows] = jnp.where(lane < CH, piece, 0.0).astype(BF)
        for i, out in enumerate((g1_ref, g2_ref)):
            here = (lane >= CH + 3 * i) & (lane < CH + 3 * i + 3)
            out[rows] = jnp.sum(jnp.where(here, piece, 0.0), axis=1, keepdims=True)
    x = x_ref[...].astype(F32)
    r1 = lax.rsqrt(jnp.sum(x * x, axis=0, keepdims=True) / D + EPSILON)
    r1_ref[...] = r1
    n1_ref[...] = (x * r1 * g1_ref[...]).astype(BF)
    for k in range(ROWS):
        lanes = pl.ds(pl.multiple_of((ix ^ k) * ODD, ODD), ODD)
        for j in range(ROWS):
            rows = rows_at((sc[1] + ROWS - j) % ROWS)
            w5_ref[k, rows] = w_rows[k][j * FB : (j + 1) * FB, :PACK]
            w5_ref[GROUPS - 1, rows, lanes] = w_rows[k][j * FB : (j + 1) * FB, PACK:]
    cos_a = cos_ref[...]
    sin_a = sin_ref[...]
    for g in range(GROUPS):
        p = tn(w5_ref[g, :, :SLOT_W], n1_ref[...])
        for j in range(QPK + 1):
            first, second = rope(
                p[j * HD : j * HD + HALF], p[j * HD + HALF : (j + 1) * HD], cos_a, sin_a
            )
            first = first.astype(BF)
            second = second.astype(BF)
            if j < QPK:
                qs_ref[g, j * HD : j * HD + HALF] = (first.astype(F32) * HD**-0.5).astype(BF)
                qs_ref[g, j * HD + HALF : (j + 1) * HD] = (second.astype(F32) * HD**-0.5).astype(BF)
            else:
                kv_ref[g, :HALF] = first
                kv_ref[g, HALF:HD] = second
        kv_ref[g, HD:] = p[(QPK + 1) * HD :].astype(BF)


def attend_kernel(
    sc, qs_ref, kv0, kv1, kv2, kv3, bias_ref, w_ref, x_ref, gain_ref,
    o_ref, lse_ref, h_ref, n2_ref, r2_ref, m_s, l_s, acc_s,
):
    g = pl.program_id(0)
    kvs = (kv0, kv1, kv2, kv3)

    def fold(k, fresh):
        keys = kvs[k][0, :HD]
        values = kvs[k][0, HD:]
        bias = bias_ref[k]
        for j in range(QPK):
            s = tn(keys, qs_ref[0, j * HD : (j + 1) * HD]) + bias
            top = jnp.max(s, axis=0, keepdims=True)
            if fresh:
                m = top
                e = jnp.exp(s - m)
                l_s[j : j + 1] = jnp.sum(e, axis=0, keepdims=True)
                acc_s[j * HD : (j + 1) * HD] = nn(values, e.astype(BF))
            else:
                old = m_s[j : j + 1]
                m = jnp.maximum(old, top)
                fade = jnp.exp(old - m)
                e = jnp.exp(s - m)
                l_s[j : j + 1] = l_s[j : j + 1] * fade + jnp.sum(e, axis=0, keepdims=True)
                acc_s[j * HD : (j + 1) * HD] = acc_s[j * HD : (j + 1) * HD] * fade + nn(
                    values, e.astype(BF)
                )
            m_s[j : j + 1] = m

    fold(0, True)
    for k in range(1, ROWS):
        pl.when(sc[4 + k] != 0)(functools.partial(fold, k, False))
    for j in range(QPK):
        total = l_s[j : j + 1]
        o_ref[0, j * HD : (j + 1) * HD] = (acc_s[j * HD : (j + 1) * HD] / total).astype(BF)
        lse_ref[0, j : j + 1] = m_s[j : j + 1] + jnp.log(total)
    part = nn(w_ref[0, :, SLOT_W:], o_ref[0])

    @pl.when(g == 0)
    def _():
        h_ref[...] = x_ref[...].astype(F32) + part

    @pl.when(g != 0)
    def _():
        h_ref[...] += part

    @pl.when(g == GROUPS - 1)
    def _():
        h = h_ref[...]
        r2 = lax.rsqrt(jnp.sum(h * h, axis=0, keepdims=True) / D + EPSILON)
        r2_ref[...] = r2
        n2_ref[...] = (h * r2 * gain_ref[...]).astype(BF)


def row_sums(values):
    return lax.dot_general(
        jnp.ones((16, CP), F32), values, (((1,), (1,)), ((), ())),
        precision=lax.Precision.HIGHEST, preferred_element_type=F32,
    )


def attend_back_kernel(
    sc, qs_ref, kv0, kv1, kv2, kv3, bias_ref, w_ref, o_ref, lse_ref, n1_ref, cos_ref, sin_ref,
    dn_a, dn_b, dn_c, h_ref, r2_ref, gain_ref, dy_ref,
    dq_ref, d0, d1, d2, d3, dh_ref, gg_ref, pa0, pa1, pa2, pa3, datt_s, do_s, dl_s, dq_s,
):
    g = pl.program_id(0)
    kvs = (kv0, kv1, kv2, kv3)
    outs = (d0, d1, d2, d3)
    packs = (pa0, pa1, pa2, pa3)

    @pl.when(g == 0)
    def _():
        dn2 = dn_a[...].astype(F32) + dn_b[...].astype(F32) + dn_c[...].astype(F32)
        h = h_ref[...]
        r2 = r2_ref[...]
        weighted = dn2 * gain_ref[...]
        inner = jnp.sum(weighted * h, axis=0, keepdims=True)
        dh = dy_ref[...].astype(F32) + r2 * weighted - h * (r2 * r2 * r2 * inner / D)
        dh_ref[...] = dh
        datt_s[...] = dh.astype(BF)
        for b in range(ROWS):
            rows = slice(b * FB, (b + 1) * FB)
            gg_ref[b] = row_sums(dn2[rows] * h[rows] * r2)

    do_s[...] = tn(w_ref[0, :, SLOT_W:], datt_s[...]).astype(BF)
    for j in range(QPK):
        rows = slice(j * HD, (j + 1) * HD)
        dl_s[j : j + 1] = jnp.sum(
            do_s[rows].astype(F32) * o_ref[0, rows].astype(F32), axis=0, keepdims=True
        )

    def fold(k, fresh):
        keys = kvs[k][0, :HD]
        values = kvs[k][0, HD:]
        bias = bias_ref[k]
        dk = jnp.zeros((HD, CP), F32)
        dv = jnp.zeros((HD, CP), F32)
        for j in range(QPK):
            rows = slice(j * HD, (j + 1) * HD)
            s = tn(keys, qs_ref[0, rows]) + bias
            p = jnp.exp(s - lse_ref[0, j : j + 1])
            do_j = do_s[rows]
            dp = tn(values, do_j)
            ds = (p * (dp - dl_s[j : j + 1])).astype(BF)
            dv = dv + nt(do_j, p.astype(BF))
            dk = dk + nt(qs_ref[0, rows], ds)
            dq = nn(keys, ds)
            if fresh:
                dq_s[rows] = dq
            else:
                dq_s[rows] += dq
        outs[k][0, :HD] = dk.astype(outs[k].dtype)
        outs[k][0, HD:] = dv.astype(outs[k].dtype)

    fold(0, True)
    for k in range(1, ROWS):
        pl.when(sc[4 + k] != 0)(functools.partial(fold, k, False))

        @pl.when(sc[4 + k] == 0)
        def _(k=k):
            outs[k][...] = jnp.zeros(outs[k].shape, outs[k].dtype)

    cos_a = cos_ref[...]
    sin_a = sin_ref[...]
    for j in range(QPK):
        first, second = rope(
            dq_s[j * HD : j * HD + HALF] * HD**-0.5,
            dq_s[j * HD + HALF : (j + 1) * HD] * HD**-0.5,
            cos_a, -sin_a,
        )
        dq_ref[0, j * HD : j * HD + HALF] = first.astype(BF)
        dq_ref[0, j * HD + HALF : (j + 1) * HD] = second.astype(BF)

    for b in range(ROWS):
        rows = slice(b * FB, (b + 1) * FB)
        block = jnp.concatenate(
            [nt(dq_ref[0], n1_ref[rows]).astype(BF), nt(o_ref[0], datt_s[rows]).astype(BF)], axis=0
        )
        for k in range(ROWS):

            @pl.when(g == k)
            def _(k=k, block=block, b=b):
                packs[k][b, :AW] = block

        @pl.when(g == GROUPS - 1)
        def _(block=block, b=b):
            for k in range(ROWS):
                share = AW // ROWS
                for q in range(ROWS):

                    @pl.when((sc[0] ^ k) == q)
                    def _(k=k, q=q):
                        packs[k][b, AW:] = block[q * share : (q + 1) * share]


def final_kernel(
    sc, dq_ref, d0, d1, d2, w_ref, n1_ref, cos_ref, sin_ref, x_ref, r1_ref, gain_ref, dh_ref, gg_ref,
    h_ref, mlp_a, mlp_b, mlp_c,
    pb0, pb1, pb2, pb3, out0, out1, out2, out3, dn_s, dpg_s, dx_s, lo_s,
):
    g = pl.program_id(0)
    packs = (pb0, pb1, pb2, pb3)
    outs = (out0, out1, out2, out3)
    dkv = d0[0] + d1[0].astype(F32) + d2[0].astype(F32)
    first, second = rope(dkv[:HALF], dkv[HALF:HD], cos_ref[...], -sin_ref[...])
    dpg_s[:QW] = dq_ref[0]
    dpg_s[QW : QW + HALF] = first.astype(BF)
    dpg_s[QW + HALF : QW + HD] = second.astype(BF)
    dpg_s[QW + HD :] = dkv[HD:].astype(BF)
    part = nn(w_ref[0, :, :SLOT_W], dpg_s[...])

    @pl.when(g == 0)
    def _():
        dn_s[...] = part

    @pl.when(g != 0)
    def _():
        dn_s[...] += part

    for b in range(ROWS):
        block = nt(dpg_s[QW:], n1_ref[b * FB : (b + 1) * FB]).astype(BF)
        for k in range(ROWS):

            @pl.when(g == k)
            def _(k=k, block=block, b=b):
                packs[k][b, :KV] = block

        @pl.when(g == GROUPS - 1)
        def _(block=block, b=b):
            share = KV // ROWS
            for k in range(ROWS):
                for q in range(ROWS):

                    @pl.when((sc[0] ^ k) == q)
                    def _(k=k, q=q):
                        packs[k][b, KV : KV + share] = block[q * share : (q + 1) * share]

    @pl.when(g == GROUPS - 1)
    def _():
        dn1 = dn_s[...]
        x = x_ref[...].astype(F32)
        r1 = r1_ref[...]
        weighted = dn1 * gain_ref[...]
        inner = jnp.sum(weighted * x, axis=0, keepdims=True)
        dx = dh_ref[...] + r1 * weighted - x * (r1 * r1 * r1 * inner / D)
        dx_s[...] = dx.astype(BF)
        row = lax.broadcasted_iota(jnp.int32, (16, FB), 0)
        for b in range(ROWS):
            rows = slice(b * FB, (b + 1) * FB)
            sums = row_sums(dn1[rows] * x[rows] * r1)
            sums = jnp.where(row == 0, sums, jnp.where(row == 1, gg_ref[b], 0.0)).astype(BF)
            for k in range(ROWS):
                packs[k][b, KV + KV // ROWS :] = sums
        lo_s[...] = (
            h_ref[...] + mlp_a[...].astype(F32) + mlp_b[...].astype(F32) + mlp_c[...].astype(F32)
        ).astype(BF)
        for k in range(ROWS):
            outs[k][:FB] = lo_s[rows_at(sc[0] ^ k)]
            outs[k][FB:] = dx_s[rows_at(sc[0] ^ k)]


def mlp_kernel(count, halves, sc, *refs):
    if halves:
        w = refs[-1]
        part = refs[0].shape[0] // ROWS
        for h in range(2):
            shift = (FB - part) * (sc[3] if h == 0 else 1 - sc[3])
            for b in range(ROWS):
                w[pl.ds(pl.multiple_of(b * FB + shift, 16), part)] = refs[h][b * part : (b + 1) * part]
        wd = refs[2]
        refs = refs[3:-1]
    else:
        w, wd = refs[:2]
        refs = refs[2:]
    width = wd.shape[1]
    for i in range(count):
        n2 = refs[i]
        dy = refs[count + i]
        a_ref, dg_ref, du_ref, mlp_ref, dn_ref = refs[2 * count + 5 * i : 2 * count + 5 * i + 5]
        step = width
        for f in range(0, width, step):
            cols = slice(f, f + step)
            gate = tn(w[:, f : f + step], n2[...])
            up = tn(w[:, width + f : width + f + step], n2[...])
            da = tn(wd[:, cols], dy[...])
            sigma = jax.nn.sigmoid(gate)
            silu = gate * sigma
            a_ref[cols] = (silu * up).astype(BF)
            dg_ref[cols] = (da * up * sigma * (1.0 + gate * (1.0 - sigma))).astype(BF)
            du_ref[cols] = (da * silu).astype(BF)
        dn_ref[...] = (nn(w[:, :width], dg_ref[...]) + nn(w[:, width : 2 * width], du_ref[...])).astype(BF)
        mlp_ref[...] = nn(wd[...], a_ref[...]).astype(BF)


def mlp_grad_kernel(*refs):
    n2s, dys, acts, gates, ups = (refs[ROWS * i : ROWS * (i + 1)] for i in range(5))
    outs = refs[-2:]
    width = acts[0].shape[0]
    edge = outs[0].shape[1]
    for part, (left, right) in enumerate(((n2s, gates), (n2s, ups), (dys, acts))):
        begin = part * width
        cuts = [begin] + ([edge] if begin < edge < begin + width else []) + [begin + width]
        for low, high in zip(cuts[:-1], cuts[1:]):
            total = nt(left[0][...], right[0][low - begin : high - begin])
            for k in range(1, ROWS):
                total = total + nt(left[k][...], right[k][low - begin : high - begin])
            outs[low // edge][:, low % edge : low % edge + high - low] = total.astype(BF)


def grads_kernel(sc, g_ref, o0, o1, o2, o3, qkv_ref, out_ref, gains_ref, oa_s, ob_s):
    ix = sc[0]
    share_a = AW // ROWS
    share_b = KV // ROWS
    for k, odd in enumerate((o0, o1, o2, o3)):
        oa_s[pl.ds(pl.multiple_of((ix ^ k) * share_a, 8), share_a)] = odd[:share_a]
        ob_s[pl.ds(pl.multiple_of((ix ^ k) * share_b, 8), share_b)] = odd[share_a:]
    live = (ix == sc[2]).astype(F32)
    oa = oa_s[...] * live
    ob = ob_s[...] * live
    qkv_ref[...] = jnp.transpose(
        jnp.concatenate([g_ref[:QW], g_ref[AP : AP + KV], oa[:QW], ob], axis=0)
    )
    out_ref[...] = jnp.transpose(jnp.concatenate([g_ref[QW:AW], oa[QW:]], axis=0))
    gains_ref[...] = g_ref[AP + KV + share_b : AP + KV + share_b + 8]


def whole(*shape):
    return pl.BlockSpec(shape, lambda *_: (0,) * len(shape))


def per_group(*shape):
    return pl.BlockSpec((1,) + shape, lambda g, *_: (g,) + (0,) * len(shape))


def kv_blocks():
    def spec(k):
        return pl.BlockSpec((1, KV, CP), lambda g, *_: (jnp.where(g < ROWS, g ^ k, g), 0, 0))

    return [spec(k) for k in range(ROWS)]


def sds(shape, dtype):
    return jax.ShapeDtypeStruct(shape, dtype)


MICROSECONDS = {
    "split": 5, "qkv": 7, "attend": 18, "mlp_near": 13, "mlp_far": 13,
    "mlp_grad": 18, "attend_back": 30, "final": 19, "merge": 2, "grads": 3,
}


def cost(name):
    return pl.CostEstimate(
        flops=MICROSECONDS[name] * 100 * 10**6, bytes_accessed=MICROSECONDS[name] * 3000 * 100, transcendentals=0
    )


def simple(kernel, name, outs, *operands, scalars=None, scratch=(), limit=VMEM_LIMIT):
    specs = [pl.BlockSpec(memory_space=pltpu.VMEM)] * len(operands)
    if scalars is not None:
        specs = [pl.BlockSpec(memory_space=pltpu.SMEM)] + specs
        operands = (scalars,) + operands
    return pl.pallas_call(
        kernel,
        in_specs=specs,
        out_specs=[pl.BlockSpec(memory_space=pltpu.VMEM)] * len(outs),
        out_shape=list(outs),
        scratch_shapes=list(scratch),
        compiler_params=pltpu.CompilerParams(vmem_limit_bytes=limit),
        cost_estimate=cost(name),
        name=name,
    )(*operands)


def grouped(kernel, name, in_specs, outs, out_specs, scratch, sc, *operands):
    return pl.pallas_call(
        kernel,
        grid_spec=pltpu.PrefetchScalarGridSpec(
            num_scalar_prefetch=1,
            grid=(GROUPS,),
            in_specs=in_specs,
            out_specs=out_specs,
            scratch_shapes=scratch,
        ),
        out_shape=outs,
        compiler_params=pltpu.CompilerParams(vmem_limit_bytes=VMEM_LIMIT),
        cost_estimate=cost(name),
        name=name,
    )(sc, *operands)


def swap(values, bit):
    return lax.ppermute(values, "gx", [(i, i ^ bit) for i in range(ROWS)])


def row_gather(own):
    far = swap(own, 2)
    mate = swap(own, 1)
    return own, mate, far, swap(far, 1)


def after(values, *first):
    return lax.optimization_barrier((values,) + first)[0]


def row_near(blocks):
    far = (blocks[2].astype(F32) + swap(blocks[3], 1).astype(F32)).astype(BF)
    return blocks[0], swap(blocks[1], 1), far


def row_terms(blocks, first=()):
    a, b, far = row_near(blocks)
    if first:
        far = after(far, *first)
    return a, b, swap(far, 2)


def row_scatter(blocks, first=()):
    a, b, c = row_terms(blocks, first)
    return (a.astype(F32) + b.astype(F32) + c.astype(F32)).astype(BF)


def ring(values):
    return lax.ppermute(values, "gy", [(i, (i + 1) % ROWS) for i in range(ROWS)])


def ring_scatter(blocks, iy):
    def take(at):
        return lax.dynamic_index_in_dim(blocks, at % ROWS, 0, keepdims=False)

    moving = take(iy + 3)
    for s in range(ROWS - 1):
        moving = (ring(moving).astype(F32) + take(iy + 2 - s).astype(F32)).astype(BF)
    return moving


def dp_sum(values):
    if lax.axis_size("dp") == 2:
        return values.astype(F32) + lax.ppermute(values, "dp", [(0, 1), (1, 0)]).astype(F32)
    return lax.psum(values, "dp").astype(F32)


def to_token(k, piece):
    pairs = [(a * ROWS + b, (b ^ k) * ROWS + SEQ_MAP[a]) for a in range(ROWS) for b in range(ROWS)]
    return lax.ppermute(piece, ("gx", "gy"), pairs)


def to_features(pieces):
    back = []
    for k in range(ROWS):
        pairs = [(a * ROWS + b, SEQ_BACK[b] * ROWS + (a ^ k)) for a in range(ROWS) for b in range(ROWS)]
        back.append(lax.ppermute(pieces[k], ("gx", "gy"), pairs))
    return back


def per_device(
    tokens, segment_ids, slot_table, w_qkv, w_out, w_gate_up, w_down, gain_attn, gain_mlp, cotangent
):
    ix = lax.axis_index("gx")
    iy = lax.axis_index("gy")
    ff = w_down.shape[1]
    odd_row = jnp.sum(jnp.where(slot_table % 2 == 1, slot_table // 2, 0))

    seg = lax.ppermute(segment_ids, "gy", [(i, SEQ_MAP[i]) for i in range(ROWS)]).reshape(ROWS, CH)
    seg_own = lax.dynamic_index_in_dim(seg, ix, 0, keepdims=False)
    starts = [jnp.sum(seg < s).astype(jnp.int32) for s in range(SEGS)]
    first = sum(jnp.where(seg_own == s, starts[s], 0) for s in range(SEGS))
    at_own = jnp.arange(CP, dtype=jnp.int32)
    position = (ix * CH + at_own - jnp.pad(first, (0, CP - CH))).astype(F32)
    frequency = THETA_BASE ** (-2.0 * jnp.arange(HALF, dtype=F32) / HD)
    angles = frequency[:, None] * position[None, :]
    cos_a = jnp.cos(angles)
    sin_a = jnp.sin(angles)
    query_docs = jnp.pad(seg_own, (0, CP - CH), constant_values=-1)
    biases = []
    flags = []
    for k in range(ROWS):
        seg_k = lax.dynamic_index_in_dim(seg, ix ^ k, 0, keepdims=False)
        key_docs = jnp.pad(seg_k, (0, CP - CH), constant_values=-2)
        allowed = (key_docs[:, None] == query_docs[None, :]) & (
            ((ix ^ k) * CH + at_own)[:, None] <= (ix * CH + at_own)[None, :]
        )
        biases.append(jnp.where(allowed, 0.0, NEGATIVE).astype(F32))
        flags.append(((ix ^ k) <= ix) & (seg_k[CH - 1] >= seg_own[0]))
    bias = jnp.stack(biases)
    idp = lax.axis_index("dp")
    at = jnp.stack([ix, iy, odd_row, idp]).astype(jnp.int32)
    sc = jnp.concatenate([at, jnp.stack(flags).astype(jnp.int32)])

    pieces = simple(
        split_kernel, "split", [sds((2 * FB, CP), BF)] * ROWS,
        tokens, cotangent, gain_attn[:, None], gain_mlp[:, None], scalars=at,
    )
    odd = jnp.concatenate([w_qkv[:, SLOT_W:], w_out[:, QW:]], axis=1)
    odd = jnp.where(ix == odd_row, odd, jnp.zeros_like(odd))
    quarter = row_scatter([lax.dynamic_slice(odd, (0, ODD * (ix ^ k)), (FB, ODD)) for k in range(ROWS)])
    w_pieces = [after(jnp.concatenate([w_qkv[:, :SLOT_W], w_out[:, :QW], quarter], axis=1), pieces[0])]
    toks = []
    for k in range(ROWS):
        toks.append(to_token(k, after(pieces[k], *w_pieces[1:])))
        if k < ROWS - 1:
            w_pieces.append(ring(after(w_pieces[-1], *toks[:k])))
    w_own = jnp.concatenate(w_pieces, axis=0)
    w_far = jnp.concatenate([swap(w, 2) for w in w_pieces], axis=0)
    w_rows = [w_own, swap(after(w_own, toks[2]), 1), w_far, swap(after(w_far, toks[2], toks[3]), 1)]
    w_gu = jnp.concatenate([w_gate_up[:, 0], w_gate_up[:, 1]], axis=1)
    halves = lax.axis_size("dp") == 2
    if halves:
        w_gu = lax.dynamic_slice(w_gu, ((FB - 128) * idp, 0), (128, 2 * ff))
    w_gu = [lax.all_gather(after(w_gu, *toks), "gy", axis=0, tiled=True)]
    if halves:
        w_gu.append(lax.ppermute(w_gu[0], "dp", [(0, 1), (1, 0)]))
    x, dy, n1, r1, gain_one, gain_two, w5, qs, kv = simple(
        qkv_kernel, "qkv",
        [
            sds((D, CP), BF), sds((D, CP), BF), sds((D, CP), BF), sds((1, CP), F32), sds((D, 1), F32), sds((D, 1), F32),
            sds((GROUPS, D, PACK), BF), sds((GROUPS, QW, CP), BF), sds((GROUPS, KV, CP), BF),
        ],
        *toks, *w_rows, cos_a, sin_a,
        scalars=at,
    )

    w_d = lax.all_gather(w_down, "gy", axis=0, tiled=True)

    kvs = row_gather(kv)
    dys = row_gather(after(dy, kvs[2]))
    o, lse, h, n2, r2 = grouped(
        attend_kernel, "attend",
        [per_group(QW, CP)] + kv_blocks()
        + [whole(ROWS, CP, CP), per_group(D, PACK), whole(D, CP), whole(D, 1)],
        [
            sds((GROUPS, QW, CP), BF), sds((GROUPS, 8, CP), F32), sds((D, CP), F32), sds((D, CP), BF),
            sds((1, CP), F32),
        ],
        [per_group(QW, CP), per_group(8, CP), whole(D, CP), whole(D, CP), whole(1, CP)],
        [pltpu.VMEM((8, CP), F32), pltpu.VMEM((8, CP), F32), pltpu.VMEM((QW, CP), F32)],
        sc, after(qs, w_gu[0]), *kvs, bias, w5, x, gain_two,
    )

    n2s = row_gather(n2)
    per_block = [sds((ff, CP), BF)] * 3 + [sds((D, CP), BF)] * 2
    def feed_forward(name, some_n2, some_dy):
        return simple(
            functools.partial(mlp_kernel, 2, halves), name, per_block * 2, *w_gu, w_d, *some_n2, *some_dy,
            scalars=at, scratch=[pltpu.VMEM((D, 2 * ff), BF)] if halves else [],
        )

    far = feed_forward("mlp_far", n2s[2:], dys[2:])
    near = feed_forward("mlp_near", [after(n2s[0], far[9]), n2s[1]], dys[:2])
    blocks = [near[:5], near[5:], far[:5], far[5:]]
    dn2_terms = list(row_near([b[4] for b in blocks]))
    mlp_terms = list(row_near([b[3] for b in blocks]))

    dn2_terms[2] = swap(dn2_terms[2], 2)
    wide = (3 * ff // 2 + 127) // 128 * 128
    g_mlp = simple(
        mlp_grad_kernel, "mlp_grad", [sds((D, wide), BF), sds((D, 3 * ff - wide), BF)],
        after(n2s[0], dn2_terms[2]), *n2s[1:], *dys,
        *[b[0] for b in blocks], *[b[1] for b in blocks], *[b[2] for b in blocks],
    )

    pack_a = sds((ROWS, AP, FB), BF)

    def beside_back(far, *operands):
        return swap(far, 2), grouped(
        attend_back_kernel, "attend_back",
        [per_group(QW, CP)] + kv_blocks()
        + [whole(ROWS, CP, CP), per_group(D, PACK), per_group(QW, CP), per_group(8, CP), whole(D, CP),
           whole(HALF, CP), whole(HALF, CP)]
        + [whole(D, CP)] * 4 + [whole(1, CP), whole(D, 1), whole(D, CP)],
        [sds((GROUPS, QW, CP), BF), sds((GROUPS, KV, CP), F32)] + [sds((GROUPS, KV, CP), BF)] * 3
        + [sds((D, CP), F32), sds((ROWS, 16, FB), F32)] + [pack_a] * ROWS,
        [per_group(QW, CP)] + kv_blocks() + [whole(D, CP), whole(ROWS, 16, FB)]
        + [whole(ROWS, AP, FB)] * ROWS,
        [pltpu.VMEM((D, CP), BF), pltpu.VMEM((QW, CP), BF), pltpu.VMEM((8, CP), F32), pltpu.VMEM((QW, CP), F32)],
            *operands,
        )

    mlp_terms[2] = after(mlp_terms[2], dn2_terms[2])
    dn2_terms[1] = after(dn2_terms[1], g_mlp[0], mlp_terms[2])
    mlp_terms[2], back = beside_back(
        mlp_terms[2],
        sc, qs, *kvs, bias, w5, o, lse, n1, cos_a, sin_a, *dn2_terms, h, r2, gain_two, dy,
    )
    dq, dkv, dh, gg, packs_a = back[0], list(back[1:5]), back[5], back[6], back[7:]
    g_mlp = [lax.psum_scatter(g, "gy", scatter_dimension=0, tiled=True) for g in g_mlp]
    dkv[2] = after(dkv[2], mlp_terms[2], g_mlp[0])
    dkv_terms = list(row_terms(dkv))
    a_terms = list(row_near(packs_a))
    a_terms[2] = after(a_terms[2], dkv_terms[2])
    dkv_terms[0] = after(dkv_terms[0], a_terms[2])
    a_terms[2] = swap(a_terms[2], 2)
    final = grouped(
        final_kernel, "final",
        [per_group(QW, CP)] + [per_group(KV, CP)] * 3
        + [per_group(D, PACK), whole(D, CP), whole(HALF, CP), whole(HALF, CP), whole(D, CP), whole(1, CP),
           whole(D, 1), whole(D, CP), whole(ROWS, 16, FB)] + [whole(D, CP)] * 4,
        [sds((ROWS, BP, FB), BF)] * ROWS + [sds((2 * FB, CP), BF)] * ROWS,
        [whole(ROWS, BP, FB)] * ROWS + [whole(2 * FB, CP)] * ROWS,
        [pltpu.VMEM((D, CP), F32), pltpu.VMEM((SLOT_W, CP), BF)] + [pltpu.VMEM((D, CP), BF)] * 2,
        sc, dq, *dkv_terms, w5, n1, cos_a, sin_a, x, r1, gain_one, dh, gg, h, *mlp_terms,
    )
    packs_b, out_pieces = final[:ROWS], final[ROWS:]
    back = to_features(out_pieces)
    layer_out, input_grad = simple(merge_kernel, "merge", [sds((FB, L), BF)] * 2, *back, scalars=at)

    g_mlp = jnp.concatenate([dp_sum(g) for g in g_mlp], axis=1)
    grad_down = g_mlp[:, 2 * ff :]
    a_terms[0] = after(a_terms[0], packs_b[0])
    g_a = (
        (a_terms[0].astype(F32) + a_terms[1].astype(F32)) + a_terms[2].astype(F32)
    ).astype(BF)
    packs_b = list(packs_b)
    packs_b[3] = after(packs_b[3], g_a)
    g_all = jnp.concatenate([g_a, row_scatter(packs_b)], axis=1).reshape(ROWS * (AP + BP), FB)
    g_all = lax.psum_scatter(g_all, "gy", scatter_dimension=0, tiled=True)
    g_all = dp_sum(after(g_all, *back))
    odds = jnp.concatenate([g_all[AW:AP], g_all[AP + KV : AP + KV + KV // ROWS]], axis=0)
    grad_qkv, grad_out, grad_gains = simple(
        grads_kernel, "grads",
        [sds((FB, 2 * SLOT_W), F32), sds((FB, 2 * QW), F32), sds((8, FB), F32)],
        g_all, *row_gather(odds), scalars=at,
        scratch=[pltpu.VMEM((AW, FB), F32), pltpu.VMEM((KV, FB), F32)],
    )
    grad_gate_up = jnp.stack([g_mlp[:, :ff], g_mlp[:, ff : 2 * ff]], axis=1)
    return (
        layer_out,
        input_grad,
        grad_qkv,
        grad_out,
        grad_gate_up,
        grad_down,
        grad_gains[0],
        grad_gains[1],
    )


def solution(mesh):
    placed = (
        P("gy", ("dp", "gx")),
        P(("dp", "gy"), None),
        P(),
        P("gy", "gx"),
        P("gy", "gx"),
        P("gy", None, "gx"),
        P("gy", "gx"),
        P("gy"),
        P("gy"),
        P("gy", ("dp", "gx")),
    )
    return jax.shard_map(
        per_device,
        mesh=mesh,
        in_specs=placed,
        out_specs=(
            P("gy", ("dp", "gx")),
            P("gy", ("dp", "gx")),
            P("gy", "gx"),
            P("gy", "gx"),
            P("gy", None, "gx"),
            P("gy", "gx"),
            P("gy"),
            P("gy"),
        ),
        check_vma=False,
    )
```
